32 devices in a mesh: mp: 2 (over y), dp: 16 (over z, x, core).
Axes of the slice: x: 2, y: 2, z: 4, core: 2. Of those that a mesh axis runs over, the one named last changes fastest.
Arguments:
- stream: bfloat16 [32768, 1024], P(('dp', 'mp')), may hold values from -6 to 6
- cotangent: bfloat16 [32768, 1024], P(('dp', 'mp')), may hold values from -6 to 6
- segments: int32 [16, 2048], P('dp'), may hold values from 0 to 7, never falling along the last dimension, each value on 1 to 1500 neighbouring positions
- owners: int32 [2, 736], P('mp'), may hold values from 0 to 735, as said below
- master: float32 [2, 736, 128, 128], P('mp', 'dp'), may hold values from -1 to 1
- average: float32 [2, 736, 128, 128], P('mp', 'dp'), may hold values from -1 to 1
- left_stats: float32 [2, 736, 128, 128], P('mp', 'dp'), may hold values from -27596 to 55189, as said below
- right_stats: float32 [2, 736, 128, 128], P('mp', 'dp'), may hold values from -27596 to 55189, as said below
- left_root: float32 [2, 736, 128, 128], P('mp', 'dp'), may hold values from -4 to 10, as said below
- right_root: float32 [2, 736, 128, 128], P('mp', 'dp'), may hold values from -4 to 10, as said below
- gains: float32 [5, 1024], replicated, may hold values from 0.5 to 1.5
- kernel: float32 [5, 1024], replicated, may hold values from -2.5 to 2.5
Outputs:
- output: bfloat16 [32768, 1024], P(('dp', 'mp'))
- stream_grad: float32 [32768, 1024], P(('dp', 'mp'))
- block_grads: float32 [2, 736, 128, 128], P('mp', 'dp')
- left_new: float32 [2, 736, 128, 128], P('mp', 'dp')
- right_new: float32 [2, 736, 128, 128], P('mp', 'dp')
- master_new: float32 [2, 736, 128, 128], P('mp', 'dp')
- average_new: float32 [2, 736, 128, 128], P('mp', 'dp')
- gain_grads: float32 [5, 1024], replicated
- gains_new: float32 [5, 1024], replicated
- kernel_grads: float32 [5, 1024], replicated
- kernel_new: float32 [5, 1024], replicated
The draws below stay inside these ranges and needn't reach their ends.
Inputs may be any that keep to these rules, and one draw needn't show every extreme that they name: `owners`: each row names 736 different slots. `segments`: along each row the numbers never fall, every number up to 7 is used, and no number holds more than 1500 rows. `left_stats`: each block is symmetric. `right_stats`: each block is symmetric. `left_root`: each block is symmetric. `right_root`: each block is symmetric.
All inputs are finite; a program needn't handle non-finite values.
Results may differ from the reference program's by a relative error of at most 0.025.
Values may be sent and summed in bfloat16 or wider, within the bound.
No kernel may reach another device: no remote copies, remote signals or barrier semaphores. Data moves between devices by JAX's collectives and lax.ppermute only.
A program may use at most 320 MiB of HBM per device.

```python
import math
import jax
import jax.numpy as jnp
import numpy as np
from jax import lax

D = 1024
FF = 4096
HEADS = 8
HEAD_DIM = 128
KERNEL = 5
STEP = 4
BLOCK = 128
MAXLEN = 1500
GROUP = 2048
NSEQ = 8
TOKENS = 32768
BLOCKS_MP = 736
SLOTS = 736
N_MP = 2
N_DP = 16


def owner_table(key):

    def one_row(row_key):
        first_key, second_key = jax.random.split(row_key)
        middle = (jax.random.permutation(first_key, SLOTS - 2) + 1).astype(jnp.int32)
        chosen = jnp.concatenate([jnp.array([0, SLOTS - 1], jnp.int32), middle[:BLOCKS_MP - 2]])
        return jax.random.permutation(second_key, chosen)
    return jax.vmap(one_row)(jax.random.split(key, N_MP))


def block_scales():
    fshard = FF // N_MP
    cshard = D // N_MP
    shapes = [(D, fshard), (fshard, D), (D, cshard), (D, cshard), (D, cshard), (cshard, D), (D, cshard), (D, cshard), (cshard, D), (D, fshard), (fshard, D)]
    fans = [D, FF, D, D, D, D // 16, D, D, D, D, FF]
    pieces = [jnp.full((height * breadth // (BLOCK * BLOCK),), float(fan_size) ** (-0.5), jnp.float32) for (height, breadth), fan_size in zip(shapes, fans)]
    return jnp.concatenate(pieces)


def slot_scales(key):
    table = owner_table(key)
    slot_match = table[:, None, :] == jnp.arange(SLOTS)[None, :, None]
    scales = jnp.sum(jnp.where(slot_match, block_scales()[None, None, :], 0.0), axis=-1)
    return jnp.where(jnp.any(slot_match, axis=-1), scales, float(D) ** (-0.5))


def symmetric(key, diagonal, spread):
    noise = jnp.clip(jax.random.normal(key, (N_MP, SLOTS, BLOCK, BLOCK), jnp.float32), -5.0, 5.0)
    noise = (noise + jnp.swapaxes(noise, -1, -2)) * (0.7071 * spread / math.sqrt(BLOCK))
    identity = (jnp.arange(BLOCK)[:, None] == jnp.arange(BLOCK)[None, :]).astype(jnp.float32)
    return noise * (1.0 - identity) + identity * diagonal[..., None]


def stat_draw(key, magnitude):
    diag_key, off_key = jax.random.split(key)
    diagonal = magnitude * jax.random.uniform(diag_key, (N_MP, SLOTS, BLOCK), jnp.float32, 1.0, 4.0)
    return symmetric(off_key, diagonal, 0.5 * magnitude)


def root_draw(key):
    diag_key, off_key = jax.random.split(key)
    diagonal = jnp.exp(jax.random.uniform(diag_key, (N_MP, SLOTS, BLOCK), jnp.float32, 0.0, math.log(10.0)))
    return symmetric(off_key, diagonal, 1.2)


def draw_owners(key, part):
    table = owner_table(key)
    return table


def draw_master(key, part):
    scales = slot_scales(key)
    key = jax.random.fold_in(key, 11)
    noise = jnp.clip(jax.random.normal(key, (N_MP, SLOTS, BLOCK, BLOCK), jnp.float32), -4.0, 4.0)
    return noise * scales[:, :, None, None]


def draw_average(key, part):
    scales = slot_scales(key)
    key = jax.random.fold_in(key, 12)
    noise = jnp.clip(jax.random.normal(key, (N_MP, SLOTS, BLOCK, BLOCK), jnp.float32), -4.0, 4.0)
    return noise * scales[:, :, None, None]


def draw_left_stats(key, part):
    key = jax.random.fold_in(key, 13)
    return stat_draw(key, BLOCK * TOKENS / 304.0)


def draw_right_stats(key, part):
    key = jax.random.fold_in(key, 14)
    return stat_draw(key, BLOCK * TOKENS / 304.0)


def draw_left_root(key, part):
    key = jax.random.fold_in(key, 15)
    return root_draw(key)


def draw_right_root(key, part):
    key = jax.random.fold_in(key, 16)
    return root_draw(key)


def levels(stream_key, dims, cuts, least, high):
    def one(position, shards_of):
        steps = jax.random.uniform(jax.random.fold_in(jax.random.fold_in(stream_key, 6), position), (shards_of,), jnp.float32, least / len(cuts), high / len(cuts))
        return jnp.repeat(jnp.exp(steps), dims[position] // shards_of).reshape((-1,) + (1,) * (len(dims) - position - 1))

    factor_of = one(*cuts[0])
    for cut in cuts[1:]:
        factor_of = factor_of * one(*cut)
    return factor_of


def length_profile(number_of, total, bound, skew):
    loads = [(1 << 20) // math.isqrt(rank ** skew) + 1 for rank in range(2, number_of + 1)]
    rest, counts = total - bound - (number_of - 1), [1] * (number_of - 1)
    while rest > 0:
        free = [i for i in range(number_of - 1) if counts[i] < bound]
        pool, remaining = sum([loads[i] for i in free]), rest
        for i in free:
            extra = min(bound - counts[i], max(1, remaining * loads[i] // pool), rest)
            counts[i] = counts[i] + extra
            rest = rest - extra
    return np.array([bound] + counts)


def ragged(stream_key, amount, total, most, skew):
    if amount == 2:
        one = jax.random.randint(stream_key, (), max(1, total - most), min(most, total - 1) + 1)
        return jnp.stack([one, total - one])
    tallies = jnp.asarray(length_profile(amount, total, most, skew), jnp.int32)
    couples = (amount - 1) // 2
    giver, sink = tallies[1:1 + 2 * couples:2], tallies[2:2 + 2 * couples:2]
    margin = jnp.minimum(giver - 1, most - sink)
    moved = jax.random.randint(jax.random.fold_in(stream_key, 1), (couples,), 0, 1 << 20) % (margin + 1)
    tallies = tallies.at[1:1 + 2 * couples:2].set(giver - moved).at[2:2 + 2 * couples:2].set(sink + moved)
    return tallies[jax.random.permutation(jax.random.fold_in(stream_key, 2), amount)]


def bell_draw(key, dims, deviation, limit, cuts=(), held_as=jnp.bfloat16):
    factor_of = levels(key, dims, cuts, -0.22, 0.18) if cuts else 1.0
    values = jax.random.normal(key, dims, jnp.float32) * deviation * factor_of
    return jnp.minimum(jnp.maximum(values, -limit), limit).astype(held_as)


def setup_inputs(seed: int = 0) -> dict:
    keys = jax.random.split(jax.random.key(seed), 13)
    stream = bell_draw(keys[0], (TOKENS, D), 1.0, 6.0, ((0, 32),))
    cotangent = bell_draw(keys[1], (TOKENS, D), 1.0, 6.0, ((0, 32),))
    segments = jax.vmap(lambda own: jnp.searchsorted(jnp.cumsum(ragged(own, NSEQ, GROUP, MAXLEN, 2)), jnp.arange(GROUP), side="right"))(jax.random.split(keys[2], N_DP)).reshape((N_DP, GROUP)).astype(jnp.int32)
    owners = draw_owners(jax.random.fold_in(keys[12], 71), 0)
    master = draw_master(jax.random.fold_in(keys[12], 71), 0)
    average = draw_average(jax.random.fold_in(keys[12], 71), 0)
    left_stats = draw_left_stats(jax.random.fold_in(keys[12], 71), 0)
    right_stats = draw_right_stats(jax.random.fold_in(keys[12], 71), 0)
    left_root = draw_left_root(jax.random.fold_in(keys[12], 71), 0)
    right_root = draw_right_root(jax.random.fold_in(keys[12], 71), 0)
    gains = jnp.clip(1.0 + 0.1 * jax.random.normal(keys[10], (5, D), jnp.float32), 0.5, 1.5)
    kernel = bell_draw(keys[11], (KERNEL, D), KERNEL ** -0.5, 2.5, (), jnp.float32)
    return {"stream": stream, "cotangent": cotangent, "segments": segments, "owners": owners, "master": master, "average": average, "left_stats": left_stats, "right_stats": right_stats, "left_root": left_root, "right_root": right_root, "gains": gains, "kernel": kernel}


EPSILON = 1e-05
DECAY_STAT = 0.95
RATE_BLOCK = 0.02
RATE_VECTOR = 0.2
DECAY_AVERAGE = 0.9999
MASKED = -1e+30
HIGH = lax.Precision.HIGHEST

@jax.custom_vjp
def low(v):
    return lax.optimization_barrier(v.astype(jnp.bfloat16)).astype(jnp.float32)

@jax.custom_vjp
def low_back(v):
    return v

def low_keep(v):
    return (low(v), None)

def low_pass(kept, grad):
    return (grad,)

def back_keep(v):
    return (v, None)

def back_low(kept, grad):
    return (low(grad),)
low.defvjp(low_keep, low_pass)
low_back.defvjp(back_keep, back_low)

def silu(values):
    return values * jax.nn.sigmoid(values)

def layer_norm(values, norm_gain):
    center = values - lax.optimization_barrier(jnp.mean(values, axis=-1, keepdims=True))
    spread = lax.optimization_barrier(jnp.mean(center * center, axis=-1, keepdims=True))
    return center * lax.rsqrt(spread + EPSILON) * norm_gain

def product(left_op, right_op):
    return jnp.dot(left_op, right_op, precision=HIGH, preferred_element_type=jnp.float32)

def shard_shapes():
    fshard = FF // N_MP
    cshard = D // N_MP
    return [(D, fshard), (fshard, D), (D, cshard), (D, cshard), (D, cshard), (cshard, D), (D, cshard), (D, cshard), (cshard, D), (D, fshard), (fshard, D)]

def unblock(blocks, height, breadth):
    shaped = blocks.reshape(height // BLOCK, breadth // BLOCK, BLOCK, BLOCK)
    return shaped.transpose(0, 2, 1, 3).reshape(height, breadth)

def split_blocks(blocks):
    pieces = []
    offset = 0
    for height, breadth in shard_shapes():
        block_count = height * breadth // (BLOCK * BLOCK)
        pieces.append(unblock(blocks[offset:offset + block_count], height, breadth))
        offset = offset + block_count
    return pieces

def neighbour_masks(segment_ids):
    half = KERNEL // 2
    length = segment_ids.shape[0]
    padded = jnp.pad(segment_ids, (half, half), constant_values=-1)
    return [(padded[tap_index:tap_index + length] == segment_ids).astype(jnp.float32)[:, None] for tap_index in range(KERNEL)]

def depthwise(glu_rows, taps, seg_masks):
    half = KERNEL // 2
    length = glu_rows.shape[0]
    padded = jnp.pad(glu_rows, ((half, half), (0, 0)))
    summed = jnp.zeros_like(glu_rows)
    for tap_index in range(KERNEL):
        summed = summed + taps[tap_index] * padded[tap_index:tap_index + length] * seg_masks[tap_index]
    return summed

def head_slopes():
    return 2.0 ** (-8.0 * (jnp.arange(HEADS).astype(jnp.float32) + 1.0) / HEADS)

def feed_forward(stream_rows, norm_gain, uppers, lowers):
    normed = low(layer_norm(stream_rows, norm_gain))
    summed = jnp.zeros_like(stream_rows)
    for model_parallel_rank in range(N_MP):
        copied = low_back(normed)
        pre_act = low_back(product(copied, uppers[model_parallel_rank]))
        summed = summed + low(product(low(silu(pre_act)), lowers[model_parallel_rank]))
    return stream_rows + 0.5 * low_back(summed)

def attention(stream_rows, norm_gain, query_weights, key_weights, value_weights, out_weights, segment_ids):
    length = stream_rows.shape[0]
    heads_local = HEADS // N_MP
    normed = low(layer_norm(stream_rows, norm_gain))
    positions = jnp.arange(length)
    distance = jnp.abs(positions[:, None] - positions[None, :]).astype(jnp.float32)
    same_seg = (segment_ids[:, None] == segment_ids[None, :])[None]
    slopes = head_slopes()
    summed = jnp.zeros_like(stream_rows)
    for model_parallel_rank in range(N_MP):
        copied = low_back(normed)
        queries = low(low_back(product(copied, query_weights[model_parallel_rank]))).reshape(length, heads_local, HEAD_DIM)
        key_rows = low(low_back(product(copied, key_weights[model_parallel_rank]))).reshape(length, heads_local, HEAD_DIM)
        value_rows = low(low_back(product(copied, value_weights[model_parallel_rank]))).reshape(length, heads_local, HEAD_DIM)
        raw_scores = jnp.einsum('qhd,khd->hqk', queries, key_rows, precision=HIGH) / math.sqrt(HEAD_DIM)
        head_slope = slopes[model_parallel_rank * heads_local:(model_parallel_rank + 1) * heads_local]
        scores = low_back(raw_scores - head_slope[:, None, None] * distance[None])
        masked = jnp.where(same_seg, scores, MASKED)
        shifted = jnp.exp(masked - lax.optimization_barrier(jnp.max(masked, axis=-1, keepdims=True)))
        probs = shifted / lax.optimization_barrier(jnp.sum(shifted, axis=-1, keepdims=True))
        mixed_rows = jnp.einsum('hqk,khd->qhd', low(probs), value_rows, precision=HIGH).reshape(length, heads_local * HEAD_DIM)
        summed = summed + low(product(low(low_back(mixed_rows)), out_weights[model_parallel_rank]))
    return stream_rows + low_back(summed)

def convolution(stream_rows, norm_gain, value_weights, gate_weights, out_weights, kernel, segment_ids):
    cshard = D // N_MP
    normed = low(layer_norm(stream_rows, norm_gain))
    seg_masks = neighbour_masks(segment_ids)
    summed = jnp.zeros_like(stream_rows)
    for model_parallel_rank in range(N_MP):
        copied = low_back(normed)
        linear = low_back(product(copied, value_weights[model_parallel_rank]))
        gate_pre = low_back(product(copied, gate_weights[model_parallel_rank]))
        taps = kernel[:, model_parallel_rank * cshard:(model_parallel_rank + 1) * cshard]
        conved = depthwise(linear * jax.nn.sigmoid(gate_pre), taps, seg_masks)
        summed = summed + low(product(low(silu(conved)), out_weights[model_parallel_rank]))
    return stream_rows + low_back(summed)

def block_forward(stream_rows, blocks, gains, kernel, segment_ids):
    shards = [split_blocks(blocks[model_parallel_rank]) for model_parallel_rank in range(N_MP)]
    weights = [[shards[model_parallel_rank][number] for model_parallel_rank in range(N_MP)] for number in range(11)]
    after_ffn = feed_forward(stream_rows, gains[0], weights[0], weights[1])
    after_attn = attention(after_ffn, gains[1], weights[2], weights[3], weights[4], weights[5], segment_ids)
    after_conv = convolution(after_attn, gains[2], weights[6], weights[7], weights[8], kernel, segment_ids)
    after_last = feed_forward(after_conv, gains[3], weights[9], weights[10])
    return layer_norm(after_last, gains[4])

def vector_step(params, grads):
    mean_sq = lax.optimization_barrier(jnp.mean(grads * grads, axis=-1, keepdims=True))
    return params - RATE_VECTOR * grads * lax.rsqrt(mean_sq + 1e-06)

def shampoo(grads, left_stats, right_stats, left_root, right_root, master, average):
    left_new = DECAY_STAT * left_stats + (1.0 - DECAY_STAT) * jnp.einsum('...ij,...kj->...ik', grads, grads, precision=HIGH)
    right_new = DECAY_STAT * right_stats + (1.0 - DECAY_STAT) * jnp.einsum('...ji,...jk->...ik', grads, grads, precision=HIGH)
    inner_side = jnp.einsum('...ij,...jk->...ik', grads, right_root, precision=HIGH)
    direction = jnp.einsum('...ij,...jk->...ik', left_root, inner_side, precision=HIGH)
    mean_sq = lax.optimization_barrier(jnp.mean(direction * direction, axis=(-2, -1), keepdims=True))
    master_new = master - RATE_BLOCK * direction * lax.rsqrt(mean_sq + 1e-06)
    old_bias = 1.0 - DECAY_AVERAGE ** (STEP - 1)
    new_bias = 1.0 - DECAY_AVERAGE ** STEP
    average_new = (DECAY_AVERAGE * (average * old_bias) + (1.0 - DECAY_AVERAGE) * master_new) / new_bias
    return (left_new, right_new, master_new, average_new)

def reference(stream, cotangent, segments, owners, master, average, left_stats, right_stats, left_root, right_root, gains, kernel):
    rank_ids = jnp.arange(N_MP)[:, None]
    blocks = low(master)[rank_ids, owners]
    inputs = stream.astype(jnp.float32).reshape(N_DP, GROUP, D)
    cotangents = cotangent.astype(jnp.float32).reshape(N_DP, GROUP, D)

    def one_group(carried, group_items):
        group_rows, group_cot, group_segs = group_items

        def forward(rows_in, blocks_in, gains_in, kernel_in):
            return block_forward(rows_in, blocks_in, gains_in, kernel_in, group_segs)
        result, pullback = jax.vjp(forward, group_rows, blocks, gains, kernel)
        row_grad, block_grad, gain_grad, kernel_grad = pullback(group_cot)
        summed = (carried[0] + block_grad, carried[1] + gain_grad, carried[2] + kernel_grad)
        return (summed, (result, row_grad))
    initial = (jnp.zeros_like(blocks), jnp.zeros_like(gains), jnp.zeros_like(kernel))
    (block_grads, gain_grads, kernel_grads), (results, row_grads) = lax.scan(one_group, initial, (inputs, cotangents, segments))
    slot_grads = jnp.zeros_like(master).at[rank_ids, owners].set(block_grads)
    left_new, right_new, master_new, average_new = shampoo(slot_grads, left_stats, right_stats, left_root, right_root, master, average)
    return (results.reshape(N_DP * GROUP, D).astype(jnp.bfloat16), row_grads.reshape(N_DP * GROUP, D), slot_grads, left_new, right_new, master_new, average_new, gain_grads, vector_step(gains, gain_grads), kernel_grads, vector_step(kernel, kernel_grads))
```

```python
import math

import jax
import jax.numpy as jnp
import numpy as np
from jax import lax
from jax.experimental import pallas as pl
from jax.experimental.pallas import tpu as pltpu
from jax.sharding import Mesh
from jax.sharding import PartitionSpec as P

D = 1024
FF = 4096
HEADS = 8
HEAD_DIM = 128
KERNEL = 5
STEP = 4
BLOCK = 128
HALO = 16
WIDE = 8

EPSILON = 1e-05
DECAY_STAT = 0.95
RATE_BLOCK = 0.02
RATE_VECTOR = 0.2
DECAY_AVERAGE = 0.9999
MASKED = -1e30
LOG2E = math.log2(math.e)
SCORE_SCALE = 1.0 / math.sqrt(HEAD_DIM)

f32 = jnp.float32
bf16 = jnp.bfloat16
ANY = pl.BlockSpec(memory_space=pl.ANY)
SMEM = pl.BlockSpec(memory_space=pltpu.SMEM)

MATRICES = [
    (0, D, FF, True),
    (4, FF, D, False),
    (8, D, D, True),
    (9, D, D, True),
    (10, D, D, True),
    (11, D, D, False),
    (12, D, D, True),
    (13, D, D, True),
    (14, D, D, False),
    (15, D, FF, True),
    (19, FF, D, False),
]
UP1, DOWN1, QUERY, KEY, VALUE, OUT, CONV_VALUE, CONV_GATE, CONV_OUT, UP2, DOWN2 = range(11)
CHUNKS = 23
WEIGHT_BLOCKS = CHUNKS * 8 * WIDE


def at(matrix):
    return MATRICES[matrix][0]


GATHER_PIECES = [
    (0, 3, "x"),
    (3, 3, "y"),
    (6, 7, "x"),
    (13, 7, "y"),
    (20, 7, "x"),
    (27, 7, "y"),
    (34, 6, "x"),
    (40, 6, "y"),
]
SCATTER_PIECES = [
    (0, 6, "x"),
    (6, 6, "y"),
    (12, 7, "x"),
    (19, 7, "y"),
    (26, 7, "x"),
    (33, 7, "y"),
    (40, 3, "x"),
    (43, 3, "y"),
]


def params(**kw):
    return pltpu.CompilerParams(vmem_limit_bytes=58 * 2**20, **kw)


def const_spec(shape):
    return pl.BlockSpec(shape, lambda *ids: (0,) * len(shape), pipeline_mode=pl.Buffered(1))


def row_tile(rows):
    return 256 if rows % 256 == 0 else 128


def cost(flops, moved):
    return pl.CostEstimate(flops=int(flops), bytes_accessed=int(moved), transcendentals=0)


def offsets(ranks):
    out = []
    offset = 0
    for unused, height, breadth, by_columns in MATRICES:
        out.append(offset)
        offset = offset + height * breadth // (BLOCK * BLOCK * ranks)
    return out, offset


def block_number(matrix, row_block, column_block, ranks):
    starts, total = offsets(ranks)
    unused, height, breadth, by_columns = MATRICES[matrix]
    if by_columns:
        part = breadth // BLOCK // ranks
        return (
            (column_block // part) * total + starts[matrix] + row_block * part + column_block % part
        )
    part = height // BLOCK // ranks
    breadth_blocks = breadth // BLOCK
    return (
        (row_block // part) * total
        + starts[matrix]
        + (row_block % part) * breadth_blocks
        + column_block
    )


def weight_places(ranks):
    unused, total = offsets(ranks)
    places = np.zeros((ranks * total,), np.int32)
    for matrix, (chunk, height, breadth, by_columns) in enumerate(MATRICES):
        for row in range(height // BLOCK):
            for column in range(breadth // BLOCK):
                place = ((chunk + column // WIDE) * 8 + row) * WIDE + column % WIDE
                places[block_number(matrix, row, column, ranks)] = place
    return places.reshape(ranks, total)


def place_weights(weights, arrays, bases, slot_places, lanes, depth, width, rows_all):
    count = arrays[0].shape[0]
    total = count * len(arrays)

    def body(table, base_ref, *rest):
        sources = rest[: len(arrays)]
        out, sem = rest[-2], rest[-1]

        def one(t, unused):
            step = (t // width) * depth + t % width
            for number, source in enumerate(sources):
                place = table[base_ref[number] + step]
                row = pl.multiple_of((place // WIDE) * BLOCK, BLOCK)
                column = pl.multiple_of((place % WIDE) * BLOCK, BLOCK)
                pltpu.make_async_copy(
                    source.at[t], out.at[pl.ds(row, BLOCK), pl.ds(column, BLOCK)], sem
                ).start()
            return unused

        lax.fori_loop(0, count, one, 0)
        whole = sources[0] if len(sources) == 1 else out.at[pl.ds(0, total * BLOCK // WIDE), :]
        pltpu.make_async_copy(whole, whole, sem).wait()

    operands = [slot_places, bases, *arrays]
    aliases = {}
    specs = [SMEM, SMEM] + [ANY] * len(arrays)
    if weights is not None:
        aliases = {len(operands): 0}
        operands.append(weights)
        specs.append(ANY)
    return pl.pallas_call(
        body,
        out_shape=jax.ShapeDtypeStruct((rows_all, D), bf16),
        in_specs=specs,
        out_specs=ANY,
        scratch_shapes=[pltpu.SemaphoreType.DMA],
        input_output_aliases=aliases,
        compiler_params=params(has_side_effects=True),
        cost_estimate=cost(0, 2 * total * BLOCK * BLOCK * 2),
        name="place_weights",
    )(*operands)


def swap(value, axis):
    return lax.ppermute(value, axis, [(0, 1), (1, 0)])


def gather_weights(own, slot_places, coords, fast, rows_all):
    slot_dev = own.shape[0]
    if not fast:
        everything = lax.all_gather(own, ("mp", "z", "x", "core"), axis=0, tiled=True)
        return place_weights(
            None, [everything], jnp.zeros((1,), jnp.int32), slot_places, None, 0,
            everything.shape[0], rows_all,
        )
    rank, x_at, core_at = coords
    zs = lax.axis_size("z")
    weights = None
    for first, count, kind in GATHER_PIECES:
        column = lax.all_gather(own[first : first + count], "z", axis=0, tiled=True)
        if kind == "x":
            beside = swap(column, "x")
            parts = [
                (column, 0, 0),
                (beside, 0, 1),
                (swap(column, "mp"), 1, 0),
                (swap(beside, "mp"), 1, 1),
            ]
        else:
            beside = swap(column, "mp")
            parts = [
                (column, 0, 0),
                (beside, 1, 0),
                (swap(column, "x"), 0, 1),
                (swap(beside, "x"), 1, 1),
            ]
        arrays, bases = [], []
        for flip in (0, 1):
            for value, dy, dx in parts:
                arrays.append(swap(value, "core") if flip else value)
                bases.append(
                    (
                        ((rank ^ dy) * zs * 2 + (x_at ^ dx)) * 2 + (core_at ^ flip)
                    )
                    * slot_dev
                    + first
                )
        weights = place_weights(
            weights, arrays, jnp.stack(bases).astype(jnp.int32), slot_places, None,
            4 * slot_dev, count, rows_all,
        )
    return weights


def sigmoid(values):
    return 0.5 * jnp.tanh(0.5 * values) + 0.5


def norm_parts(values):
    center = values - jnp.mean(values, axis=-1, keepdims=True)
    spread = jnp.mean(center * center, axis=-1, keepdims=True)
    scale = lax.rsqrt(spread + EPSILON)
    return center * scale, scale


def norm(values, gain):
    return norm_parts(values)[0] * gain


def norm_back(values, gain, grad):
    hat, scale = norm_parts(values)
    inner = grad * gain
    mean_inner = jnp.mean(inner, axis=-1, keepdims=True)
    mean_hat = jnp.mean(inner * hat, axis=-1, keepdims=True)
    return (
        scale * (inner - mean_inner - hat * mean_hat),
        jnp.sum(grad * hat, axis=0, keepdims=True),
    )


def dot(a, b):
    return jnp.dot(a, b, preferred_element_type=f32)


def dot_right(a, b):
    return lax.dot_general(a, b, (((1,), (1,)), ((), ())), preferred_element_type=f32)


def dot_left(a, b):
    return lax.dot_general(a, b, (((0,), (0,)), ((), ())), preferred_element_type=f32)


def start_blocks(table, sums, source, sem, matrix, row_block, column_block, ranks):
    height, breadth = source.shape
    for i in range(height // BLOCK):
        for j in range(breadth // BLOCK):
            place = table[block_number(matrix, row_block + i, column_block + j, ranks)]
            pltpu.make_async_copy(
                source.at[pl.ds(i * BLOCK, BLOCK), pl.ds(j * BLOCK, BLOCK)], sums.at[place], sem
            ).start()


def wait_blocks(source, sem):
    pltpu.make_async_copy(source, source, sem).wait()


def ffn_forward(stream, gain, next_gain, weights, upper, lower):
    rows = stream.shape[0]
    tile = row_tile(rows)
    wide = 512
    steps = FF // wide

    def body(x_ref, gain_ref, next_gain_ref, up_ref, down_ref, out_ref, pre_ref, next_ref, normed):
        step = pl.program_id(0)

        @pl.when(step == 0)
        def _():
            for t in range(0, rows, tile):
                x = x_ref[t : t + tile].astype(f32)
                normed[t : t + tile] = norm(x, gain_ref[...]).astype(bf16)
                out_ref[t : t + tile] = jnp.zeros((tile, D), f32)

        for t in range(0, rows, tile):
            pre = dot(normed[t : t + tile], up_ref[...])
            pre_ref[t : t + tile] = pre.astype(bf16)
            act = (pre * sigmoid(pre)).astype(bf16)
            out_ref[t : t + tile] += dot(act, down_ref[...])

        @pl.when(step == steps - 1)
        def _():
            for t in range(0, rows, tile):
                y = x_ref[t : t + tile].astype(f32) + 0.5 * out_ref[t : t + tile]
                out_ref[t : t + tile] = y
                next_ref[t : t + tile] = norm(y, next_gain_ref[...]).astype(bf16)

    return pl.pallas_call(
        body,
        grid=(steps,),
        out_shape=(
            jax.ShapeDtypeStruct((rows, D), f32),
            jax.ShapeDtypeStruct((rows, FF), bf16),
            jax.ShapeDtypeStruct((rows, D), bf16),
        ),
        in_specs=[
            const_spec((rows, D)),
            const_spec((1, D)),
            const_spec((1, D)),
            pl.BlockSpec((D, wide), lambda f: (at(upper) + f // 2, f % 2)),
            pl.BlockSpec((wide, D), lambda f: (at(lower) * 2 + f, 0)),
        ],
        out_specs=(
            const_spec((rows, D)),
            pl.BlockSpec((rows, wide), lambda f: (0, f)),
            const_spec((rows, D)),
        ),
        scratch_shapes=[pltpu.VMEM((rows, D), bf16)],
        compiler_params=params(),
        cost_estimate=cost(4 * rows * D * FF, 4 * D * FF + 2 * rows * FF),
        name="ffn_forward",
    )(stream, gain, next_gain, weights, weights)


def ffn_backward(
    after, after_gain, after_grads, base, stream, gain, pre, weights, upper, lower, sums, table,
    ranks,
):
    rows = stream.shape[0]
    tile = row_tile(rows)
    wide = 512
    steps = FF // wide
    parts = len(after_grads)
    with_base = base is not None

    def body(table_ref, *refs):
        refs = list(refs)
        after_ref, after_gain_ref = refs[0], refs[1]
        grad_refs = refs[2 : 2 + parts]
        at_ref = 2 + parts
        base_ref = None
        if with_base:
            base_ref = refs[at_ref]
            at_ref += 1
        x_ref, gain_ref, pre_ref, up_ref, down_ref, sums_in = refs[at_ref : at_ref + 6]
        out_ref, gains_ref, sums_ref = refs[at_ref + 6 : at_ref + 9]
        (half, normed_t, grad_sum, pre_grad, act_t, up_part, down_part, up_sem, down_sem) = refs[
            at_ref + 9 :
        ]
        step = pl.program_id(0)
        slot = lax.rem(step, 2)

        @pl.when(step == 0)
        def _():
            gain_sum = jnp.zeros((1, D), f32)
            for t in range(0, rows, tile):
                here = slice(t, t + tile)
                grad = grad_refs[0][here].astype(f32)
                for other in grad_refs[1:]:
                    grad = grad + other[here].astype(f32)
                back, part = norm_back(after_ref[here], after_gain_ref[...], grad)
                gain_sum = gain_sum + part
                if with_base:
                    back = back + base_ref[here]
                out_ref[here] = back
                half[here] = (0.5 * back).astype(bf16)
                normed = norm(x_ref[here].astype(f32), gain_ref[...]).astype(bf16)
                normed_t[:, here] = normed.T
                grad_sum[here] = jnp.zeros((tile, D), f32)
            gains_ref[0:1] = gain_sum

        for t in range(0, rows, tile):
            here = slice(t, t + tile)
            act_grad = dot_right(half[here], down_ref[...])
            pre_act = pre_ref[here].astype(f32)
            sigma = sigmoid(pre_act)
            act = pre_act * sigma
            act_t[:, here] = act.astype(bf16).T
            slope = sigma + act * (1.0 - sigma)
            moved = (act_grad * slope).astype(bf16)
            pre_grad[here] = moved
            grad_sum[here] += dot_right(moved, up_ref[...])

        @pl.when(step >= 2)
        def _():
            wait_blocks(up_part.at[slot], up_sem.at[slot])
            wait_blocks(down_part.at[slot], down_sem.at[slot])

        for t in range(0, D, 256):
            up_part[slot, t : t + 256] = dot(normed_t[t : t + 256], pre_grad[...]).astype(bf16)
        for t in range(0, wide, 256):
            down_part[slot, t : t + 256] = dot(act_t[t : t + 256], half[...]).astype(bf16)
        start_blocks(
            table_ref, sums_ref, up_part.at[slot], up_sem.at[slot], upper, 0, step * 4, ranks
        )
        start_blocks(
            table_ref, sums_ref, down_part.at[slot], down_sem.at[slot], lower, step * 4, 0, ranks
        )

        @pl.when(step == steps - 1)
        def _():
            gain_sum = jnp.zeros((1, D), f32)
            for t in range(0, rows, tile):
                here = slice(t, t + tile)
                back, part = norm_back(x_ref[here].astype(f32), gain_ref[...], grad_sum[here])
                gain_sum = gain_sum + part
                out_ref[here] += back
            gains_ref[1:2] = gain_sum
            for s in range(2):
                wait_blocks(up_part.at[s], up_sem.at[s])
                wait_blocks(down_part.at[s], down_sem.at[s])

    operands = [table, after, after_gain, *after_grads]
    specs = [SMEM, const_spec((rows, D)), const_spec((1, D))] + [const_spec((rows, D))] * parts
    if with_base:
        operands.append(base)
        specs.append(const_spec((rows, D)))
    operands += [stream, gain, pre, weights, weights, sums]
    specs += [
        const_spec((rows, D)),
        const_spec((1, D)),
        pl.BlockSpec((rows, wide), lambda f: (0, f)),
        pl.BlockSpec((D, wide), lambda f: (at(upper) + f // 2, f % 2)),
        pl.BlockSpec((wide, D), lambda f: (at(lower) * 2 + f, 0)),
        ANY,
    ]
    return pl.pallas_call(
        body,
        grid=(steps,),
        out_shape=(
            jax.ShapeDtypeStruct((rows, D), f32),
            jax.ShapeDtypeStruct((2, D), f32),
            jax.ShapeDtypeStruct(sums.shape, bf16),
        ),
        in_specs=specs,
        out_specs=(const_spec((rows, D)), const_spec((2, D)), ANY),
        scratch_shapes=[
            pltpu.VMEM((rows, D), bf16),
            pltpu.VMEM((D, rows), bf16),
            pltpu.VMEM((rows, D), f32),
            pltpu.VMEM((rows, wide), bf16),
            pltpu.VMEM((wide, rows), bf16),
            pltpu.VMEM((2, D, wide), bf16),
            pltpu.VMEM((2, wide, D), bf16),
            pltpu.SemaphoreType.DMA((2,)),
            pltpu.SemaphoreType.DMA((2,)),
        ],
        input_output_aliases={len(operands) - 1: 2},
        compiler_params=params(has_side_effects=True),
        cost_estimate=cost(8 * rows * D * FF, 8 * D * FF + 2 * rows * FF),
        name="ffn_backward",
    )(*operands)


def project(values, weights, first, count):
    rows = values.shape[0]
    tile = row_tile(rows)
    wide = 512

    def body(x_ref, w_ref, out_ref):
        for t in range(0, rows, tile):
            out_ref[t : t + tile] = dot(x_ref[t : t + tile], w_ref[...]).astype(bf16)

    return pl.pallas_call(
        body,
        grid=(2 * count,),
        out_shape=jax.ShapeDtypeStruct((rows, count * D), bf16),
        in_specs=[
            const_spec((rows, D)),
            pl.BlockSpec((D, wide), lambda f: (at(first) + f // 2, f % 2)),
        ],
        out_specs=pl.BlockSpec((rows, wide), lambda f: (0, f)),
        compiler_params=params(),
        cost_estimate=cost(2 * rows * D * D * count, 2 * count * D * (D + rows)),
        name="project",
    )(values, weights)


def project_out(values, weights, matrix, stream):
    rows = values.shape[0]
    tile = row_tile(rows)

    def body(x_ref, w_ref, s_ref, out_ref):
        out_ref[...] = s_ref[...] + dot(x_ref[...], w_ref[...])

    return pl.pallas_call(
        body,
        grid=(rows // tile,),
        out_shape=jax.ShapeDtypeStruct((rows, D), f32),
        in_specs=[
            pl.BlockSpec((tile, D), lambda t: (t, 0)),
            pl.BlockSpec((D, D), lambda t: (at(matrix), 0)),
            pl.BlockSpec((tile, D), lambda t: (t, 0)),
        ],
        out_specs=pl.BlockSpec((tile, D), lambda t: (t, 0)),
        compiler_params=params(),
        cost_estimate=cost(2 * rows * D * D, 2 * D * D + 10 * rows * D),
        name="project_out",
    )(values, weights, stream)


def project_out_back(grad, weights, matrix, attended, sums, table, ranks):
    rows = grad.shape[0]
    tile = row_tile(rows)
    wide = 512

    def body(table_ref, g_ref, w_ref, a_ref, sums_in, out_ref, sums_ref, low, part, sem):
        step = pl.program_id(0)

        @pl.when(step == 0)
        def _():
            for t in range(0, rows, tile):
                low[t : t + tile] = g_ref[t : t + tile].astype(bf16)

        for t in range(0, rows, tile):
            out_ref[t : t + tile] = dot_right(low[t : t + tile], w_ref[...]).astype(bf16)
        for t in range(0, wide, 256):
            part[step, t : t + 256] = dot_left(a_ref[:, t : t + 256], low[...]).astype(bf16)
        start_blocks(table_ref, sums_ref, part.at[step], sem.at[step], matrix, step * 4, 0, ranks)

        @pl.when(step == 1)
        def _():
            for s in range(2):
                wait_blocks(part.at[s], sem.at[s])

    return pl.pallas_call(
        body,
        grid=(2,),
        out_shape=(
            jax.ShapeDtypeStruct((rows, D), bf16),
            jax.ShapeDtypeStruct(sums.shape, bf16),
        ),
        in_specs=[
            SMEM,
            const_spec((rows, D)),
            pl.BlockSpec((wide, D), lambda f: (at(matrix) * 2 + f, 0)),
            pl.BlockSpec((rows, wide), lambda f: (0, f)),
            ANY,
        ],
        out_specs=(pl.BlockSpec((rows, wide), lambda f: (0, f)), ANY),
        scratch_shapes=[
            pltpu.VMEM((rows, D), bf16),
            pltpu.VMEM((2, wide, D), bf16),
            pltpu.SemaphoreType.DMA((2,)),
        ],
        input_output_aliases={4: 1},
        compiler_params=params(has_side_effects=True),
        cost_estimate=cost(4 * rows * D * D, 4 * D * D + 8 * rows * D),
        name="project_out_back",
    )(table, grad, weights, attended, sums)


def input_gradient(key_grad, value_grad, weights):
    rows = key_grad.shape[0]
    tile = row_tile(rows)

    def body(k_ref, v_ref, wk_ref, wv_ref, out_ref):
        out_ref[...] = (
            dot_right(k_ref[...], wk_ref[...]) + dot_right(v_ref[...], wv_ref[...])
        ).astype(bf16)

    return pl.pallas_call(
        body,
        grid=(rows // tile,),
        out_shape=jax.ShapeDtypeStruct((rows, D), bf16),
        in_specs=[
            pl.BlockSpec((tile, D), lambda t: (t, 0)),
            pl.BlockSpec((tile, D), lambda t: (t, 0)),
            pl.BlockSpec((D, D), lambda t: (at(KEY), 0)),
            pl.BlockSpec((D, D), lambda t: (at(VALUE), 0)),
        ],
        out_specs=pl.BlockSpec((tile, D), lambda t: (t, 0)),
        compiler_params=params(),
        cost_estimate=cost(4 * rows * D * D, 4 * D * D + 6 * rows * D),
        name="input_gradient",
    )(key_grad, value_grad, weights, weights)


def projections_back(normed, query_grad, sources, own_keys, weights, sums, table, ranks):
    rows = normed.shape[0]
    tile = row_tile(rows)
    wide = 512
    count = len(sources)
    lengths = [source[0].shape[0] for source in sources]

    def body(table_ref, n_ref, q_ref, *refs):
        normed_refs = refs[:count]
        key_refs = refs[count : 2 * count]
        value_refs = refs[2 * count : 3 * count]
        w_ref, sums_in, out_ref, sums_ref = refs[3 * count : 3 * count + 4]
        scratch = refs[3 * count + 4 :]
        own_t = scratch[0]
        source_t = scratch[1 : 1 + count]
        part, sem = scratch[1 + count :]
        step = pl.program_id(0)
        slot = lax.rem(step, 2)

        @pl.when(step == 0)
        def _():
            for t in range(0, rows, tile):
                own_t[:, t : t + tile] = n_ref[t : t + tile].T
            for n_from, n_to, length in zip(normed_refs, source_t, lengths):
                small = row_tile(length)
                for t in range(0, length, small):
                    n_to[:, t : t + small] = n_from[t : t + small].T

        @pl.when(step >= 2)
        def _():
            wait_blocks(part.at[slot], sem.at[slot])

        @pl.when(step < 2)
        def _():
            for t in range(0, rows, tile):
                new = dot_right(q_ref[t : t + tile], w_ref[...])

                @pl.when(step == 0)
                def _():
                    out_ref[t : t + tile] = new

                @pl.when(step == 1)
                def _():
                    out_ref[t : t + tile] += new

            for t in range(0, D, 256):
                part[slot, t : t + 256] = dot(own_t[t : t + 256], q_ref[...]).astype(bf16)
            start_blocks(
                table_ref, sums_ref, part.at[slot], sem.at[slot], QUERY, 0, lax.rem(step, 2) * 4,
                ranks,
            )

        def other(grad_refs, matrix):
            if own_keys:
                for t in range(0, rows, tile):
                    out_ref[t : t + tile] += dot_right(grad_refs[0][t : t + tile], w_ref[...])
            for t in range(0, D, 256):
                total = dot(source_t[0][t : t + 256], grad_refs[0][...])
                for n_t, grad_ref in zip(source_t[1:], grad_refs[1:]):
                    total = total + dot(n_t[t : t + 256], grad_ref[...])
                part[slot, t : t + 256] = total.astype(bf16)
            start_blocks(
                table_ref, sums_ref, part.at[slot], sem.at[slot], matrix, 0, lax.rem(step, 2) * 4,
                ranks,
            )

        @pl.when((step >= 2) & (step < 4))
        def _():
            other(key_refs, KEY)

        @pl.when(step >= 4)
        def _():
            other(value_refs, VALUE)

        @pl.when(step == 5)
        def _():
            for s in range(2):
                wait_blocks(part.at[s], sem.at[s])

    operands = [table, normed, query_grad]
    specs = [
        SMEM,
        const_spec((rows, D)),
        pl.BlockSpec((rows, wide), lambda f: (0, jnp.minimum(f, 1))),
    ]
    operands += [source[0] for source in sources]
    specs += [const_spec((length, D)) for length in lengths]
    operands += [source[1] for source in sources]
    specs += [
        pl.BlockSpec((length, wide), lambda f: (0, jnp.clip(f - 2, 0, 1))) for length in lengths
    ]
    operands += [source[2] for source in sources]
    specs += [
        pl.BlockSpec((length, wide), lambda f: (0, jnp.clip(f - 4, 0, 1))) for length in lengths
    ]
    operands += [weights, sums]
    specs += [pl.BlockSpec((D, wide), lambda f: (at(QUERY) + f // 2, f % 2)), ANY]
    return pl.pallas_call(
        body,
        grid=(6,),
        out_shape=(
            jax.ShapeDtypeStruct((rows, D), f32),
            jax.ShapeDtypeStruct(sums.shape, bf16),
        ),
        in_specs=specs,
        out_specs=(const_spec((rows, D)), ANY),
        scratch_shapes=[pltpu.VMEM((D, rows), bf16)]
        + [pltpu.VMEM((D, length), bf16) for length in lengths]
        + [pltpu.VMEM((2, D, wide), bf16), pltpu.SemaphoreType.DMA((2,))],
        input_output_aliases={len(operands) - 1: 1},
        compiler_params=params(has_side_effects=True),
        cost_estimate=cost(
            (4 * rows + sum(4 * length for length in lengths) + 4 * rows) * D * D, 30 * D * D
        ),
        name="projections_back",
    )(*operands)


def attention_forward(queries, sources, segments, rank, spans, slopes):
    rows = queries.shape[0]
    tall = row_tile(rows)
    broad = 512
    count = len(sources)
    lengths = [source[0].shape[0] for source in sources]
    bases = jnp.stack([jnp.asarray(source[2], jnp.int32) for source in sources] + [rank * rows])
    columns = [
        lax.dynamic_slice_in_dim(segments, source[2], length).reshape(1, length)
        for source, length in zip(sources, lengths)
    ]
    own = lax.dynamic_slice_in_dim(segments, rank * rows, rows).reshape(rows, 1)

    def body(base_ref, span_ref, slope_ref, seg_ref, *refs):
        q_ref, own_ref = refs[0], refs[1]
        key_refs = refs[2 : 2 + count]
        value_refs = refs[2 + count : 2 + 2 * count]
        column_refs = refs[2 + 2 * count : 2 + 3 * count]
        out_ref, total_ref = refs[2 + 3 * count : 4 + 3 * count]
        peak, total, mixed = refs[4 + 3 * count :]
        head, block = pl.program_id(0), pl.program_id(1)
        slope = slope_ref[head] * LOG2E
        first = base_ref[count] + block * tall
        peak[...] = jnp.full(peak.shape, MASKED, f32)
        total[...] = jnp.zeros(total.shape, f32)
        mixed[...] = jnp.zeros(mixed.shape, f32)
        query = q_ref[...]
        apart = (
            lax.broadcasted_iota(jnp.int32, (tall, broad), 0)
            - lax.broadcasted_iota(jnp.int32, (tall, broad), 1)
        ).astype(f32)
        same_rows = seg_ref[first] == seg_ref[first + tall - 1]

        for number in range(count):
            base = base_ref[number]

            def step(k, unused, number=number, base=base):
                here = pl.ds(pl.multiple_of(k * broad, broad), broad)
                key = key_refs[number][here, :]
                value = value_refs[number][here, :]
                start = base + k * broad
                scores = dot_right(query, key) * (SCORE_SCALE * LOG2E)
                scores = scores - slope * jnp.abs(apart + (first - start).astype(f32))

                def finish(scores):
                    old = peak[:, 0:1]
                    new = jnp.maximum(old, jnp.max(scores, axis=-1, keepdims=True))
                    shifted = jnp.exp2(scores - new)
                    fade = jnp.exp2(old - new)
                    peak[...] = jnp.broadcast_to(new, peak.shape)
                    total[...] = total[...] * fade + jnp.sum(shifted, axis=-1, keepdims=True)
                    mixed[...] = mixed[...] * fade + dot(shifted.astype(bf16), value)

                inside = (
                    same_rows
                    & (seg_ref[start] == seg_ref[start + broad - 1])
                    & (seg_ref[start] == seg_ref[first])
                )

                @pl.when(inside)
                def _():
                    finish(scores)

                @pl.when(jnp.logical_not(inside))
                def _():
                    related = own_ref[...] == column_refs[number][:, here]
                    finish(jnp.where(related, scores, MASKED))

                return unused

            span = (block * count + number) * 2
            lax.fori_loop(span_ref[span], span_ref[span + 1], step, 0)
        out_ref[...] = (mixed[...] / total[...]).astype(bf16)
        logs = peak[...] + jnp.log2(total[...])
        total_ref[...] = logs.T[0:1, :].reshape(1, 1, tall)

    specs = [SMEM, SMEM, SMEM, SMEM]
    specs += [
        pl.BlockSpec((tall, HEAD_DIM), lambda h, q: (q, h)),
        pl.BlockSpec((tall, 1), lambda h, q: (q, 0)),
    ]
    operands = [bases, spans, slopes, segments, queries, own]
    for shift in (0, HEADS):
        for (array, column, unused), length in zip(sources, lengths):
            operands.append(array)
            specs.append(
                pl.BlockSpec(
                    (length, HEAD_DIM), lambda h, q, c=column + shift: (0, c + h)
                )
            )
    for segment_row, length in zip(columns, lengths):
        operands.append(segment_row)
        specs.append(const_spec((1, length)))
    return pl.pallas_call(
        body,
        grid=(HEADS, rows // tall),
        out_shape=(
            jax.ShapeDtypeStruct((rows, D), bf16),
            jax.ShapeDtypeStruct((HEADS, 1, rows), f32),
        ),
        in_specs=specs,
        out_specs=(
            pl.BlockSpec((tall, HEAD_DIM), lambda h, q: (q, h)),
            pl.BlockSpec((1, 1, tall), lambda h, q: (h, 0, q)),
        ),
        scratch_shapes=[pltpu.VMEM((tall, HEAD_DIM), f32)] * 3,
        compiler_params=params(),
        cost_estimate=cost(2 * rows * sum(lengths) * D, 8 * rows * D),
        name="attention_forward",
    )(*operands)


def attention_backward(queries, sources, segments, rank, spans, slopes, logs, grads, attended):
    rows = queries.shape[0]
    tall = row_tile(rows)
    broad = 512
    count = len(sources)
    lengths = [source[0].shape[0] for source in sources]
    bases = jnp.stack([jnp.asarray(source[2], jnp.int32) for source in sources] + [rank * rows])
    columns = [
        lax.dynamic_slice_in_dim(segments, source[2], length).reshape(length, 1)
        for source, length in zip(sources, lengths)
    ]
    own = lax.dynamic_slice_in_dim(segments, rank * rows, rows).reshape(1, rows)

    def body(base_ref, span_ref, slope_ref, seg_ref, *refs):
        q_ref, own_ref, log_ref, grad_ref, att_ref = refs[:5]
        key_refs = refs[5 : 5 + count]
        value_refs = refs[5 + count : 5 + 2 * count]
        column_refs = refs[5 + 2 * count : 5 + 3 * count]
        out_ref = refs[5 + 3 * count]
        key_out = refs[6 + 3 * count : 6 + 4 * count]
        value_out = refs[6 + 4 * count : 6 + 5 * count]
        scratch = refs[6 + 5 * count :]
        query_sum = scratch[0]
        key_sum = scratch[1 : 1 + count]
        value_sum = scratch[1 + count : 1 + 2 * count]
        head, block = pl.program_id(0), pl.program_id(1)
        slope = slope_ref[head] * LOG2E
        first = base_ref[count] + block * tall

        @pl.when(block == 0)
        def _():
            for ref in (*key_sum, *value_sum):
                ref[...] = jnp.zeros(ref.shape, f32)

        query_sum[...] = jnp.zeros(query_sum.shape, f32)
        query = q_ref[...]
        grad = grad_ref[...]
        products = grad.astype(f32) * att_ref[...].astype(f32)
        delta = lax.dot_general(
            jnp.ones((8, HEAD_DIM), f32),
            products,
            (((1,), (1,)), ((), ())),
            precision=lax.Precision.HIGHEST,
            preferred_element_type=f32,
        )[0:1, :]
        log_row = log_ref[0]
        apart = (
            lax.broadcasted_iota(jnp.int32, (broad, tall), 1)
            - lax.broadcasted_iota(jnp.int32, (broad, tall), 0)
        ).astype(f32)
        same_rows = seg_ref[first] == seg_ref[first + tall - 1]

        for number in range(count):
            base = base_ref[number]

            def step(k, unused, number=number, base=base):
                here = pl.ds(pl.multiple_of(k * broad, broad), broad)
                key = key_refs[number][here, :]
                value = value_refs[number][here, :]
                start = base + k * broad
                scores = dot_right(key, query) * (SCORE_SCALE * LOG2E)
                scores = scores - slope * jnp.abs(apart + (first - start).astype(f32))

                def finish(scores):
                    probs = jnp.exp2(scores - log_row)
                    value_sum[number][here, :] += dot(probs.astype(bf16), grad)
                    prob_grad = dot_right(value, grad)
                    score_grad = (probs * (prob_grad - delta)).astype(bf16)
                    key_sum[number][here, :] += dot(score_grad, query)
                    query_sum[...] += dot_left(score_grad, key)

                inside = (
                    same_rows
                    & (seg_ref[start] == seg_ref[start + broad - 1])
                    & (seg_ref[start] == seg_ref[first])
                )

                @pl.when(inside)
                def _():
                    finish(scores)

                @pl.when(jnp.logical_not(inside))
                def _():
                    related = own_ref[...] == column_refs[number][here, :]
                    finish(jnp.where(related, scores, MASKED))

                return unused

            span = (block * count + number) * 2
            lax.fori_loop(span_ref[span], span_ref[span + 1], step, 0)
        out_ref[...] = (query_sum[...] * SCORE_SCALE).astype(bf16)

        @pl.when(block == pl.num_programs(1) - 1)
        def _():
            for number in range(count):
                key_out[number][...] = (key_sum[number][...] * SCORE_SCALE).astype(bf16)
                value_out[number][...] = value_sum[number][...].astype(bf16)

    row_spec = pl.BlockSpec((tall, HEAD_DIM), lambda h, q: (q, h))
    specs = [SMEM, SMEM, SMEM, SMEM]
    specs += [
        row_spec,
        pl.BlockSpec((1, tall), lambda h, q: (0, q)),
        pl.BlockSpec((1, 1, tall), lambda h, q: (h, 0, q)),
        row_spec,
        row_spec,
    ]
    operands = [bases, spans, slopes, segments, queries, own, logs, grads, attended]
    for shift in (0, HEADS):
        for (array, column, unused), length in zip(sources, lengths):
            operands.append(array)
            specs.append(
                pl.BlockSpec(
                    (length, HEAD_DIM), lambda h, q, c=column + shift: (0, c + h)
                )
            )
    for segment_column, length in zip(columns, lengths):
        operands.append(segment_column)
        specs.append(const_spec((length, 1)))
    source_specs = [pl.BlockSpec((length, HEAD_DIM), lambda h, q: (0, h)) for length in lengths]
    source_shapes = [jax.ShapeDtypeStruct((length, D), bf16) for length in lengths]
    sums = [pltpu.VMEM((length, HEAD_DIM), f32) for length in lengths]
    out = pl.pallas_call(
        body,
        grid=(HEADS, rows // tall),
        out_shape=(jax.ShapeDtypeStruct((rows, D), bf16), *source_shapes, *source_shapes),
        in_specs=specs,
        out_specs=(row_spec, *source_specs, *source_specs),
        scratch_shapes=[pltpu.VMEM((tall, HEAD_DIM), f32), *sums, *sums],
        compiler_params=params(),
        cost_estimate=cost(5 * rows * sum(lengths) * D, 12 * rows * D),
        name="attention_backward",
    )(*operands)
    return out[0], out[1 : 1 + count], out[1 + count :]


def key_spans(segments, rank, rows, sources):
    tall = row_tile(rows)
    broad = 512
    blocks = rows // tall
    own = lax.dynamic_slice_in_dim(segments, rank * rows, rows).reshape(blocks, tall)
    low = jnp.sum(segments[None, :] < own[:, :1], axis=1)
    high = jnp.sum(segments[None, :] <= own[:, -1:], axis=1)
    spans = []
    for length, base in sources:
        start = jnp.clip(low - base, 0, length)
        end = jnp.clip(high - base, 0, length)
        first = start // broad
        last = jnp.where(end > start, (end + broad - 1) // broad, first)
        spans.append(jnp.stack([first, last], axis=-1))
    return jnp.stack(spans, axis=1).reshape(-1).astype(jnp.int32)


def conv_forward(stream, before, behind, gain, weights, taps, masks):
    rows = stream.shape[0]
    tall = rows + 2 * HALO
    tile = row_tile(rows)
    wide = 256
    steps = D // wide

    def body(
        x_ref, before_ref, behind_ref, gain_ref, taps_ref, mask_ref, value_ref, gate_ref, out_w_ref,
        out_ref, linear_ref, gate_out_ref, normed, glu,
    ):
        step = pl.program_id(0)

        @pl.when(step == 0)
        def _():
            gain_row = gain_ref[...]
            normed[0:HALO] = norm(before_ref[...], gain_row).astype(bf16)
            normed[rows + HALO :] = norm(behind_ref[...], gain_row).astype(bf16)
            for t in range(0, rows, tile):
                x = x_ref[t : t + tile]
                normed[HALO + t : HALO + t + tile] = norm(x, gain_row).astype(bf16)
                out_ref[t : t + tile] = x

        pieces = [(0, HALO)]
        pieces += [(HALO + t, tile) for t in range(0, rows, tile)]
        pieces += [(rows + HALO, HALO)]
        for t, size in pieces:
            here = slice(t, t + size)
            linear = dot(normed[here], value_ref[...])
            gate = dot(normed[here], gate_ref[...])
            linear_ref[here] = linear.astype(bf16)
            gate_out_ref[here] = gate.astype(bf16)
            glu[here] = linear * sigmoid(gate)
        for t in range(0, rows, tile):
            sums = []
            for half in range(0, wide, 128):
                total = jnp.zeros((tile, 128), f32)
                for k in range(KERNEL):
                    moved = glu[HALO + t + k - 2 : HALO + t + k - 2 + tile, half : half + 128]
                    mask = mask_ref[k, HALO + t : HALO + t + tile]
                    total = total + taps_ref[k : k + 1, half : half + 128] * moved * mask
                sums.append(total)
            conved = jnp.concatenate(sums, axis=1)
            act = (conved * sigmoid(conved)).astype(bf16)
            out_ref[t : t + tile] += dot(act, out_w_ref[...])

    return pl.pallas_call(
        body,
        grid=(steps,),
        out_shape=(
            jax.ShapeDtypeStruct((rows, D), f32),
            jax.ShapeDtypeStruct((tall, D), bf16),
            jax.ShapeDtypeStruct((tall, D), bf16),
        ),
        in_specs=[
            const_spec((rows, D)),
            const_spec((HALO, D)),
            const_spec((HALO, D)),
            const_spec((1, D)),
            pl.BlockSpec((KERNEL, wide), lambda c: (0, c)),
            const_spec((KERNEL, tall, 128)),
            pl.BlockSpec((D, wide), lambda c: (at(CONV_VALUE), c)),
            pl.BlockSpec((D, wide), lambda c: (at(CONV_GATE), c)),
            pl.BlockSpec((wide, D), lambda c: (at(CONV_OUT) * 4 + c, 0)),
        ],
        out_specs=(
            const_spec((rows, D)),
            pl.BlockSpec((tall, wide), lambda c: (0, c)),
            pl.BlockSpec((tall, wide), lambda c: (0, c)),
        ),
        scratch_shapes=[pltpu.VMEM((tall, D), bf16), pltpu.VMEM((tall, wide), f32)],
        compiler_params=params(),
        cost_estimate=cost(6 * rows * D * D, 6 * D * D + 12 * rows * D),
        name="conv_forward",
    )(stream, before, behind, gain, taps, masks, weights, weights, weights)


def conv_backward(
    grad, before, behind, stream, gain, linear, gate, weights, taps, masks, sums, table, ranks
):
    rows = stream.shape[0]
    tall = rows + 2 * HALO
    tile = row_tile(rows)
    wide = 256
    steps = D // wide

    def body(
        table_ref, g_ref, before_ref, behind_ref, x_ref, gain_ref, linear_ref, gate_ref, taps_ref,
        mask_ref, value_ref, gate_w_ref, out_w_ref, sums_in, out_ref, gain_out_ref, taps_out_ref,
        sums_ref, low, normed_t, grad_sum, glu, conv_grad, act_t, value_grad, gate_grad,
        value_part, gate_part, out_part, value_sem, gate_sem, out_sem,
    ):
        step = pl.program_id(0)
        slot = lax.rem(step, 2)

        @pl.when(step == 0)
        def _():
            low[0:HALO] = before_ref[...]
            low[rows + HALO :] = behind_ref[...]
            for t in range(0, rows, tile):
                here = slice(t, t + tile)
                low[HALO + t : HALO + t + tile] = g_ref[here].astype(bf16)
                normed_t[:, here] = norm(x_ref[here], gain_ref[...]).astype(bf16).T
                grad_sum[here] = jnp.zeros((tile, D), f32)

        pieces = [(0, HALO)]
        pieces += [(HALO + t, tile) for t in range(0, rows, tile)]
        pieces += [(rows + HALO, HALO)]
        for t, size in pieces:
            here = slice(t, t + size)
            glu[here] = linear_ref[here].astype(f32) * sigmoid(gate_ref[here].astype(f32))

        edge = 8
        pieces = [(HALO - edge, edge)]
        pieces += [(HALO + t, tile) for t in range(0, rows, tile)]
        pieces += [(rows + HALO, edge)]
        for t, size in pieces:
            totals = []
            for half in range(0, wide, 128):
                total = jnp.zeros((size, 128), f32)
                for k in range(KERNEL):
                    moved = glu[t + k - 2 : t + k - 2 + size, half : half + 128]
                    mask = mask_ref[k, t : t + size]
                    total = total + taps_ref[k : k + 1, half : half + 128] * moved * mask
                totals.append(total)
            conved = jnp.concatenate(totals, axis=1)
            sigma = sigmoid(conved)
            act = conved * sigma
            if size == tile:
                act_t[:, t - HALO : t - HALO + size] = act.astype(bf16).T
                rows_grad = dot_right(low[t : t + size], out_w_ref[...])
            elif t < HALO:
                rows_grad = dot_right(low[0:HALO], out_w_ref[...])[edge:]
            else:
                rows_grad = dot_right(low[rows + HALO :], out_w_ref[...])[:edge]
            conv_grad[t : t + size] = rows_grad * (sigma + act * (1.0 - sigma))

        tap_sums = [[jnp.zeros((1, 128), f32) for k in range(KERNEL)] for half in range(2)]
        for t in range(0, rows, tile):
            values, gates = [], []
            for number, half in enumerate(range(0, wide, 128)):
                lanes = slice(half, half + 128)
                start = HALO + t
                center = conv_grad[start : start + tile, lanes]
                total = jnp.zeros((tile, 128), f32)
                for k in range(KERNEL):
                    back = KERNEL - 1 - k
                    moved = conv_grad[start + 2 - k : start + 2 - k + tile, lanes]
                    total = total + taps_ref[k : k + 1, lanes] * moved * mask_ref[
                        back, start : start + tile
                    ]
                    shifted = glu[start + k - 2 : start + k - 2 + tile, lanes]
                    tap_sums[number][k] = tap_sums[number][k] + jnp.sum(
                        center * shifted * mask_ref[k, start : start + tile],
                        axis=0,
                        keepdims=True,
                    )
                sigma = sigmoid(gate_ref[start : start + tile, lanes].astype(f32))
                moved_value = total * sigma
                values.append(moved_value.astype(bf16))
                gates.append(
                    (
                        moved_value
                        * linear_ref[start : start + tile, lanes].astype(f32)
                        * (1.0 - sigma)
                    ).astype(bf16)
                )
            value_tile = jnp.concatenate(values, axis=1)
            gate_tile = jnp.concatenate(gates, axis=1)
            here = slice(t, t + tile)
            value_grad[here] = value_tile
            gate_grad[here] = gate_tile
            grad_sum[here] += dot_right(value_tile, value_ref[...]) + dot_right(
                gate_tile, gate_w_ref[...]
            )
        for k in range(KERNEL):
            taps_out_ref[k : k + 1] = jnp.concatenate([tap_sums[0][k], tap_sums[1][k]], axis=1)

        @pl.when(step >= 2)
        def _():
            wait_blocks(value_part.at[slot], value_sem.at[slot])
            wait_blocks(gate_part.at[slot], gate_sem.at[slot])
            wait_blocks(out_part.at[slot], out_sem.at[slot])

        for t in range(0, D, 256):
            value_part[slot, t : t + 256] = dot(normed_t[t : t + 256], value_grad[...]).astype(bf16)
            gate_part[slot, t : t + 256] = dot(normed_t[t : t + 256], gate_grad[...]).astype(bf16)
        out_part[slot] = dot(act_t[...], low[HALO : rows + HALO]).astype(bf16)
        start_blocks(
            table_ref, sums_ref, value_part.at[slot], value_sem.at[slot], CONV_VALUE, 0, step * 2,
            ranks,
        )
        start_blocks(
            table_ref, sums_ref, gate_part.at[slot], gate_sem.at[slot], CONV_GATE, 0, step * 2,
            ranks,
        )
        start_blocks(
            table_ref, sums_ref, out_part.at[slot], out_sem.at[slot], CONV_OUT, step * 2, 0, ranks
        )

        @pl.when(step == steps - 1)
        def _():
            gain_sum = jnp.zeros((1, D), f32)
            for t in range(0, rows, tile):
                here = slice(t, t + tile)
                back, part = norm_back(x_ref[here], gain_ref[...], grad_sum[here])
                gain_sum = gain_sum + part
                out_ref[here] = g_ref[here] + back
            gain_out_ref[...] = gain_sum
            for s in range(2):
                wait_blocks(value_part.at[s], value_sem.at[s])
                wait_blocks(gate_part.at[s], gate_sem.at[s])
                wait_blocks(out_part.at[s], out_sem.at[s])

    operands = [
        table, grad, before, behind, stream, gain, linear, gate, taps, masks, weights, weights,
        weights, sums,
    ]
    return pl.pallas_call(
        body,
        grid=(steps,),
        out_shape=(
            jax.ShapeDtypeStruct((rows, D), f32),
            jax.ShapeDtypeStruct((1, D), f32),
            jax.ShapeDtypeStruct((KERNEL, D), f32),
            jax.ShapeDtypeStruct(sums.shape, bf16),
        ),
        in_specs=[
            SMEM,
            const_spec((rows, D)),
            const_spec((HALO, D)),
            const_spec((HALO, D)),
            const_spec((rows, D)),
            const_spec((1, D)),
            pl.BlockSpec((tall, wide), lambda c: (0, c)),
            pl.BlockSpec((tall, wide), lambda c: (0, c)),
            pl.BlockSpec((KERNEL, wide), lambda c: (0, c)),
            const_spec((KERNEL, tall, 128)),
            pl.BlockSpec((D, wide), lambda c: (at(CONV_VALUE), c)),
            pl.BlockSpec((D, wide), lambda c: (at(CONV_GATE), c)),
            pl.BlockSpec((wide, D), lambda c: (at(CONV_OUT) * 4 + c, 0)),
            ANY,
        ],
        out_specs=(
            const_spec((rows, D)),
            const_spec((1, D)),
            pl.BlockSpec((KERNEL, wide), lambda c: (0, c)),
            ANY,
        ),
        scratch_shapes=[
            pltpu.VMEM((tall, D), bf16),
            pltpu.VMEM((D, rows), bf16),
            pltpu.VMEM((rows, D), f32),
            pltpu.VMEM((tall, wide), f32),
            pltpu.VMEM((tall, wide), f32),
            pltpu.VMEM((wide, rows), bf16),
            pltpu.VMEM((rows, wide), bf16),
            pltpu.VMEM((rows, wide), bf16),
            pltpu.VMEM((2, D, wide), bf16),
            pltpu.VMEM((2, D, wide), bf16),
            pltpu.VMEM((2, wide, D), bf16),
            pltpu.SemaphoreType.DMA((2,)),
            pltpu.SemaphoreType.DMA((2,)),
            pltpu.SemaphoreType.DMA((2,)),
        ],
        input_output_aliases={len(operands) - 1: 3},
        compiler_params=params(has_side_effects=True),
        cost_estimate=cost(12 * rows * D * D, 12 * D * D + 16 * rows * D),
        name="conv_backward",
    )(*operands)


def shampoo(grads, left_stats, right_stats, left_root, right_root, master, average):
    slots = grads.shape[0]
    each = 2 if slots % 2 == 0 else 1
    old_bias = 1.0 - DECAY_AVERAGE ** (STEP - 1)
    new_bias = 1.0 - DECAY_AVERAGE**STEP

    def body(g_ref, ls_ref, rs_ref, lr_ref, rr_ref, m_ref, a_ref, go, lo, ro, mo, ao):
        for n in range(each):
            grad = g_ref[n]
            go[n] = grad.astype(f32)
            lo[n] = DECAY_STAT * ls_ref[n] + (1.0 - DECAY_STAT) * dot_right(grad, grad)
            ro[n] = DECAY_STAT * rs_ref[n] + (1.0 - DECAY_STAT) * dot_left(grad, grad)
            inner = dot(grad, rr_ref[n].astype(bf16))
            turned = dot(lr_ref[n].astype(bf16), inner.astype(bf16))
            mean_sq = jnp.mean(turned * turned, axis=(0, 1), keepdims=True)
            new = m_ref[n] - RATE_BLOCK * turned * lax.rsqrt(mean_sq + 1e-06)
            mo[n] = new
            ao[n] = (DECAY_AVERAGE * old_bias / new_bias) * a_ref[n] + (
                (1.0 - DECAY_AVERAGE) / new_bias
            ) * new

    spec = pl.BlockSpec((each, BLOCK, BLOCK), lambda s: (s, 0, 0))
    shape = jax.ShapeDtypeStruct((slots, BLOCK, BLOCK), f32)
    return pl.pallas_call(
        body,
        grid=(slots // each,),
        out_shape=(shape,) * 5,
        in_specs=[spec] * 7,
        out_specs=(spec,) * 5,
        compiler_params=params(),
        name="shampoo",
    )(grads, left_stats, right_stats, left_root, right_root, master, average)


def vector_step(values, grads):
    mean_sq = jnp.mean(grads * grads, axis=-1, keepdims=True)
    return values - RATE_VECTOR * grads * lax.rsqrt(mean_sq + 1e-06)


def scatter_position(owner, rank, coords, fast, slot_dev):
    if not fast:
        slots = slot_dev * lax.axis_size(("z", "x", "core"))
        return rank * slots + owner
    own_rank, own_x, unused = coords
    device = owner // slot_dev
    slot = owner % slot_dev
    core = device % 2
    x_at = (device // 2) % 2
    z_at = device // 4
    dy = rank ^ own_rank
    dx = x_at ^ own_x
    position = jnp.zeros_like(owner)
    for first, count, kind in SCATTER_PIECES:
        outer, inner = (dx, dy) if kind == "x" else (dy, dx)
        here = (
            32 * first
            + (((core * 2 + outer) * 2 + inner) * 4 + z_at) * count
            + slot
            - first
        )
        position = jnp.where((slot >= first) & (slot < first + count), here, position)
    return position


def scatter_sums(sums, fast):
    if not fast:
        return lax.psum_scatter(sums, ("mp", "z", "x", "core"), scatter_dimension=0, tiled=True)
    results = []
    for first, count, kind in SCATTER_PIECES:
        piece = sums[32 * first : 32 * (first + count)]
        mine = lax.psum_scatter(piece, "core", scatter_dimension=0, tiled=True)
        for axis in ("x", "mp") if kind == "x" else ("mp", "x"):
            half = mine.shape[0] // 2
            arrived = swap(mine[half:], axis)
            mine = (mine[:half].astype(f32) + arrived.astype(f32)).astype(bf16)
        results.append(lax.psum_scatter(mine, "z", scatter_dimension=0, tiled=True))
    return jnp.concatenate(results, axis=0)


def total(values):
    return lax.psum(values, ("mp", "z", "x", "core"))


def edges(first_rows, last_rows, ranks):
    before = lax.ppermute(last_rows, "mp", [(r, r + 1) for r in range(ranks - 1)])
    behind = lax.ppermute(first_rows, "mp", [(r + 1, r) for r in range(ranks - 1)])
    return before, behind


def local(fast):
    def run(
        stream, cotangent, segments, owners, master, average, left_stats, right_stats, left_root,
        right_root, gains, kernel,
    ):
        ranks = lax.axis_size("mp")
        rank = lax.axis_index("mp")
        coords = (rank, lax.axis_index("x"), lax.axis_index("core"))
        rows = stream.shape[0]
        slot_dev = master.shape[1]
        chips = lax.axis_size("z") * lax.axis_size("x") * 2
        slots = slot_dev * chips
        segment_ids = segments[0]
        group = segment_ids.shape[0]
        unused, blocks = offsets(ranks)

        owners_all = lax.all_gather(owners, "mp", axis=0, tiled=True)
        places = jnp.asarray(weight_places(ranks))
        match = owners_all[:, None, :] == jnp.arange(slots)[None, :, None]
        slot_places = jnp.sum(jnp.where(match, places[:, None, :], 0), axis=-1)
        rows_all = CHUNKS * D
        if slots > blocks:
            slot_places = jnp.where(jnp.any(match, axis=-1), slot_places, WEIGHT_BLOCKS)
            rows_all = rows_all + BLOCK
        slot_places = slot_places.reshape(-1).astype(jnp.int32)
        table = scatter_position(
            owners_all, jnp.arange(ranks)[:, None], coords, fast, slot_dev
        ).reshape(-1).astype(jnp.int32)

        slopes = 2.0 ** (-8.0 * (jnp.arange(HEADS).astype(f32) + 1.0) / HEADS)
        padded = jnp.pad(segment_ids, (HALO, HALO), constant_values=-1)
        wide_ids = jnp.pad(padded, (2, 2), constant_values=-2)
        tall = rows + 2 * HALO
        here = lax.dynamic_slice_in_dim(padded, rank * rows, tall)
        masks = jnp.stack(
            [
                (lax.dynamic_slice_in_dim(wide_ids, rank * rows + k, tall) == here).astype(f32)
                for k in range(KERNEL)
            ]
        )
        masks = jnp.broadcast_to(masks[:, :, None], (KERNEL, tall, 128))
        if fast:
            source_rows = [(rows, rank * rows), (rows, (1 - rank) * rows)]
        else:
            source_rows = [(group, 0)]
        spans = key_spans(segment_ids, rank, rows, source_rows)

        weights = gather_weights(
            master[0].astype(bf16), slot_places, coords, fast, rows_all
        )

        def gain(n):
            return gains[n : n + 1]

        after_first, pre_first, normed_attn = ffn_forward(
            stream, gain(0), gain(1), weights, UP1, DOWN1
        )
        if fast:
            other = swap(normed_attn, "mp")
            qkv = project(normed_attn, weights, QUERY, 3)
            other_kv = project(other, weights, KEY, 2)
            queries = qkv
            sources = [(qkv, HEADS, source_rows[0][1]), (other_kv, 0, source_rows[1][1])]
        else:
            other = lax.all_gather(normed_attn, "mp", axis=0, tiled=True)
            queries = project(normed_attn, weights, QUERY, 1)
            sources = [(project(other, weights, KEY, 2), 0, 0)]
        attended, logs = attention_forward(queries, sources, segment_ids, rank, spans, slopes)
        after_attn = project_out(attended, weights, OUT, after_first)
        before, behind = edges(after_attn[:HALO], after_attn[-HALO:], ranks)
        after_conv, linear, gate = conv_forward(
            after_attn, before, behind, gain(2), weights, kernel, masks
        )
        after_second, pre_second, output = ffn_forward(
            after_conv, gain(3), gain(4), weights, UP2, DOWN2
        )

        sums_shape = (ranks * slots, BLOCK, BLOCK)
        sums = jnp.zeros(sums_shape, bf16)
        grad_conv, gains_a, sums = ffn_backward(
            after_second, gain(4), [cotangent], None, after_conv, gain(3), pre_second, weights,
            UP2, DOWN2, sums, table, ranks,
        )
        before, behind = edges(
            grad_conv[:HALO].astype(bf16), grad_conv[-HALO:].astype(bf16), ranks
        )
        grad_attn, gains_b, tap_grads, sums = conv_backward(
            grad_conv, before, behind, after_attn, gain(2), linear, gate, weights, kernel, masks,
            sums, table, ranks,
        )
        mixed_grad, sums = project_out_back(
            grad_attn, weights, OUT, attended, sums, table, ranks
        )
        query_grad, key_grads, value_grads = attention_backward(
            queries, sources, segment_ids, rank, spans, slopes, logs, mixed_grad, attended
        )
        away = input_gradient(key_grads[-1], value_grads[-1], weights)
        if fast:
            arrived = swap(away, "mp")
            normed_sources = [normed_attn, other]
        else:
            arrived = lax.psum_scatter(away, "mp", scatter_dimension=0, tiled=True)
            normed_sources = [other]
        near, sums = projections_back(
            normed_attn, query_grad, list(zip(normed_sources, key_grads, value_grads)), fast,
            weights, sums, table, ranks,
        )
        stream_grad, gains_c, sums = ffn_backward(
            after_first, gain(1), [near, arrived], grad_attn, stream, gain(0), pre_first, weights,
            UP1, DOWN1, sums, table, ranks,
        )

        own_grads = scatter_sums(sums, fast)
        small = jnp.concatenate(
            [gains_c[1:2], gains_c[0:1], gains_b, gains_a[1:2], gains_a[0:1], tap_grads]
        )
        small = total(small)
        gain_grads, kernel_grads = small[:5], small[5:]
        block_grads, left_new, right_new, master_new, average_new = shampoo(
            own_grads, left_stats[0], right_stats[0], left_root[0], right_root[0], master[0],
            average[0],
        )
        return (
            output,
            stream_grad,
            block_grads[None],
            left_new[None],
            right_new[None],
            master_new[None],
            average_new[None],
            gain_grads,
            vector_step(gains, gain_grads),
            kernel_grads,
            vector_step(kernel, kernel_grads),
        )

    return run


def solution(mesh):
    ranks, pieces = mesh.shape["mp"], mesh.shape["dp"]
    fast = ranks == 2 and pieces == 16
    xs = 2 if fast else 1
    grid = Mesh(
        np.asarray(mesh.devices).reshape(ranks, pieces // (2 * xs), xs, 2), ("mp", "z", "x", "core")
    )
    dp = ("z", "x", "core")
    rows = P((*dp, "mp"), None)
    slots = P("mp", dp, None, None)
    return jax.shard_map(
        local(fast),
        mesh=grid,
        in_specs=(
            rows, rows, P(dp, None), P("mp", None), slots, slots, slots, slots, slots, slots, P(),
            P(),
        ),
        out_specs=(rows, rows, slots, slots, slots, slots, slots, P(), P(), P(), P()),
        check_vma=False,
    )
```

```python
import math

import jax
import jax.numpy as jnp
import numpy as np
from jax import lax
from jax.experimental import pallas as pl
from jax.experimental.pallas import tpu as pltpu
from jax.sharding import Mesh
from jax.sharding import PartitionSpec as P

D = 1024
FF = 4096
HEADS = 8
HEAD_DIM = 128
KERNEL = 5
STEP = 4
BLOCK = 128
HALO = 16
WIDE = 8

EPSILON = 1e-05
DECAY_STAT = 0.95
RATE_BLOCK = 0.02
RATE_VECTOR = 0.2
DECAY_AVERAGE = 0.9999
MASKED = -1e30
LOG2E = math.log2(math.e)
SCORE_SCALE = 1.0 / math.sqrt(HEAD_DIM)

f32 = jnp.float32
bf16 = jnp.bfloat16
ANY = pl.BlockSpec(memory_space=pl.ANY)
SMEM = pl.BlockSpec(memory_space=pltpu.SMEM)

MATRICES = [
    (0, 0, D, FF, True),
    (0, 4, FF, D, False),
    (1, 0, D, D, True),
    (1, 1, D, D, True),
    (1, 2, D, D, True),
    (1, 3, D, D, False),
    (2, 0, D, D, True),
    (2, 1, D, D, True),
    (2, 2, D, D, False),
    (3, 0, D, FF, True),
    (3, 4, FF, D, False),
]
UP1, DOWN1, QUERY, KEY, VALUE, OUT, CONV_VALUE, CONV_GATE, CONV_OUT, UP2, DOWN2 = range(11)
GROUPS = [(0, 2), (2, 6), (6, 9), (9, 11)]
GROUP_CHUNKS = [8, 4, 3, 8]


def at(matrix):
    return MATRICES[matrix][1]


ROUNDS = [4, 3, 4, 9, 3]
LARGE = 3
EARLY = [9, 6, 2]


def params(**kw):
    return pltpu.CompilerParams(vmem_limit_bytes=58 * 2**20, **kw)


def const_spec(shape):
    return pl.BlockSpec(shape, lambda *ids: (0,) * len(shape), pipeline_mode=pl.Buffered(1))


def row_tile(rows):
    return 256 if rows % 256 == 0 else 128


def cost(flops, moved):
    return pl.CostEstimate(flops=int(flops), bytes_accessed=int(moved), transcendentals=0)


def offsets(ranks):
    out = []
    offset = 0
    for unused, unused_chunk, height, breadth, by_columns in MATRICES:
        out.append(offset)
        offset = offset + height * breadth // (BLOCK * BLOCK * ranks)
    return out, offset


def block_number(matrix, row_block, column_block, ranks):
    starts, total = offsets(ranks)
    unused, unused_chunk, height, breadth, by_columns = MATRICES[matrix]
    if by_columns:
        part = breadth // BLOCK // ranks
        return (
            (column_block // part) * total + starts[matrix] + row_block * part + column_block % part
        )
    part = height // BLOCK // ranks
    breadth_blocks = breadth // BLOCK
    return (
        (row_block // part) * total
        + starts[matrix]
        + (row_block % part) * breadth_blocks
        + column_block
    )


def weight_places(ranks):
    unused, total = offsets(ranks)
    places = np.zeros((ranks * total,), np.int32)
    for matrix, (unused, chunk, height, breadth, by_columns) in enumerate(MATRICES):
        for row in range(height // BLOCK):
            for column in range(breadth // BLOCK):
                place = ((chunk + column // WIDE) * 8 + row) * WIDE + column % WIDE
                places[block_number(matrix, row, column, ranks)] = place
    return places.reshape(ranks, total)


def copy_in_place(out, source, place, sem):
    row = pl.multiple_of((place // WIDE) * BLOCK, BLOCK)
    column = pl.multiple_of((place % WIDE) * BLOCK, BLOCK)
    pltpu.make_async_copy(
        source, out.at[pl.ds(row, BLOCK), pl.ds(column, BLOCK)], sem
    ).start()


def unsort(slots, sources, places, chunks, listed):
    count = sources.shape[0]
    each = max(n for n in range(1, 65) if count % n == 0)
    steps = count // each

    def body(source_ref, place_ref, slots_ref, *rest):
        out = rest[0]
        list_ref = rest[1] if listed else None
        held, read_sem, write_sem, list_sem = rest[-4:]
        step = pl.program_id(0)
        slot = lax.rem(step, 2)

        def read(number, into):
            def one(n, unused):
                pltpu.make_async_copy(
                    slots_ref.at[source_ref[number * each + n]], held.at[into, n], read_sem.at[into]
                ).start()
                return unused

            lax.fori_loop(0, each, one, 0)

        def written(number, into):
            pltpu.make_async_copy(held.at[into], held.at[into], write_sem.at[into]).wait()
            if listed:
                pltpu.make_async_copy(held.at[into], held.at[into], list_sem.at[into]).wait()

        @pl.when(step == 0)
        def _():
            read(0, 0)

        @pl.when(step >= 1)
        def _():
            written(step - 1, 1 - slot)

        @pl.when(step + 1 < steps)
        def _():
            read(step + 1, 1 - slot)

        pltpu.make_async_copy(held.at[slot], held.at[slot], read_sem.at[slot]).wait()

        def one(n, unused):
            copy_in_place(out, held.at[slot, n], place_ref[step * each + n], write_sem.at[slot])
            return unused

        lax.fori_loop(0, each, one, 0)
        if listed:
            pltpu.make_async_copy(
                held.at[slot], list_ref.at[pl.ds(step * each, each)], list_sem.at[slot]
            ).start()

        @pl.when(step == steps - 1)
        def _():
            written(step, slot)

    shapes = [jax.ShapeDtypeStruct((chunks * D, D), bf16)]
    if listed:
        shapes.append(jax.ShapeDtypeStruct((count, BLOCK, BLOCK), bf16))
    return pl.pallas_call(
        body,
        grid=(steps,),
        out_shape=tuple(shapes),
        in_specs=[SMEM, SMEM, ANY],
        out_specs=(ANY,) * len(shapes),
        scratch_shapes=[
            pltpu.VMEM((2, each, BLOCK, BLOCK), bf16),
            pltpu.SemaphoreType.DMA((2,)),
            pltpu.SemaphoreType.DMA((2,)),
            pltpu.SemaphoreType.DMA((2,)),
        ],
        compiler_params=params(has_side_effects=True),
        cost_estimate=cost(0, 3 * count * BLOCK * BLOCK * 2),
        name="unsort",
    )(sources, places, slots)


def place_weights(weights, arrays, bases, places):
    count = arrays[0].shape[0]
    number = len(arrays)
    each = max(n for n in range(1, 128 // number + 1) if count % n == 0)

    def body(table, base_ref, *rest):
        sources = rest[:number]
        out, sem = rest[-2], rest[-1]
        start = pl.program_id(0) * each

        def one(t, unused):
            for a, source in enumerate(sources):
                copy_in_place(out, source.at[t], table[base_ref[a] + start + t], sem.at[a])
            return unused

        lax.fori_loop(0, each, one, 0)
        for a, source in enumerate(sources):
            pltpu.make_async_copy(source, source, sem.at[a]).wait()

    operands = [places, jnp.stack(bases).astype(jnp.int32), *arrays, weights]
    return pl.pallas_call(
        body,
        grid=(count // each,),
        out_shape=jax.ShapeDtypeStruct(weights.shape, bf16),
        in_specs=[SMEM, SMEM]
        + [pl.BlockSpec((each, BLOCK, BLOCK), lambda n: (n, 0, 0))] * number
        + [ANY],
        out_specs=ANY,
        scratch_shapes=[pltpu.SemaphoreType.DMA((number,))],
        input_output_aliases={len(operands) - 1: 0},
        compiler_params=params(has_side_effects=True),
        cost_estimate=cost(0, 2 * number * count * BLOCK * BLOCK * 2),
        name="place_weights",
    )(*operands)


PAIR = [(0, 1), (1, 0)]
MOVES = {
    "x": ("x", PAIR),
    "mp": ("mp", PAIR),
    "core": ("core", PAIR),
    "near": ("z", [(0, 1), (1, 0), (2, 3), (3, 2)]),
    "far": ("z", [(0, 2), (2, 0), (1, 3), (3, 1)]),
    "both": (("x", "core"), [(n, 3 - n) for n in range(4)]),
    "across": (("mp", "z"), [(n, (n // 4 * 4) ^ 4 | (n % 4) ^ 1) for n in range(8)]),
}
for _step in (-3, -2, -1, 1, 2, 3):
    MOVES[_step] = ("z", [(z, z + _step) for z in range(4) if 0 <= z + _step < 4])


def swap(value, move):
    axis, pairs = MOVES[move]
    return lax.ppermute(value, axis, pairs)


def tied(*values):
    return lax.optimization_barrier(values)


def together(transfers, *held):
    values = tied(*[value for value, unused in transfers])
    arrived = [swap(value, move) for value, (unused, move) in zip(values, transfers)]
    out = tied(*arrived, *held)
    return list(out[: len(arrived)]), out[len(arrived) :]


def sigmoid(values):
    return 0.5 * jnp.tanh(0.5 * values) + 0.5


def norm_parts(values):
    center = values - jnp.mean(values, axis=-1, keepdims=True)
    spread = jnp.mean(center * center, axis=-1, keepdims=True)
    scale = lax.rsqrt(spread + EPSILON)
    return center * scale, scale


def norm(values, gain):
    return norm_parts(values)[0] * gain


def norm_back(values, gain, grad):
    hat, scale = norm_parts(values)
    inner = grad * gain
    mean_inner = jnp.mean(inner, axis=-1, keepdims=True)
    mean_hat = jnp.mean(inner * hat, axis=-1, keepdims=True)
    return (
        scale * (inner - mean_inner - hat * mean_hat),
        jnp.sum(grad * hat, axis=0, keepdims=True),
    )


def dot(a, b):
    return jnp.dot(a, b, preferred_element_type=f32)


def dot_right(a, b):
    return lax.dot_general(a, b, (((1,), (1,)), ((), ())), preferred_element_type=f32)


def dot_left(a, b):
    return lax.dot_general(a, b, (((0,), (0,)), ((), ())), preferred_element_type=f32)


def start_blocks(table, targets, source, sem, matrix, row_block, column_block, ranks):
    height, breadth = source.shape
    for i in range(height // BLOCK):
        for j in range(breadth // BLOCK):
            place = table[block_number(matrix, row_block + i, column_block + j, ranks)]
            block = source.at[pl.ds(i * BLOCK, BLOCK), pl.ds(j * BLOCK, BLOCK)]
            if len(targets) == 1:
                pltpu.make_async_copy(block, targets[0].at[place], sem).start()
                continue
            limit = targets[0].shape[0]

            @pl.when(place < limit)
            def _(place=place, block=block):
                pltpu.make_async_copy(block, targets[0].at[place], sem).start()

            @pl.when(place >= limit)
            def _(place=place, block=block):
                pltpu.make_async_copy(block, targets[1].at[place - limit], sem).start()


def wait_blocks(source, sem):
    pltpu.make_async_copy(source, source, sem).wait()


def ffn_forward(stream, gain, next_gain, weights, upper, lower):
    rows = stream.shape[0]
    tile = row_tile(rows)
    wide = D
    steps = FF // wide

    def body(x_ref, gain_ref, next_gain_ref, up_ref, down_ref, out_ref, pre_ref, next_ref, normed):
        step = pl.program_id(0)

        @pl.when(step == 0)
        def _():
            for t in range(0, rows, tile):
                x = x_ref[t : t + tile].astype(f32)
                normed[t : t + tile] = norm(x, gain_ref[...]).astype(bf16)
                out_ref[t : t + tile] = jnp.zeros((tile, D), f32)

        for t in range(0, rows, tile):
            pre = dot(normed[t : t + tile], up_ref[...])
            pre_ref[t : t + tile] = pre.astype(bf16)
            act = (pre * sigmoid(pre)).astype(bf16)
            out_ref[t : t + tile] += dot(act, down_ref[...])

        @pl.when(step == steps - 1)
        def _():
            for t in range(0, rows, tile):
                y = x_ref[t : t + tile].astype(f32) + 0.5 * out_ref[t : t + tile]
                out_ref[t : t + tile] = y
                next_ref[t : t + tile] = norm(y, next_gain_ref[...]).astype(bf16)

    return pl.pallas_call(
        body,
        grid=(steps,),
        out_shape=(
            jax.ShapeDtypeStruct((rows, D), f32),
            jax.ShapeDtypeStruct((rows, FF), bf16),
            jax.ShapeDtypeStruct((rows, D), bf16),
        ),
        in_specs=[
            const_spec((rows, D)),
            const_spec((1, D)),
            const_spec((1, D)),
            pl.BlockSpec((D, wide), lambda f: (at(upper) + f, 0)),
            pl.BlockSpec((wide, D), lambda f: (at(lower) + f, 0)),
        ],
        out_specs=(
            const_spec((rows, D)),
            pl.BlockSpec((rows, wide), lambda f: (0, f)),
            const_spec((rows, D)),
        ),
        scratch_shapes=[pltpu.VMEM((rows, D), bf16)],
        compiler_params=params(),
        cost_estimate=cost(4 * rows * D * FF, 4 * D * FF + 2 * rows * FF),
        name="ffn_forward",
    )(stream, gain, next_gain, weights, weights)


def norm_rows(values, gain):
    rows = values.shape[0]
    tile = row_tile(rows)

    def body(x_ref, gain_ref, out_ref):
        out_ref[...] = norm(x_ref[...].astype(f32), gain_ref[...]).astype(bf16)

    spec = pl.BlockSpec((tile, D), lambda t: (t, 0))
    return pl.pallas_call(
        body,
        grid=(rows // tile,),
        out_shape=jax.ShapeDtypeStruct((rows, D), bf16),
        in_specs=[spec, const_spec((1, D))],
        out_specs=spec,
        compiler_params=params(),
        name="norm_rows",
    )(values, gain)


def ffn_half(normed, weights, upper, lower, part, keep, pre=None):
    rows = normed.shape[0]
    tile = row_tile(rows)
    steps = FF // D // 2

    def body(part_ref, x_ref, up_ref, down_ref, *rest):
        out_ref = rest[-3] if keep else rest[-2]
        pre_ref = rest[-2]
        total = rest[-1]
        step = pl.program_id(0)
        for t in range(0, rows, tile):
            here = slice(t, t + tile)
            value = dot(x_ref[here], up_ref[...])
            if keep:
                pre_ref[here] = value.astype(bf16)
            act = (value * sigmoid(value)).astype(bf16)
            new = dot(act, down_ref[...])

            @pl.when(step == 0)
            def _(new=new, here=here):
                total[here] = new

            @pl.when(step == steps - 1)
            def _(new=new, here=here):
                out_ref[here] = (total[here] + new).astype(bf16)

    operands = [part.reshape(1), normed, weights, weights]
    specs = [
        pl.BlockSpec((rows, D), lambda f, p: (0, 0), pipeline_mode=pl.Buffered(1)),
        pl.BlockSpec((D, D), lambda f, p: (at(upper) + p[0] * steps + f, 0)),
        pl.BlockSpec((D, D), lambda f, p: (at(lower) + p[0] * steps + f, 0)),
    ]
    shapes = [jax.ShapeDtypeStruct((rows, D), bf16)]
    out_specs = [pl.BlockSpec((rows, D), lambda f, p: (0, 0), pipeline_mode=pl.Buffered(1))]
    aliases = {}
    if keep:
        shapes.append(jax.ShapeDtypeStruct((rows, FF), bf16))
        out_specs.append(pl.BlockSpec((rows, D), lambda f, p: (0, p[0] * steps + f)))
        if pre is not None:
            aliases = {len(operands): 1}
            operands.append(pre)
            specs.append(ANY)
    return pl.pallas_call(
        body,
        grid_spec=pltpu.PrefetchScalarGridSpec(
            num_scalar_prefetch=1,
            grid=(steps,),
            in_specs=specs,
            out_specs=tuple(out_specs),
            scratch_shapes=[pltpu.VMEM((rows, D), f32)],
        ),
        out_shape=tuple(shapes),
        input_output_aliases=aliases,
        compiler_params=params(),
        cost_estimate=cost(2 * rows * D * FF, 2 * D * FF),
        name="ffn_half",
    )(*operands)


def join(base, one, other, next_gain):
    rows = base.shape[0]
    tile = row_tile(rows)

    def body(base_ref, one_ref, other_ref, gain_ref, out_ref, next_ref):
        both = one_ref[...].astype(f32) + other_ref[...].astype(f32)
        y = base_ref[...].astype(f32) + 0.5 * both
        out_ref[...] = y
        next_ref[...] = norm(y, gain_ref[...]).astype(bf16)

    spec = pl.BlockSpec((tile, D), lambda t: (t, 0))
    return pl.pallas_call(
        body,
        grid=(rows // tile,),
        out_shape=(
            jax.ShapeDtypeStruct((rows, D), f32),
            jax.ShapeDtypeStruct((rows, D), bf16),
        ),
        in_specs=[spec, spec, spec, const_spec((1, D))],
        out_specs=(spec, spec),
        compiler_params=params(),
        name="join",
    )(base, one, other, next_gain)


def ffn_backward(
    after, after_gain, after_grads, base, stream, gain, pre, weights, upper, lower, sums, table,
    ranks, kept=None,
):
    rows = stream.shape[0]
    tile = row_tile(rows)
    wide = 512
    steps = FF // wide
    parts = len(after_grads)
    targets = len(sums)
    with_base = base is not None
    again = kept is not None

    def body(table_ref, *refs):
        refs = list(refs)
        after_ref, after_gain_ref = refs[0], refs[1]
        grad_refs = refs[2 : 2 + parts]
        at_ref = 2 + parts
        base_ref = None
        if with_base:
            base_ref = refs[at_ref]
            at_ref += 1
        x_ref, gain_ref, up_ref, down_ref, pre_ref = refs[at_ref : at_ref + 5]
        kept_ref = refs[at_ref + 5]
        out_ref, gains_ref = refs[-13 - targets : -11 - targets]
        sums_ref = refs[-11 - targets : -11]
        (
            half, normed, pre_here, normed_t, grad_sum, pre_grad, act_t, up_part, down_part, up_sem,
            down_sem,
        ) = refs[-11:]
        step = pl.program_id(0)

        @pl.when(step == 0)
        def _():
            gain_sum = jnp.zeros((1, D), f32)
            for t in range(0, rows, tile):
                here = slice(t, t + tile)
                grad = grad_refs[0][here].astype(f32)
                for other in grad_refs[1:]:
                    grad = grad + other[here].astype(f32)
                back, part = norm_back(after_ref[here], after_gain_ref[...], grad)
                gain_sum = gain_sum + part
                if with_base:
                    back = back + base_ref[here]
                out_ref[here] = back
                half[here] = (0.5 * back).astype(bf16)
                low = norm(x_ref[here].astype(f32), gain_ref[...]).astype(bf16)
                if again:
                    normed[here] = low
                normed_t[:, here] = low.T
                grad_sum[here] = jnp.zeros((tile, D), f32)
            gains_ref[0:1] = gain_sum

        if again:

            @pl.when(step // (steps // 2) == kept_ref[0])
            def _():
                pre_here[...] = pre_ref[...]

            @pl.when(step // (steps // 2) != kept_ref[0])
            def _():
                for t in range(0, rows, tile):
                    here = slice(t, t + tile)
                    pre_here[here] = dot(normed[here], up_ref[...]).astype(bf16)

        for t in range(0, rows, tile):
            here = slice(t, t + tile)
            act_grad = dot_right(half[here], down_ref[...])
            pre_act = (pre_here if again else pre_ref)[here].astype(f32)
            sigma = sigmoid(pre_act)
            act = pre_act * sigma
            act_t[:, here] = act.astype(bf16).T
            slope = sigma + act * (1.0 - sigma)
            moved = (act_grad * slope).astype(bf16)
            pre_grad[here] = moved
            grad_sum[here] += dot_right(moved, up_ref[...])

        @pl.when(step >= 1)
        def _():
            wait_blocks(up_part, up_sem)
            wait_blocks(down_part, down_sem)

        for t in range(0, D, 256):
            up_part[t : t + 256] = dot(normed_t[t : t + 256], pre_grad[...]).astype(bf16)
        for t in range(0, wide, 256):
            down_part[t : t + 256] = dot(act_t[t : t + 256], half[...]).astype(bf16)
        start_blocks(
            table_ref, sums_ref, up_part, up_sem, upper, 0, step * 4, ranks
        )
        start_blocks(
            table_ref, sums_ref, down_part, down_sem, lower, step * 4, 0, ranks
        )

        @pl.when(step == steps - 1)
        def _():
            gain_sum = jnp.zeros((1, D), f32)
            for t in range(0, rows, tile):
                here = slice(t, t + tile)
                back, part = norm_back(x_ref[here].astype(f32), gain_ref[...], grad_sum[here])
                gain_sum = gain_sum + part
                out_ref[here] += back
            gains_ref[1:2] = gain_sum
            wait_blocks(up_part, up_sem)
            wait_blocks(down_part, down_sem)

    operands = [table, after, after_gain, *after_grads]
    specs = [SMEM, const_spec((rows, D)), const_spec((1, D))] + [const_spec((rows, D))] * parts
    if with_base:
        operands.append(base)
        specs.append(const_spec((rows, D)))
    operands += [stream, gain, weights, weights]
    specs += [
        const_spec((rows, D)),
        const_spec((1, D)),
        pl.BlockSpec((D, wide), lambda f: (at(upper) + f // 2, f % 2)),
        pl.BlockSpec((wide, D), lambda f: (at(lower) * 2 + f, 0)),
    ]
    operands.append(pre)
    specs.append(pl.BlockSpec((rows, wide), lambda f: (0, f)))
    if again:
        operands.append(kept.reshape(1))
        specs.append(SMEM)
    aliases = {}
    if not isinstance(sums[0], tuple):
        for n, target in enumerate(sums):
            aliases[len(operands)] = 2 + n
            operands.append(target)
            specs.append(ANY)
        sums = [target.shape for target in sums]
    return pl.pallas_call(
        body,
        grid=(steps,),
        out_shape=(
            jax.ShapeDtypeStruct((rows, D), f32),
            jax.ShapeDtypeStruct((2, D), f32),
            *[jax.ShapeDtypeStruct(shape, bf16) for shape in sums],
        ),
        in_specs=specs,
        out_specs=(const_spec((rows, D)), const_spec((2, D))) + (ANY,) * targets,
        scratch_shapes=[
            pltpu.VMEM((rows, D), bf16),
            pltpu.VMEM((rows, D) if again else (16, 128), bf16),
            pltpu.VMEM((rows, wide) if again else (16, 128), bf16),
            pltpu.VMEM((D, rows), bf16),
            pltpu.VMEM((rows, D), f32),
            pltpu.VMEM((rows, wide), bf16),
            pltpu.VMEM((wide, rows), bf16),
            pltpu.VMEM((D, wide), bf16),
            pltpu.VMEM((wide, D), bf16),
            pltpu.SemaphoreType.DMA,
            pltpu.SemaphoreType.DMA,
        ],
        input_output_aliases=aliases,
        compiler_params=params(has_side_effects=True),
        cost_estimate=cost(8 * rows * D * FF, 8 * D * FF + 2 * rows * FF),
        name="ffn_backward",
    )(*operands)


def project(values, weights, first, count, part=None, parts=1, into=None):
    rows = values.shape[0]
    tile = row_tile(rows)
    wide = D

    def body(part_ref, x_ref, w_ref, *rest):
        out_ref = rest[-1]
        for t in range(0, rows, tile):
            out_ref[t : t + tile] = dot(x_ref[t : t + tile], w_ref[...]).astype(bf16)

    operands = [jnp.asarray(0 if part is None else part, jnp.int32).reshape(1), values, weights]
    specs = [
        pl.BlockSpec((rows, D), lambda f, part: (0, 0), pipeline_mode=pl.Buffered(1)),
        pl.BlockSpec((D, wide), lambda f, part: (at(first) + f, 0)),
    ]
    aliases = {}
    if into is not None:
        aliases = {3: 0}
        operands.append(into)
        specs.append(ANY)
    return pl.pallas_call(
        body,
        grid_spec=pltpu.PrefetchScalarGridSpec(
            num_scalar_prefetch=1,
            grid=(count,),
            in_specs=specs,
            out_specs=pl.BlockSpec((rows, wide), lambda f, part: (part[0], f)),
        ),
        out_shape=jax.ShapeDtypeStruct((parts * rows, count * D), bf16),
        input_output_aliases=aliases,
        compiler_params=params(),
        cost_estimate=cost(2 * rows * D * D * count, 2 * count * D * (D + rows)),
        name="project",
    )(*operands)


def project_out(values, weights, matrix, stream):
    rows = values.shape[0]
    tile = row_tile(rows)

    def body(x_ref, w_ref, s_ref, out_ref):
        out_ref[...] = s_ref[...] + dot(x_ref[...], w_ref[...])

    return pl.pallas_call(
        body,
        grid=(rows // tile,),
        out_shape=jax.ShapeDtypeStruct((rows, D), f32),
        in_specs=[
            pl.BlockSpec((tile, D), lambda t: (t, 0)),
            pl.BlockSpec((D, D), lambda t: (at(matrix), 0)),
            pl.BlockSpec((tile, D), lambda t: (t, 0)),
        ],
        out_specs=pl.BlockSpec((tile, D), lambda t: (t, 0)),
        compiler_params=params(),
        cost_estimate=cost(2 * rows * D * D, 2 * D * D + 10 * rows * D),
        name="project_out",
    )(values, weights, stream)


def project_out_back(grad, weights, matrix, attended, sums, table, ranks):
    rows = grad.shape[0]
    tile = row_tile(rows)
    wide = 512

    targets = len(sums)

    def body(table_ref, g_ref, w_ref, a_ref, *refs):
        out_ref = refs[targets]
        sums_ref = refs[targets + 1 : 2 * targets + 1]
        low, part, sem = refs[2 * targets + 1 :]
        step = pl.program_id(0)

        @pl.when(step == 0)
        def _():
            for t in range(0, rows, tile):
                low[t : t + tile] = g_ref[t : t + tile].astype(bf16)

        for t in range(0, rows, tile):
            out_ref[t : t + tile] = dot_right(low[t : t + tile], w_ref[...]).astype(bf16)
        for t in range(0, wide, 256):
            part[step, t : t + 256] = dot_left(a_ref[:, t : t + 256], low[...]).astype(bf16)
        start_blocks(table_ref, sums_ref, part.at[step], sem.at[step], matrix, step * 4, 0, ranks)

        @pl.when(step == 1)
        def _():
            for s in range(2):
                wait_blocks(part.at[s], sem.at[s])

    return pl.pallas_call(
        body,
        grid=(2,),
        out_shape=(
            jax.ShapeDtypeStruct((rows, D), bf16),
            *[jax.ShapeDtypeStruct(target.shape, bf16) for target in sums],
        ),
        in_specs=[
            SMEM,
            const_spec((rows, D)),
            pl.BlockSpec((wide, D), lambda f: (at(matrix) * 2 + f, 0)),
            pl.BlockSpec((rows, wide), lambda f: (0, f)),
        ]
        + [ANY] * targets,
        out_specs=(pl.BlockSpec((rows, wide), lambda f: (0, f)),) + (ANY,) * targets,
        scratch_shapes=[
            pltpu.VMEM((rows, D), bf16),
            pltpu.VMEM((2, wide, D), bf16),
            pltpu.SemaphoreType.DMA((2,)),
        ],
        input_output_aliases={4 + n: 1 + n for n in range(targets)},
        compiler_params=params(has_side_effects=True),
        cost_estimate=cost(4 * rows * D * D, 4 * D * D + 8 * rows * D),
        name="project_out_back",
    )(table, grad, weights, attended, *sums)


def input_gradient(key_grad, value_grad, weights, part, rows):
    tile = row_tile(rows)
    steps = rows // tile

    def body(part_ref, k_ref, v_ref, wk_ref, wv_ref, out_ref):
        out_ref[...] = (
            dot_right(k_ref[...], wk_ref[...]) + dot_right(v_ref[...], wv_ref[...])
        ).astype(bf16)

    return pl.pallas_call(
        body,
        grid_spec=pltpu.PrefetchScalarGridSpec(
            num_scalar_prefetch=1,
            grid=(steps,),
            in_specs=[
                pl.BlockSpec((tile, D), lambda t, part: (part[0] * steps + t, 0)),
                pl.BlockSpec((tile, D), lambda t, part: (part[0] * steps + t, 0)),
                pl.BlockSpec((D, D), lambda t, part: (at(KEY), 0)),
                pl.BlockSpec((D, D), lambda t, part: (at(VALUE), 0)),
            ],
            out_specs=pl.BlockSpec((tile, D), lambda t, part: (t, 0)),
        ),
        out_shape=jax.ShapeDtypeStruct((rows, D), bf16),
        compiler_params=params(),
        cost_estimate=cost(4 * rows * D * D, 4 * D * D + 6 * rows * D),
        name="input_gradient",
    )(part.reshape(1), key_grad, value_grad, weights, weights)


def projections_back(
    normed, query_grad, key_grad, value_grad, sources, own_keys, weights, sums, table, ranks
):
    rows = normed.shape[0]
    tile = row_tile(rows)
    wide = 512
    count = len(sources)
    targets = len(sums)
    lengths = [source[0].shape[0] for source in sources]

    def body(part_ref, table_ref, n_ref, q_ref, *refs):
        normed_refs = refs[:count]
        key_refs = refs[count : 2 * count]
        value_refs = refs[2 * count : 3 * count]
        w_ref = refs[3 * count]
        outs = refs[3 * count + 1 + targets :]
        out_ref, sums_ref, scratch = outs[0], outs[1 : 1 + targets], outs[1 + targets :]
        own_t = scratch[0]
        source_t = scratch[1 : 1 + count]
        part, sem = scratch[1 + count :]
        step = pl.program_id(0)
        slot = lax.rem(step, 2)

        @pl.when(step == 0)
        def _():
            for t in range(0, rows, tile):
                own_t[:, t : t + tile] = n_ref[t : t + tile].T
            for n_from, n_to, length in zip(normed_refs, source_t, lengths):
                small = row_tile(length)
                for t in range(0, length, small):
                    n_to[:, t : t + small] = n_from[t : t + small].T

        @pl.when(step >= 2)
        def _():
            wait_blocks(part.at[slot], sem.at[slot])

        @pl.when(step < 2)
        def _():
            for t in range(0, rows, tile):
                new = dot_right(q_ref[t : t + tile], w_ref[...])

                @pl.when(step == 0)
                def _():
                    out_ref[t : t + tile] = new

                @pl.when(step == 1)
                def _():
                    out_ref[t : t + tile] += new

            for t in range(0, D, 256):
                part[slot, t : t + 256] = dot(own_t[t : t + 256], q_ref[...]).astype(bf16)
            start_blocks(
                table_ref, sums_ref, part.at[slot], sem.at[slot], QUERY, 0, lax.rem(step, 2) * 4,
                ranks,
            )

        def other(grad_refs, matrix):
            if own_keys:
                for t in range(0, rows, tile):
                    out_ref[t : t + tile] += dot_right(grad_refs[0][t : t + tile], w_ref[...])
            for t in range(0, D, 256):
                total = dot(source_t[0][t : t + 256], grad_refs[0][...])
                for n_t, grad_ref in zip(source_t[1:], grad_refs[1:]):
                    total = total + dot(n_t[t : t + 256], grad_ref[...])
                part[slot, t : t + 256] = total.astype(bf16)
            start_blocks(
                table_ref, sums_ref, part.at[slot], sem.at[slot], matrix, 0, lax.rem(step, 2) * 4,
                ranks,
            )

        @pl.when((step >= 2) & (step < 4))
        def _():
            other(key_refs, KEY)

        @pl.when(step >= 4)
        def _():
            other(value_refs, VALUE)

        @pl.when(step == 5)
        def _():
            for s in range(2):
                wait_blocks(part.at[s], sem.at[s])

    parts = jnp.stack([jnp.asarray(source[1], jnp.int32) for source in sources])
    operands = [parts, table, normed, query_grad]

    def whole(shape):
        return pl.BlockSpec(shape, lambda f, part: (0, 0), pipeline_mode=pl.Buffered(1))

    specs = [
        SMEM,
        whole((rows, D)),
        pl.BlockSpec((rows, wide), lambda f, part: (0, jnp.minimum(f, 1))),
    ]
    operands += [source[0] for source in sources]
    specs += [whole((length, D)) for length in lengths]
    for grads, first in ((key_grad, 2), (value_grad, 4)):
        for n, length in enumerate(lengths):
            operands.append(grads)
            specs.append(
                pl.BlockSpec(
                    (length, wide),
                    lambda f, part, n=n, first=first: (part[n], jnp.clip(f - first, 0, 1)),
                )
            )
    operands += [weights, *sums]
    specs += [pl.BlockSpec((D, wide), lambda f, part: (at(QUERY) + f // 2, f % 2))]
    specs += [ANY] * targets
    return pl.pallas_call(
        body,
        grid_spec=pltpu.PrefetchScalarGridSpec(
            num_scalar_prefetch=1,
            grid=(6,),
            in_specs=specs,
            out_specs=(whole((rows, D)),) + (ANY,) * targets,
            scratch_shapes=[pltpu.VMEM((D, rows), bf16)]
            + [pltpu.VMEM((D, length), bf16) for length in lengths]
            + [pltpu.VMEM((2, D, wide), bf16), pltpu.SemaphoreType.DMA((2,))],
        ),
        out_shape=(
            jax.ShapeDtypeStruct((rows, D), f32),
            *[jax.ShapeDtypeStruct(target.shape, bf16) for target in sums],
        ),
        input_output_aliases={len(operands) - targets + n: 1 + n for n in range(targets)},
        compiler_params=params(has_side_effects=True),
        cost_estimate=cost(
            (4 * rows + sum(4 * length for length in lengths) + 4 * rows) * D * D, 30 * D * D
        ),
        name="projections_back",
    )(*operands)


def attention_tiles(rows):
    return (512 if rows % 512 == 0 else row_tile(rows)), 256


def key_windows(segments, rank, rows):
    tall, broad = attention_tiles(rows)
    group = segments.shape[0]
    blocks = rows // tall
    own = lax.dynamic_slice_in_dim(segments, rank * rows, rows).reshape(blocks, tall)
    low = jnp.sum(segments[None, :] < own[:, :1], axis=1)
    high = jnp.sum(segments[None, :] <= own[:, -1:], axis=1)
    start = low // 128 * 128
    steps = (high - start + broad - 1) // broad
    start = jnp.minimum(start, group - steps * broad)
    return jnp.stack([start, steps], axis=-1).reshape(-1).astype(jnp.int32)

def attention_forward(queries, keys, segments, rank, windows, slopes):
    rows = queries.shape[0]
    group = keys.shape[0]
    tall, broad = attention_tiles(rows)
    most = group // broad
    own = lax.dynamic_slice_in_dim(segments, rank * rows, rows).reshape(rows, 1)

    def body(rank_ref, window_ref, slope_ref, q_ref, own_ref, key_ref, value_ref, columns_ref, out_ref, total_ref, scores):
        head, block = pl.program_id(0), pl.program_id(1)
        slope = slope_ref[head] * LOG2E
        start = window_ref[2 * block]
        steps = window_ref[2 * block + 1]
        first = rank_ref[0] * rows + block * tall
        query = q_ref[...]
        apart = (
            lax.broadcasted_iota(jnp.int32, (tall, broad), 0)
            - lax.broadcasted_iota(jnp.int32, (tall, broad), 1)
        ).astype(f32)

        def attend(count):
            peak = jnp.full((tall, 128), MASKED, f32)
            for b in range(count):
                begin = pl.multiple_of(start + b * broad, 128)
                here = pl.ds(begin, broad)
                score = dot_right(query, key_ref[here, :]) * (SCORE_SCALE * LOG2E)
                score = score - slope * jnp.abs(apart + (first - begin).astype(f32))
                score = jnp.where(own_ref[...] == columns_ref[:, here], score, MASKED)
                scores[:, b * broad : (b + 1) * broad] = score
                for lane in range(0, broad, 128):
                    peak = jnp.maximum(peak, score[:, lane : lane + 128])
            top = jnp.max(peak, axis=-1, keepdims=True)
            total = jnp.zeros((tall, 128), f32)
            mixed = jnp.zeros((tall, HEAD_DIM), f32)
            for b in range(count):
                here = pl.ds(pl.multiple_of(start + b * broad, 128), broad)
                shifted = jnp.exp2(scores[:, b * broad : (b + 1) * broad] - top)
                for lane in range(0, broad, 128):
                    total = total + shifted[:, lane : lane + 128]
                mixed = mixed + dot(shifted.astype(bf16), value_ref[here, :])
            total = jnp.sum(total, axis=-1, keepdims=True)
            out_ref[...] = (mixed / total).astype(bf16)
            logs = jnp.broadcast_to(top + jnp.log2(total), (tall, 128))
            total_ref[...] = logs.T[0:1, :].reshape(1, 1, tall)

        for count in range(1, most + 1):
            @pl.when(steps == count)
            def _(count=count):
                attend(count)

    return pl.pallas_call(
        body,
        grid=(HEADS, rows // tall),
        out_shape=(
            jax.ShapeDtypeStruct((rows, D), bf16),
            jax.ShapeDtypeStruct((HEADS, 1, rows), f32),
        ),
        in_specs=[
            SMEM, SMEM, SMEM,
            pl.BlockSpec((tall, HEAD_DIM), lambda h, q: (q, h)),
            pl.BlockSpec((tall, 1), lambda h, q: (q, 0)),
            pl.BlockSpec((group, HEAD_DIM), lambda h, q: (0, h)),
            pl.BlockSpec((group, HEAD_DIM), lambda h, q: (0, HEADS + h)),
            const_spec((1, group)),
        ],
        out_specs=(
            pl.BlockSpec((tall, HEAD_DIM), lambda h, q: (q, h)),
            pl.BlockSpec((1, 1, tall), lambda h, q: (h, 0, q)),
        ),
        scratch_shapes=[pltpu.VMEM((tall, group), f32)],
        compiler_params=params(),
        name="attention_forward",
    )(jnp.asarray(rank,jnp.int32).reshape(1), windows, slopes, queries, own, keys, keys, segments.reshape(1, group))

def attention_backward(queries, keys, segments, rank, windows, slopes, logs, grads, attended):
    rows = queries.shape[0]
    group = keys.shape[0]
    tall, broad = attention_tiles(rows)
    most = group // broad
    own = lax.dynamic_slice_in_dim(segments, rank * rows, rows).reshape(1, rows)

    def body(rank_ref, window_ref, slope_ref, q_ref, own_ref, log_ref, grad_ref, att_ref, key_ref, value_ref, columns_ref,
             out_ref, key_out, value_out, key_sum, value_sum):
        head, block = pl.program_id(0), pl.program_id(1)
        slope = slope_ref[head] * LOG2E
        start = window_ref[2 * block]
        steps = window_ref[2 * block + 1]
        first = rank_ref[0] * rows + block * tall

        @pl.when(block == 0)
        def _():
            key_sum[...] = jnp.zeros(key_sum.shape, f32)
            value_sum[...] = jnp.zeros(value_sum.shape, f32)

        query = q_ref[...]
        grad = grad_ref[...]
        products = grad.astype(f32) * att_ref[...].astype(f32)
        delta = jnp.broadcast_to(jnp.sum(products, axis=-1, keepdims=True), (tall, 128)).T[0:1, :]
        log_row = log_ref[0]
        apart = (
            lax.broadcasted_iota(jnp.int32, (broad, tall), 1)
            - lax.broadcasted_iota(jnp.int32, (broad, tall), 0)
        ).astype(f32)

        def attend(count):
            query_sum = jnp.zeros((tall, HEAD_DIM), f32)
            for b in range(count):
                begin = pl.multiple_of(start + b * broad, 128)
                here = pl.ds(begin, broad)
                key = key_ref[here, :]
                score = dot_right(key, query) * (SCORE_SCALE * LOG2E)
                score = score - slope * jnp.abs(apart + (first - begin).astype(f32))
                score = jnp.where(own_ref[...] == columns_ref[here, :], score, MASKED)
                probs = jnp.exp2(score - log_row)
                prob_grad = dot_right(value_ref[here, :], grad)
                value_sum[here, :] += dot(probs.astype(bf16), grad)
                score_grad = (probs * (prob_grad - delta)).astype(bf16)
                key_sum[here, :] += dot(score_grad, query)
                query_sum = query_sum + dot_left(score_grad, key)
            out_ref[...] = (query_sum * SCORE_SCALE).astype(bf16)

        for count in range(1, most + 1):
            @pl.when(steps == count)
            def _(count=count):
                attend(count)

        @pl.when(block == pl.num_programs(1) - 1)
        def _():
            key_out[...] = (key_sum[...] * SCORE_SCALE).astype(bf16)
            value_out[...] = value_sum[...].astype(bf16)

    row_spec = pl.BlockSpec((tall, HEAD_DIM), lambda h, q: (q, h))
    key_spec = pl.BlockSpec((group, HEAD_DIM), lambda h, q: (0, h))
    return pl.pallas_call(
        body,
        grid=(HEADS, rows // tall),
        out_shape=(jax.ShapeDtypeStruct((rows, D), bf16),) + (jax.ShapeDtypeStruct((group, D), bf16),) * 2,
        in_specs=[
            SMEM, SMEM, SMEM,
            pl.BlockSpec((tall, HEAD_DIM), lambda h, q: (q, h)),
            pl.BlockSpec((1, tall), lambda h, q: (0, q)),
            pl.BlockSpec((1, 1, tall), lambda h, q: (h, 0, q)),
            row_spec, row_spec, key_spec,
            pl.BlockSpec((group, HEAD_DIM), lambda h, q: (0, HEADS + h)),
            const_spec((group, 1)),
        ],
        out_specs=(row_spec, key_spec, key_spec),
        scratch_shapes=[pltpu.VMEM((group, HEAD_DIM), f32)] * 2,
        compiler_params=params(),
        name="attention_backward",
    )(jnp.asarray(rank,jnp.int32).reshape(1), windows, slopes, queries, own, logs, grads, attended, keys, keys, segments.reshape(group, 1))


def conv_forward(stream, before, behind, gain, next_gain, weights, taps, masks):
    rows = stream.shape[0]
    tall = rows + 2 * HALO
    tile = row_tile(rows)
    wide = 256
    steps = D // wide

    def body(
        x_ref, before_ref, behind_ref, gain_ref, next_gain_ref, taps_ref, mask_ref, value_ref, gate_ref, out_w_ref,
        out_ref, linear_ref, gate_out_ref, next_ref, normed, glu,
    ):
        step = pl.program_id(0)

        @pl.when(step == 0)
        def _():
            gain_row = gain_ref[...]
            normed[0:HALO] = norm(before_ref[...], gain_row).astype(bf16)
            normed[rows + HALO :] = norm(behind_ref[...], gain_row).astype(bf16)
            for t in range(0, rows, tile):
                x = x_ref[t : t + tile]
                normed[HALO + t : HALO + t + tile] = norm(x, gain_row).astype(bf16)
                out_ref[t : t + tile] = x

        pieces = [(0, HALO)]
        pieces += [(HALO + t, tile) for t in range(0, rows, tile)]
        pieces += [(rows + HALO, HALO)]
        for t, size in pieces:
            here = slice(t, t + size)
            linear = dot(normed[here], value_ref[...])
            gate = dot(normed[here], gate_ref[...])
            linear_ref[here] = linear.astype(bf16)
            gate_out_ref[here] = gate.astype(bf16)
            glu[here] = linear * sigmoid(gate)
        for t in range(0, rows, tile):
            sums = []
            for half in range(0, wide, 128):
                total = jnp.zeros((tile, 128), f32)
                for k in range(KERNEL):
                    moved = glu[HALO + t + k - 2 : HALO + t + k - 2 + tile, half : half + 128]
                    if k != KERNEL // 2:
                        moved = moved * mask_ref[k, HALO + t : HALO + t + tile]
                    total = total + taps_ref[k : k + 1, half : half + 128] * moved
                sums.append(total)
            conved = jnp.concatenate(sums, axis=1)
            act = (conved * sigmoid(conved)).astype(bf16)
            out_ref[t : t + tile] += dot(act, out_w_ref[...])

        @pl.when(step == steps - 1)
        def _():
            for t in range(0, rows, tile):
                next_ref[t : t + tile] = norm(out_ref[t : t + tile], next_gain_ref[...]).astype(bf16)

    return pl.pallas_call(
        body,
        grid=(steps,),
        out_shape=(
            jax.ShapeDtypeStruct((rows, D), f32),
            jax.ShapeDtypeStruct((tall, D), bf16),
            jax.ShapeDtypeStruct((tall, D), bf16),
            jax.ShapeDtypeStruct((rows, D), bf16),
        ),
        in_specs=[
            const_spec((rows, D)),
            const_spec((HALO, D)),
            const_spec((HALO, D)),
            const_spec((1, D)),
            const_spec((1, D)),
            pl.BlockSpec((KERNEL, wide), lambda c: (0, c)),
            const_spec((KERNEL, tall, 128)),
            pl.BlockSpec((D, wide), lambda c: (at(CONV_VALUE), c)),
            pl.BlockSpec((D, wide), lambda c: (at(CONV_GATE), c)),
            pl.BlockSpec((wide, D), lambda c: (at(CONV_OUT) * 4 + c, 0)),
        ],
        out_specs=(
            const_spec((rows, D)),
            pl.BlockSpec((tall, wide), lambda c: (0, c)),
            pl.BlockSpec((tall, wide), lambda c: (0, c)),
            const_spec((rows, D)),
        ),
        scratch_shapes=[pltpu.VMEM((tall, D), bf16), pltpu.VMEM((tall, wide), f32)],
        compiler_params=params(),
        cost_estimate=cost(6 * rows * D * D, 6 * D * D + 12 * rows * D),
        name="conv_forward",
    )(stream, before, behind, gain, next_gain, taps, masks, weights, weights, weights)


def conv_backward(
    grad, before, behind, stream, gain, linear, gate, weights, taps, masks, sums, table, ranks
):
    rows = stream.shape[0]
    tall = rows + 2 * HALO
    tile = row_tile(rows)
    wide = 256
    steps = D // wide
    targets = len(sums)

    def body(
        table_ref, g_ref, before_ref, behind_ref, x_ref, gain_ref, linear_ref, gate_ref, taps_ref,
        mask_ref, value_ref, gate_w_ref, out_w_ref, *refs,
    ):
        out_ref, gain_out_ref, taps_out_ref = refs[targets : targets + 3]
        sums_ref = refs[targets + 3 : 2 * targets + 3]
        (
            low, normed_t, grad_sum, glu, conv_grad, act_t, value_grad, gate_grad, value_part,
            gate_part, out_part, value_sem, gate_sem, out_sem,
        ) = refs[2 * targets + 3 :]
        step = pl.program_id(0)
        slot = lax.rem(step, 2)

        @pl.when(step == 0)
        def _():
            low[0:HALO] = before_ref[...]
            low[rows + HALO :] = behind_ref[...]
            for t in range(0, rows, tile):
                here = slice(t, t + tile)
                low[HALO + t : HALO + t + tile] = g_ref[here].astype(bf16)
                normed_t[:, here] = norm(x_ref[here], gain_ref[...]).astype(bf16).T
                grad_sum[here] = jnp.zeros((tile, D), f32)

        pieces = [(0, HALO)]
        pieces += [(HALO + t, tile) for t in range(0, rows, tile)]
        pieces += [(rows + HALO, HALO)]
        for t, size in pieces:
            here = slice(t, t + size)
            glu[here] = linear_ref[here].astype(f32) * sigmoid(gate_ref[here].astype(f32))

        edge = 8
        pieces = [(HALO - edge, edge)]
        pieces += [(HALO + t, tile) for t in range(0, rows, tile)]
        pieces += [(rows + HALO, edge)]
        tap_sums = [[jnp.zeros((1, 128), f32) for k in range(KERNEL)] for half in range(2)]
        for t, size in pieces:
            totals, moved_rows = [], []
            for half in range(0, wide, 128):
                total = jnp.zeros((size, 128), f32)
                moved_rows.append([])
                for k in range(KERNEL):
                    moved = glu[t + k - 2 : t + k - 2 + size, half : half + 128]
                    if k != KERNEL // 2:
                        moved = moved * mask_ref[k, t : t + size]
                    moved_rows[-1].append(moved)
                    total = total + taps_ref[k : k + 1, half : half + 128] * moved
                totals.append(total)
            conved = jnp.concatenate(totals, axis=1)
            sigma = sigmoid(conved)
            act = conved * sigma
            if size == tile:
                act_t[:, t - HALO : t - HALO + size] = act.astype(bf16).T
                rows_grad = dot_right(low[t : t + size], out_w_ref[...])
            elif t < HALO:
                rows_grad = dot_right(low[0:HALO], out_w_ref[...])[edge:]
            else:
                rows_grad = dot_right(low[rows + HALO :], out_w_ref[...])[:edge]
            center = rows_grad * (sigma + act * (1.0 - sigma))
            conv_grad[t : t + size] = center
            if size == tile:
                for number in range(2):
                    lanes = center[:, number * 128 : (number + 1) * 128]
                    for k in range(KERNEL):
                        tap_sums[number][k] = tap_sums[number][k] + jnp.sum(
                            lanes * moved_rows[number][k], axis=0, keepdims=True
                        )

        for t in range(0, rows, tile):
            values, gates = [], []
            for number, half in enumerate(range(0, wide, 128)):
                lanes = slice(half, half + 128)
                start = HALO + t
                total = jnp.zeros((tile, 128), f32)
                for k in range(KERNEL):
                    moved = conv_grad[start + 2 - k : start + 2 - k + tile, lanes]
                    if k != KERNEL // 2:
                        moved = moved * mask_ref[KERNEL - 1 - k, start : start + tile]
                    total = total + taps_ref[k : k + 1, lanes] * moved
                sigma = sigmoid(gate_ref[start : start + tile, lanes].astype(f32))
                moved_value = total * sigma
                values.append(moved_value.astype(bf16))
                gates.append(
                    (
                        moved_value
                        * linear_ref[start : start + tile, lanes].astype(f32)
                        * (1.0 - sigma)
                    ).astype(bf16)
                )
            value_tile = jnp.concatenate(values, axis=1)
            gate_tile = jnp.concatenate(gates, axis=1)
            here = slice(t, t + tile)
            value_grad[here] = value_tile
            gate_grad[here] = gate_tile
            grad_sum[here] += dot_right(value_tile, value_ref[...]) + dot_right(
                gate_tile, gate_w_ref[...]
            )
        for k in range(KERNEL):
            taps_out_ref[k : k + 1] = jnp.concatenate([tap_sums[0][k], tap_sums[1][k]], axis=1)

        @pl.when(step >= 2)
        def _():
            wait_blocks(value_part.at[slot], value_sem.at[slot])
            wait_blocks(gate_part.at[slot], gate_sem.at[slot])
            wait_blocks(out_part.at[slot], out_sem.at[slot])

        for t in range(0, D, 256):
            value_part[slot, t : t + 256] = dot(normed_t[t : t + 256], value_grad[...]).astype(bf16)
            gate_part[slot, t : t + 256] = dot(normed_t[t : t + 256], gate_grad[...]).astype(bf16)
        out_part[slot] = dot(act_t[...], low[HALO : rows + HALO]).astype(bf16)
        start_blocks(
            table_ref, sums_ref, value_part.at[slot], value_sem.at[slot], CONV_VALUE, 0, step * 2,
            ranks,
        )
        start_blocks(
            table_ref, sums_ref, gate_part.at[slot], gate_sem.at[slot], CONV_GATE, 0, step * 2,
            ranks,
        )
        start_blocks(
            table_ref, sums_ref, out_part.at[slot], out_sem.at[slot], CONV_OUT, step * 2, 0, ranks
        )

        @pl.when(step == steps - 1)
        def _():
            gain_sum = jnp.zeros((1, D), f32)
            for t in range(0, rows, tile):
                here = slice(t, t + tile)
                back, part = norm_back(x_ref[here], gain_ref[...], grad_sum[here])
                gain_sum = gain_sum + part
                out_ref[here] = g_ref[here] + back
            gain_out_ref[...] = gain_sum
            for s in range(2):
                wait_blocks(value_part.at[s], value_sem.at[s])
                wait_blocks(gate_part.at[s], gate_sem.at[s])
                wait_blocks(out_part.at[s], out_sem.at[s])

    operands = [
        table, grad, before, behind, stream, gain, linear, gate, taps, masks, weights, weights,
        weights, *sums,
    ]
    return pl.pallas_call(
        body,
        grid=(steps,),
        out_shape=(
            jax.ShapeDtypeStruct((rows, D), f32),
            jax.ShapeDtypeStruct((1, D), f32),
            jax.ShapeDtypeStruct((KERNEL, D), f32),
            *[jax.ShapeDtypeStruct(target.shape, bf16) for target in sums],
        ),
        in_specs=[
            SMEM,
            const_spec((rows, D)),
            const_spec((HALO, D)),
            const_spec((HALO, D)),
            const_spec((rows, D)),
            const_spec((1, D)),
            pl.BlockSpec((tall, wide), lambda c: (0, c)),
            pl.BlockSpec((tall, wide), lambda c: (0, c)),
            pl.BlockSpec((KERNEL, wide), lambda c: (0, c)),
            const_spec((KERNEL, tall, 128)),
            pl.BlockSpec((D, wide), lambda c: (at(CONV_VALUE), c)),
            pl.BlockSpec((D, wide), lambda c: (at(CONV_GATE), c)),
            pl.BlockSpec((wide, D), lambda c: (at(CONV_OUT) * 4 + c, 0)),
        ]
        + [ANY] * targets,
        out_specs=(
            const_spec((rows, D)),
            const_spec((1, D)),
            pl.BlockSpec((KERNEL, wide), lambda c: (0, c)),
        )
        + (ANY,) * targets,
        scratch_shapes=[
            pltpu.VMEM((tall, D), bf16),
            pltpu.VMEM((D, rows), bf16),
            pltpu.VMEM((rows, D), f32),
            pltpu.VMEM((tall, wide), f32),
            pltpu.VMEM((tall, wide), f32),
            pltpu.VMEM((wide, rows), bf16),
            pltpu.VMEM((rows, wide), bf16),
            pltpu.VMEM((rows, wide), bf16),
            pltpu.VMEM((2, D, wide), bf16),
            pltpu.VMEM((2, D, wide), bf16),
            pltpu.VMEM((2, wide, D), bf16),
            pltpu.SemaphoreType.DMA((2,)),
            pltpu.SemaphoreType.DMA((2,)),
            pltpu.SemaphoreType.DMA((2,)),
        ],
        input_output_aliases={len(operands) - targets + n: 3 + n for n in range(targets)},
        compiler_params=params(has_side_effects=True),
        cost_estimate=cost(12 * rows * D * D, 12 * D * D + 16 * rows * D),
        name="conv_backward",
    )(*operands)


def shampoo(grads, arrivals, left_stats, right_stats, left_root, right_root, master, average):
    slots = master.shape[0]
    each = 8
    steps = (slots + each - 1) // each
    arrivals = jnp.pad(arrivals, (0, steps * each - slots))
    old_bias = 1.0 - DECAY_AVERAGE ** (STEP - 1)
    new_bias = 1.0 - DECAY_AVERAGE**STEP

    def body(index_ref, *refs):
        g_refs = refs[:each]
        ls_ref, rs_ref, lr_ref, rr_ref, m_ref, a_ref, go, lo, ro, mo, ao = refs[each:]
        for n in range(each):
            grad = g_refs[n][0]
            go[n] = grad.astype(f32)
            lo[n] = DECAY_STAT * ls_ref[n] + (1.0 - DECAY_STAT) * dot_right(grad, grad)
            ro[n] = DECAY_STAT * rs_ref[n] + (1.0 - DECAY_STAT) * dot_left(grad, grad)
            inner = dot(grad, rr_ref[n].astype(bf16))
            turned = dot(lr_ref[n].astype(bf16), inner.astype(bf16))
            mean_sq = jnp.mean(turned * turned, axis=(0, 1), keepdims=True)
            new = m_ref[n] - RATE_BLOCK * turned * lax.rsqrt(mean_sq + 1e-06)
            mo[n] = new
            ao[n] = (DECAY_AVERAGE * old_bias / new_bias) * a_ref[n] + (
                (1.0 - DECAY_AVERAGE) / new_bias
            ) * new

    spec = pl.BlockSpec((each, BLOCK, BLOCK), lambda s, index: (s, 0, 0))
    grad_specs = [
        pl.BlockSpec((1, BLOCK, BLOCK), lambda s, index, n=n: (index[s * each + n], 0, 0))
        for n in range(each)
    ]
    shape = jax.ShapeDtypeStruct((slots, BLOCK, BLOCK), f32)
    return pl.pallas_call(
        body,
        grid_spec=pltpu.PrefetchScalarGridSpec(
            num_scalar_prefetch=1,
            grid=(steps,),
            in_specs=grad_specs + [spec] * 6,
            out_specs=(spec,) * 5,
        ),
        out_shape=(shape,) * 5,
        compiler_params=params(),
        name="shampoo",
    )(arrivals, *[grads] * each, left_stats, right_stats, left_root, right_root, master, average)


def vector_step(values, grads):
    mean_sq = jnp.mean(grads * grads, axis=-1, keepdims=True)
    return values - RATE_VECTOR * grads * lax.rsqrt(mean_sq + 1e-06)


def round_places(number):
    place = 0
    for other, count in enumerate(ROUNDS):
        if other == number:
            break
        place = place + (32 if other == LARGE else 64) * count
    if number == LARGE:
        return place, 64 * sum(ROUNDS) - 32 * ROUNDS[LARGE]
    return place, place + 32 * ROUNDS[number]


def scatter_tables(owners_all, coords, slot_dev, blocks):
    own_rank, own_x, own_core = coords
    ranks = owners_all.shape[0]
    both = 2 * slot_dev
    chips = owners_all // both
    same = chips[:, :, None] == chips[:, None, :]
    later = jnp.arange(blocks)[None, :] > jnp.arange(blocks)[:, None]
    order = jnp.sum((same & later[None]).astype(jnp.int32), axis=-1)
    dx = (chips % 2) ^ own_x
    z_at = chips // 2
    dy = jnp.arange(ranks)[:, None] ^ own_rank
    position = jnp.zeros_like(owners_all)
    arrival = jnp.zeros_like(owners_all)
    starts, unused = offsets(ranks)
    good = jnp.array(True)
    done = 0
    for number, count in enumerate(ROUNDS):
        inside = order - 4 * done
        core = inside // (2 * count)
        kind = inside // count % 2
        slot = inside % count
        outer = jnp.where(kind == 0, dx, dy)
        inner = jnp.where(kind == 0, dy, dx)
        dc = core ^ own_core
        here = ((kind * 2 + outer) * 2 + inner) * 4 + z_at
        first, second = round_places(number)
        here = jnp.where(dc == 0, first, second) + here * count + slot
        valid = (inside >= 0) & (inside < 4 * count)
        position = jnp.where(valid, here, position)
        arrival = jnp.where(valid, dc * slot_dev + 2 * done + inside % (2 * count), arrival)
        done = done + count
        if number < len(EARLY):
            there = jnp.arange(blocks) >= starts[EARLY[number]]
            good = good & jnp.all((order >= 4 * done) | there[None])
    device = (lax.axis_index("z") * 2 + own_x) * 2 + own_core
    mine = lax.dynamic_index_in_dim(owners_all, own_rank, 0, keepdims=False)
    arrival = lax.dynamic_index_in_dim(arrival, own_rank, 0, keepdims=False)
    match = mine[None, :] == (device * slot_dev + jnp.arange(slot_dev))[:, None]
    index = jnp.sum(jnp.where(match, arrival[None, :], 0), axis=-1)
    return position.reshape(-1).astype(jnp.int32), index.astype(jnp.int32), good


def added(terms):
    return sum(term.astype(f32) for term in terms).astype(bf16)


def one_round(rounds, send, number):
    count = ROUNDS[number]
    offset = round_places(number)[0]
    (come,) = yield [(send, "core")]
    half, quarter = 16 * count, 8 * count

    def part(kind, first, length):
        start = offset + kind * half + first
        here = kind * half + first
        return [rounds.sums[start : start + length], come[here : here + length]]

    got = yield [
        (added(part(0, quarter, quarter)), "x"),
        (added(part(1, quarter, quarter)), "mp"),
    ]
    eighth = quarter // 2
    late = yield [
        (added(part(0, eighth, eighth) + [got[0][eighth:]]), "mp"),
        (added(part(1, eighth, eighth) + [got[1][eighth:]]), "x"),
    ]
    columns = [
        added(part(kind, 0, eighth) + [got[kind][:eighth], late[kind]])
        .reshape(4, count, BLOCK, BLOCK)
        for kind in range(2)
    ]
    column = jnp.concatenate(columns, axis=1)
    if number < len(ROUNDS) - 1:
        return column
    z_at = lax.axis_index("z")

    def for_z(step):
        return lax.dynamic_index_in_dim(column, jnp.clip(z_at + step, 0, 3), 0, keepdims=False)

    got = yield [(for_z(step), step) for step in (2, -2, 1, -1, 3, -3)]
    return added([for_z(0), *got])


def total_steps(values):
    for group in (("core", "x", "both"), ("mp", "near", "across"), ("far",)):
        got = yield [(values, move) for move in group]
        values = values + got[0]
        if len(got) > 1:
            values = values + (got[1] + got[2])
    return values


class Rounds:
    def __init__(self, sums, tail):
        self.running, self.waiting, self.results = {}, {}, {}
        self.sums, self.tail = sums, tail

    def add(self, name, steps):
        self.running[name] = steps
        self.waiting[name] = next(steps)

    def add_round(self, number):
        size = 32 * ROUNDS[number]
        offset = round_places(number)[1]
        send = self.tail if number == LARGE else self.sums[offset : offset + size]
        self.add(number, one_round(self, send, number))

    def beside(self, *held):
        names = list(self.waiting)
        values = [value for name in names for value, unused in self.waiting[name]]
        out = list(tied(*values, *held))
        for name in names:
            self.waiting[name] = [(out.pop(0), move) for unused, move in self.waiting[name]]
        return out

    def hold(self):
        moves = [[move for unused, move in pairs] for pairs in self.waiting.values()]
        values = [value for pairs in self.waiting.values() for value, unused in pairs]
        columns = list(self.results.items())
        out = list(tied(self.sums, *values, *[value for unused, value in columns]))
        self.sums = out.pop(0)
        for name, names in zip(self.waiting, moves):
            self.waiting[name] = [(out.pop(0), move) for move in names]
        for (name, unused), value in zip(columns, out):
            self.results[name] = value
        return self.sums, self.tail

    def step(self, names, *held, sums=None):
        names = [name for name in names if name in self.waiting]
        transfers = [pair for name in names for pair in self.waiting[name]]
        if sums is not None:
            got, held = together(transfers, *sums, *held)
            (self.sums, self.tail), held = held[:2], held[2:]
        else:
            got, held = together(transfers, *held)
        for name in names:
            count = len(self.waiting[name])
            mine, got = got[:count], got[count:]
            try:
                self.waiting[name] = self.running[name].send(mine)
            except StopIteration as end:
                self.results[name] = end.value
                del self.waiting[name]
        return held


def one_swap(value, move):
    (come,) = yield [(value, move)]
    return come


def joined(columns):
    return jnp.concatenate(columns, axis=1).reshape(-1, BLOCK, BLOCK)


def over_z(column):
    return lax.psum_scatter(column, "z", scatter_dimension=0, tiled=True)


def finish_rounds(rounds):
    rounds.add_round(3)
    rounds.step([1, 2, 3, "small"])
    rounds.add_round(4)
    rounds.step([2, 4, "small"])
    (column,) = rounds.beside(joined([rounds.results[number] for number in range(3)]))
    early = over_z(column)
    rounds.step([3, "small"])
    rounds.step([3])
    (column,) = rounds.beside(joined([rounds.results[3]]))
    late = over_z(column)
    for unused in range(3):
        rounds.step([4])
    mine = jnp.concatenate([early, late, rounds.results[4]], axis=0)
    return jnp.concatenate([mine, swap(mine, "core")], axis=0)


def all_rounds(sums, tail):
    rounds = Rounds(sums, tail)
    for number in range(3):
        rounds.add_round(number)
    rounds.step([0, 1, 2])
    rounds.step([0, 1])
    rounds.step([0])
    return finish_rounds(rounds)


def edges(first_rows, last_rows, ranks):
    before = lax.ppermute(last_rows, "mp", [(r, r + 1) for r in range(ranks - 1)])
    behind = lax.ppermute(first_rows, "mp", [(r + 1, r) for r in range(ranks - 1)])
    return before, behind


def local(fast):
    def run(
        stream, cotangent, segments, owners, master, average, left_stats, right_stats, left_root,
        right_root, gains, kernel,
    ):
        ranks = lax.axis_size("mp")
        rank = lax.axis_index("mp")
        coords = (rank, lax.axis_index("x"), lax.axis_index("core"))
        rows = stream.shape[0]
        slot_dev = master.shape[1]
        chips = lax.axis_size("z") * lax.axis_size("x") * 2
        slots = slot_dev * chips
        segment_ids = segments[0]
        group = segment_ids.shape[0]
        unused, blocks = offsets(ranks)

        if fast:
            pair = jnp.concatenate([owners, swap(owners, "mp")])
            owners_all = jnp.where(rank == 0, pair, pair[::-1])
        else:
            owners_all = lax.all_gather(owners, "mp", axis=0, tiled=True)
        places = jnp.asarray(weight_places(ranks))
        if fast:
            table, arrivals, good = scatter_tables(owners_all, coords, slot_dev, blocks)
        else:
            table = (owners_all + jnp.arange(ranks)[:, None] * slots).reshape(-1)
            arrivals = jnp.arange(slot_dev, dtype=jnp.int32)

        slopes = 2.0 ** (-8.0 * (jnp.arange(HEADS).astype(f32) + 1.0) / HEADS)
        padded = jnp.pad(segment_ids, (HALO, HALO), constant_values=-1)
        wide_ids = jnp.pad(padded, (2, 2), constant_values=-2)
        tall = rows + 2 * HALO
        here = lax.dynamic_slice_in_dim(padded, rank * rows, tall)
        masks = jnp.stack(
            [
                (lax.dynamic_slice_in_dim(wide_ids, rank * rows + k, tall) == here).astype(f32)
                for k in range(KERNEL)
            ]
        )
        masks = jnp.broadcast_to(masks[:, :, None], (KERNEL, tall, 128))
        windows = key_windows(segment_ids, rank, rows)

        def gain(n):
            return gains[n : n + 1]

        starts = [offsets(ranks)[0][first] for first, unused in GROUPS] + [blocks]
        low = master[0].astype(bf16)
        if fast:
            across = 1 - rank
            core_at = coords[2]
            own_places = places[rank]
            all_places = places.reshape(-1)
            column = lax.all_gather(low, ("z", "x", "core"), axis=0, tiled=True)
            normed_own = norm_rows(stream, gain(0))
            normed_other = swap(normed_own, "mp")

            def own_part(group):
                here = slice(starts[group], starts[group + 1])
                return unsort(
                    column, owners[0, here], own_places[here], GROUP_CHUNKS[group], True
                )

            def outgoing(listed, first, count):
                half = count // 2
                return lax.dynamic_slice_in_dim(listed, first + core_at * half, half)

            def put(weights, one, two, group, first):
                base = across * blocks + starts[group] + first
                half = one.shape[0]
                return place_weights(
                    weights, [one, two],
                    [base + core_at * half, base + (1 - core_at) * half], all_places,
                )

            w_attn, list_attn = own_part(1)
            send_attn = outgoing(list_attn, 0, 96)

            def first_half():
                w_one, list_one = own_part(0)
                (product,) = ffn_half(normed_other, w_one, UP1, DOWN1, rank, False)
                return w_one, list_one, product

            w_one, list_one, product = first_half()
            (come_attn,), (w_one, list_one, product) = together(
                [(send_attn, "mp")], w_one, list_one, product
            )
            own_product, pre_first = ffn_half(normed_own, w_one, UP1, DOWN1, rank, True)
            w_conv, list_conv = own_part(2)
            w_two, list_two = own_part(3)
            (product, beside), (own_product, w_conv, list_conv, w_two, list_two) = together(
                [(product, "mp"), (come_attn, "core")], own_product, w_conv, list_conv, w_two,
                list_two,
            )
            after_first, normed_attn = join(stream, own_product, product, gain(1))
            w_attn = put(w_attn, come_attn, beside, 1, 0)

            queries = project(normed_attn, w_attn, QUERY, 1)
            keys = project(normed_attn, w_attn, KEY, 2, rank, 2)
            (other,), (queries, keys) = together([(normed_attn, "mp")], queries, keys)
            part_two = outgoing(list_two, 0, 64)
            list_rest = jnp.concatenate(
                [outgoing(list_attn, 96, 32), outgoing(list_conv, 0, 96)]
            )
            keys = project(other, w_attn, KEY, 2, across, 2, keys)
            attended, logs = attention_forward(
                queries, keys, segment_ids, rank, windows, slopes
            )
            (come_rest, come_two), (attended, logs) = together(
                [(list_rest, "mp"), (part_two, "mp")], attended, logs
            )
            (beside,), unused = together([(come_rest, "core")])
            w_attn = put(w_attn, come_rest[:16], beside[:16], 1, 96)
            w_conv = put(w_conv, come_rest[16:], beside[16:], 2, 0)
            after_attn = project_out(attended, w_attn, OUT, after_first)
            before, behind = edges(after_attn[:HALO], after_attn[-HALO:], ranks)
            rest_two, before, behind = tied(outgoing(list_two, 64, 192), before, behind)
            after_conv, linear, gate, normed_two = conv_forward(
                after_attn, before, behind, gain(2), gain(3), w_conv, kernel, masks
            )
            own_product, pre_second = ffn_half(normed_two, w_two, UP2, DOWN2, rank, True)
            (more_two, beside), (own_product, pre_second, w_two) = together(
                [(rest_two, "mp"), (come_two, "core")], own_product, pre_second, w_two
            )
            (more_beside,), unused = together([(more_two, "core")])
            send_one, more_two = tied(outgoing(list_one, 0, 256), more_two)
            w_two = put(w_two, come_two, beside, 3, 0)
            w_two = put(w_two, more_two, more_beside, 3, 64)
            product, pre_second = ffn_half(
                normed_two, w_two, UP2, DOWN2, across, True, pre_second
            )
            after_second, output = join(after_conv, own_product, product, gain(4))
            sources = [(normed_attn, rank), (other, across)]
        else:
            everything = lax.all_gather(low, ("mp", "z", "x", "core"), axis=0, tiled=True)
            slot_of = owners_all + jnp.arange(ranks)[:, None] * slots
            arrays = []
            for number, chunks in enumerate(GROUP_CHUNKS):
                here = slice(starts[number], starts[number + 1])
                arrays += unsort(
                    everything, slot_of[:, here].reshape(-1).astype(jnp.int32),
                    places[:, here].reshape(-1), chunks, False,
                )
            w_one, w_attn, w_conv, w_two = arrays
            after_first, pre_first, normed_attn = ffn_forward(
                stream, gain(0), gain(1), w_one, UP1, DOWN1
            )
            other = lax.all_gather(normed_attn, "mp", axis=0, tiled=True)
            queries = project(normed_attn, w_attn, QUERY, 1)
            keys = project(other, w_attn, KEY, 2)
            sources = [(other, 0)]
            attended, logs = attention_forward(
                queries, keys, segment_ids, rank, windows, slopes
            )
            after_attn = project_out(attended, w_attn, OUT, after_first)
            before, behind = edges(after_attn[:HALO], after_attn[-HALO:], ranks)
            after_conv, linear, gate, normed_two = conv_forward(
                after_attn, before, behind, gain(2), gain(3), w_conv, kernel, masks
            )
            after_second, pre_second, output = ffn_forward(
                after_conv, gain(3), gain(4), w_two, UP2, DOWN2
            )

        if fast:
            last = 32 * ROUNDS[LARGE]
            sums = ((ranks * slots - last, BLOCK, BLOCK), (last, BLOCK, BLOCK))
        else:
            sums = ((ranks * slots, BLOCK, BLOCK),)
            if slots > blocks:
                sums = (jnp.zeros(sums[0], bf16),)
        grad_conv, gains_a, *sums = ffn_backward(
            after_second, gain(4), [cotangent], None, after_conv, gain(3), pre_second, w_two,
            UP2, DOWN2, sums, table, ranks,
        )
        if fast:
            (come_one,), (grad_conv, gains_a, *sums) = together(
                [(send_one, "mp")], grad_conv, gains_a, *sums
            )
            rounds = Rounds(*sums)
            rounds.add_round(0)
            sums = rounds.hold()
        before, behind = edges(
            grad_conv[:HALO].astype(bf16), grad_conv[-HALO:].astype(bf16), ranks
        )
        grad_attn, gains_b, tap_grads, *sums = conv_backward(
            grad_conv, before, behind, after_attn, gain(2), linear, gate, w_conv, kernel, masks,
            sums, table, ranks,
        )
        if fast:
            grad_attn, gains_b, tap_grads = rounds.step(
                [0], grad_attn, gains_b, tap_grads, sums=sums
            )
            rounds.add_round(1)
            sums = rounds.hold()
        mixed_grad, *sums = project_out_back(
            grad_attn, w_attn, OUT, attended, sums, table, ranks
        )
        query_grad, key_grad, value_grad = attention_backward(
            queries, keys, segment_ids, rank, windows, slopes, logs, mixed_grad, attended
        )
        if fast:
            rounds.add("core", one_swap(come_one, "core"))
            query_grad, key_grad, value_grad = rounds.step(
                [0, 1, "core"], query_grad, key_grad, value_grad, sums=sums
            )
            sums = rounds.hold()
            away = input_gradient(key_grad, value_grad, w_attn, 1 - rank, rows)
        else:
            away = input_gradient(key_grad, value_grad, w_attn, jnp.zeros((), jnp.int32), group)
            arrived = lax.psum_scatter(away, "mp", scatter_dimension=0, tiled=True)
        near, *sums = projections_back(
            normed_attn, query_grad, key_grad, value_grad, sources, fast, w_attn, sums, table, ranks
        )
        if fast:
            w_one = put(w_one, come_one, rounds.results.pop("core"), 0, 0)
            (arrived,), (near, w_one, *sums) = together([(away, "mp")], near, w_one, *sums)
            rounds.sums, rounds.tail = sums
            rounds.add_round(2)
            sums = rounds.hold()
        stream_grad, gains_c, *sums = ffn_backward(
            after_first, gain(1), [near, arrived], grad_attn, stream, gain(0), pre_first, w_one,
            UP1, DOWN1, sums, table, ranks, rank if fast else None,
        )
        if fast:
            stream_grad, gains_c = rounds.step([0, 1, 2], stream_grad, gains_c, sums=sums)
        small = jnp.concatenate(
            [gains_c[1:2], gains_c[0:1], gains_b, gains_a[1:2], gains_a[0:1], tap_grads]
        )
        everywhere = ("mp", "z", "x", "core")
        if fast:
            rounds.add("small", total_steps(small))
            sums = (rounds.sums, rounds.tail)
            own_grads = finish_rounds(rounds)
            small = rounds.results["small"]
            own_grads = lax.cond(
                good,
                lambda sums, tail, own: own,
                lambda sums, tail, own: all_rounds(sums, tail),
                *sums,
                own_grads,
            )
        else:
            own_grads = lax.psum_scatter(sums[0], everywhere, scatter_dimension=0, tiled=True)
            small = lax.psum(small, everywhere)
        gain_grads, kernel_grads = small[:5], small[5:]
        block_grads, left_new, right_new, master_new, average_new = shampoo(
            own_grads, arrivals, left_stats[0], right_stats[0], left_root[0], right_root[0], master[0],
            average[0],
        )
        return (
            output,
            stream_grad,
            block_grads[None],
            left_new[None],
            right_new[None],
            master_new[None],
            average_new[None],
            gain_grads,
            vector_step(gains, gain_grads),
            kernel_grads,
            vector_step(kernel, kernel_grads),
        )

    return run


def solution(mesh):
    ranks, pieces = mesh.shape["mp"], mesh.shape["dp"]
    fast = ranks == 2 and pieces == 16
    xs = 2 if fast else 1
    grid = Mesh(
        np.asarray(mesh.devices).reshape(ranks, pieces // (2 * xs), xs, 2), ("mp", "z", "x", "core")
    )
    dp = ("z", "x", "core")
    rows = P((*dp, "mp"), None)
    slots = P("mp", dp, None, None)
    return jax.shard_map(
        local(fast),
        mesh=grid,
        in_specs=(
            rows, rows, P(dp, None), P("mp", None), slots, slots, slots, slots, slots, slots, P(),
            P(),
        ),
        out_specs=(rows, rows, slots, slots, slots, slots, slots, P(), P(), P(), P()),
        check_vma=False,
    )
```

```python
import math

import jax
import jax.numpy as jnp
import numpy as np
from jax import lax
from jax.experimental import pallas as pl
from jax.experimental.pallas import tpu as pltpu
from jax.sharding import Mesh
from jax.sharding import PartitionSpec as P

D = 1024
FF = 4096
HEADS = 8
HEAD_DIM = 128
KERNEL = 5
STEP = 4
BLOCK = 128
HALO = 16
WIDE = 8

EPSILON = 1e-05
DECAY_STAT = 0.95
RATE_BLOCK = 0.02
RATE_VECTOR = 0.2
DECAY_AVERAGE = 0.9999
MASKED = -1e30
LOG2E = math.log2(math.e)
SCORE_SCALE = 1.0 / math.sqrt(HEAD_DIM)

f32 = jnp.float32
bf16 = jnp.bfloat16
ANY = pl.BlockSpec(memory_space=pl.ANY)
SMEM = pl.BlockSpec(memory_space=pltpu.SMEM)

MATRICES = [
    (0, 0, D, FF, True),
    (0, 4, FF, D, False),
    (1, 0, D, D, True),
    (1, 1, D, D, True),
    (1, 2, D, D, True),
    (1, 3, D, D, False),
    (2, 0, D, D, True),
    (2, 1, D, D, True),
    (2, 2, D, D, False),
    (3, 0, D, FF, True),
    (3, 4, FF, D, False),
]
UP1, DOWN1, QUERY, KEY, VALUE, OUT, CONV_VALUE, CONV_GATE, CONV_OUT, UP2, DOWN2 = range(11)
GROUPS = [(0, 2), (2, 6), (6, 9), (9, 11)]
GROUP_CHUNKS = [8, 4, 3, 8]


def at(matrix):
    return MATRICES[matrix][1]


ROUNDS = [4, 3, 4, 9, 3]
LARGE = 3
EARLY = [9, 6, 2]


def params(**kw):
    return pltpu.CompilerParams(vmem_limit_bytes=58 * 2**20, **kw)


def const_spec(shape):
    return pl.BlockSpec(shape, lambda *ids: (0,) * len(shape), pipeline_mode=pl.Buffered(1))


def row_tile(rows):
    return 256 if rows % 256 == 0 else 128


def cost(flops, moved):
    return pl.CostEstimate(flops=int(flops), bytes_accessed=int(moved), transcendentals=0)


def offsets(ranks):
    out = []
    offset = 0
    for unused, unused_chunk, height, breadth, by_columns in MATRICES:
        out.append(offset)
        offset = offset + height * breadth // (BLOCK * BLOCK * ranks)
    return out, offset


def block_number(matrix, row_block, column_block, ranks):
    starts, total = offsets(ranks)
    unused, unused_chunk, height, breadth, by_columns = MATRICES[matrix]
    if by_columns:
        part = breadth // BLOCK // ranks
        return (
            (column_block // part) * total + starts[matrix] + row_block * part + column_block % part
        )
    part = height // BLOCK // ranks
    breadth_blocks = breadth // BLOCK
    return (
        (row_block // part) * total
        + starts[matrix]
        + (row_block % part) * breadth_blocks
        + column_block
    )


def weight_places(ranks):
    unused, total = offsets(ranks)
    places = np.zeros((ranks * total,), np.int32)
    for matrix, (unused, chunk, height, breadth, by_columns) in enumerate(MATRICES):
        for row in range(height // BLOCK):
            for column in range(breadth // BLOCK):
                place = ((chunk + column // WIDE) * 8 + row) * WIDE + column % WIDE
                places[block_number(matrix, row, column, ranks)] = place
    return places.reshape(ranks, total)


def chunks_first(blocks):
    up = blocks[:128].reshape(8, 16)
    down = blocks[128:]
    return [up[:, :8].reshape(-1), down[:64], up[:, 8:].reshape(-1), down[64:]]


def copy_in_place(out, source, place, sem):
    row = pl.multiple_of((place // WIDE) * BLOCK, BLOCK)
    column = pl.multiple_of((place % WIDE) * BLOCK, BLOCK)
    pltpu.make_async_copy(
        source, out.at[pl.ds(row, BLOCK), pl.ds(column, BLOCK)], sem
    ).start()


def unsort(slots, sources, places, chunks, listed):
    count = sources.shape[0]
    each = max(n for n in range(1, 65) if count % n == 0)
    steps = count // each

    def body(source_ref, place_ref, slots_ref, *rest):
        out = rest[0]
        list_ref = rest[1] if listed else None
        held, read_sem, write_sem, list_sem = rest[-4:]
        step = pl.program_id(0)
        slot = lax.rem(step, 2)

        def read(number, into):
            def one(n, unused):
                pltpu.make_async_copy(
                    slots_ref.at[source_ref[number * each + n]], held.at[into, n], read_sem.at[into]
                ).start()
                return unused

            lax.fori_loop(0, each, one, 0)

        def written(number, into):
            pltpu.make_async_copy(held.at[into], held.at[into], write_sem.at[into]).wait()
            if listed:
                pltpu.make_async_copy(held.at[into], held.at[into], list_sem.at[into]).wait()

        @pl.when(step == 0)
        def _():
            read(0, 0)

        @pl.when(step >= 1)
        def _():
            written(step - 1, 1 - slot)

        @pl.when(step + 1 < steps)
        def _():
            read(step + 1, 1 - slot)

        pltpu.make_async_copy(held.at[slot], held.at[slot], read_sem.at[slot]).wait()

        def one(n, unused):
            copy_in_place(out, held.at[slot, n], place_ref[step * each + n], write_sem.at[slot])
            return unused

        lax.fori_loop(0, each, one, 0)
        if listed:
            pltpu.make_async_copy(
                held.at[slot], list_ref.at[pl.ds(step * each, each)], list_sem.at[slot]
            ).start()

        @pl.when(step == steps - 1)
        def _():
            written(step, slot)

    shapes = [jax.ShapeDtypeStruct((chunks * D, D), bf16)]
    if listed:
        shapes.append(jax.ShapeDtypeStruct((count, BLOCK, BLOCK), bf16))
    return pl.pallas_call(
        body,
        grid=(steps,),
        out_shape=tuple(shapes),
        in_specs=[SMEM, SMEM, ANY],
        out_specs=(ANY,) * len(shapes),
        scratch_shapes=[
            pltpu.VMEM((2, each, BLOCK, BLOCK), bf16),
            pltpu.SemaphoreType.DMA((2,)),
            pltpu.SemaphoreType.DMA((2,)),
            pltpu.SemaphoreType.DMA((2,)),
        ],
        compiler_params=params(has_side_effects=True),
        cost_estimate=cost(0, 3 * count * BLOCK * BLOCK * 2),
        name="unsort",
    )(sources, places, slots)


def place_weights(weights, arrays, bases, places):
    count = arrays[0].shape[0]
    number = len(arrays)
    each = max(n for n in range(1, 128 // number + 1) if count % n == 0)

    def body(table, base_ref, *rest):
        sources = rest[:number]
        out, sem = rest[-2], rest[-1]
        start = pl.program_id(0) * each

        def one(t, unused):
            for a, source in enumerate(sources):
                copy_in_place(out, source.at[t], table[base_ref[a] + start + t], sem.at[a])
            return unused

        lax.fori_loop(0, each, one, 0)
        for a, source in enumerate(sources):
            pltpu.make_async_copy(source, source, sem.at[a]).wait()

    operands = [places, jnp.stack(bases).astype(jnp.int32), *arrays, weights]
    return pl.pallas_call(
        body,
        grid=(count // each,),
        out_shape=jax.ShapeDtypeStruct(weights.shape, bf16),
        in_specs=[SMEM, SMEM]
        + [pl.BlockSpec((each, BLOCK, BLOCK), lambda n: (n, 0, 0))] * number
        + [ANY],
        out_specs=ANY,
        scratch_shapes=[pltpu.SemaphoreType.DMA((number,))],
        input_output_aliases={len(operands) - 1: 0},
        compiler_params=params(has_side_effects=True),
        cost_estimate=cost(0, 2 * number * count * BLOCK * BLOCK * 2),
        name="place_weights",
    )(*operands)


PAIR = [(0, 1), (1, 0)]
MOVES = {
    "x": ("x", PAIR),
    "mp": ("mp", PAIR),
    "core": ("core", PAIR),
    "near": ("z", [(0, 1), (1, 0), (2, 3), (3, 2)]),
    "far": ("z", [(0, 2), (2, 0), (1, 3), (3, 1)]),
    "both": (("x", "core"), [(n, 3 - n) for n in range(4)]),
    "across": (("mp", "z"), [(n, (n // 4 * 4) ^ 4 | (n % 4) ^ 1) for n in range(8)]),
}
for _step in (-3, -2, -1, 1, 2, 3):
    MOVES[_step] = ("z", [(z, z + _step) for z in range(4) if 0 <= z + _step < 4])


def swap(value, move):
    axis, pairs = MOVES[move]
    return lax.ppermute(value, axis, pairs)


def tied(*values):
    return lax.optimization_barrier(values)


def together(transfers, *held):
    values = tied(*[value for value, unused in transfers])
    arrived = [swap(value, move) for value, (unused, move) in zip(values, transfers)]
    out = tied(*arrived, *held)
    return list(out[: len(arrived)]), out[len(arrived) :]


def sigmoid(values):
    return 0.5 * jnp.tanh(0.5 * values) + 0.5


def norm_parts(values):
    center = values - jnp.mean(values, axis=-1, keepdims=True)
    spread = jnp.mean(center * center, axis=-1, keepdims=True)
    scale = lax.rsqrt(spread + EPSILON)
    return center * scale, scale


def norm(values, gain):
    return norm_parts(values)[0] * gain


def norm_back(values, gain, grad):
    hat, scale = norm_parts(values)
    inner = grad * gain
    mean_inner = jnp.mean(inner, axis=-1, keepdims=True)
    mean_hat = jnp.mean(inner * hat, axis=-1, keepdims=True)
    return (
        scale * (inner - mean_inner - hat * mean_hat),
        jnp.sum(grad * hat, axis=0, keepdims=True),
    )


def dot(a, b):
    return jnp.dot(a, b, preferred_element_type=f32)


def dot_right(a, b):
    return lax.dot_general(a, b, (((1,), (1,)), ((), ())), preferred_element_type=f32)


def dot_left(a, b):
    return lax.dot_general(a, b, (((0,), (0,)), ((), ())), preferred_element_type=f32)


def start_blocks(table, targets, source, sem, matrix, row_block, column_block, ranks):
    height, breadth = source.shape
    for i in range(height // BLOCK):
        for j in range(breadth // BLOCK):
            place = table[block_number(matrix, row_block + i, column_block + j, ranks)]
            block = source.at[pl.ds(i * BLOCK, BLOCK), pl.ds(j * BLOCK, BLOCK)]
            if len(targets) == 1:
                pltpu.make_async_copy(block, targets[0].at[place], sem).start()
                continue
            limit = targets[0].shape[0]

            @pl.when(place < limit)
            def _(place=place, block=block):
                pltpu.make_async_copy(block, targets[0].at[place], sem).start()

            @pl.when(place >= limit)
            def _(place=place, block=block):
                pltpu.make_async_copy(block, targets[1].at[place - limit], sem).start()


def wait_blocks(source, sem):
    pltpu.make_async_copy(source, source, sem).wait()


def ffn_forward(stream, gain, next_gain, weights, upper, lower):
    rows = stream.shape[0]
    tile = row_tile(rows)
    wide = D
    steps = FF // wide

    def body(x_ref, gain_ref, next_gain_ref, up_ref, down_ref, out_ref, pre_ref, next_ref, normed):
        step = pl.program_id(0)

        @pl.when(step == 0)
        def _():
            for t in range(0, rows, tile):
                x = x_ref[t : t + tile].astype(f32)
                normed[t : t + tile] = norm(x, gain_ref[...]).astype(bf16)
                out_ref[t : t + tile] = jnp.zeros((tile, D), f32)

        for t in range(0, rows, tile):
            pre = dot(normed[t : t + tile], up_ref[...])
            pre_ref[t : t + tile] = pre.astype(bf16)
            act = (pre * sigmoid(pre)).astype(bf16)
            out_ref[t : t + tile] += dot(act, down_ref[...])

        @pl.when(step == steps - 1)
        def _():
            for t in range(0, rows, tile):
                y = x_ref[t : t + tile].astype(f32) + 0.5 * out_ref[t : t + tile]
                out_ref[t : t + tile] = y
                next_ref[t : t + tile] = norm(y, next_gain_ref[...]).astype(bf16)

    return pl.pallas_call(
        body,
        grid=(steps,),
        out_shape=(
            jax.ShapeDtypeStruct((rows, D), f32),
            jax.ShapeDtypeStruct((rows, FF), bf16),
            jax.ShapeDtypeStruct((rows, D), bf16),
        ),
        in_specs=[
            const_spec((rows, D)),
            const_spec((1, D)),
            const_spec((1, D)),
            pl.BlockSpec((D, wide), lambda f: (at(upper) + f, 0)),
            pl.BlockSpec((wide, D), lambda f: (at(lower) + f, 0)),
        ],
        out_specs=(
            const_spec((rows, D)),
            pl.BlockSpec((rows, wide), lambda f: (0, f)),
            const_spec((rows, D)),
        ),
        scratch_shapes=[pltpu.VMEM((rows, D), bf16)],
        compiler_params=params(),
        cost_estimate=cost(4 * rows * D * FF, 4 * D * FF + 2 * rows * FF),
        name="ffn_forward",
    )(stream, gain, next_gain, weights, weights)


def norm_rows(values, gain):
    rows = values.shape[0]
    tile = row_tile(rows)

    def body(x_ref, gain_ref, out_ref):
        out_ref[...] = norm(x_ref[...].astype(f32), gain_ref[...]).astype(bf16)

    spec = pl.BlockSpec((tile, D), lambda t: (t, 0))
    return pl.pallas_call(
        body,
        grid=(rows // tile,),
        out_shape=jax.ShapeDtypeStruct((rows, D), bf16),
        in_specs=[spec, const_spec((1, D))],
        out_specs=spec,
        compiler_params=params(),
        name="norm_rows",
    )(values, gain)


def ffn_part(normed, weights, upper, lower, first, steps, keep, pre=None):
    rows = normed.shape[0]
    tile = row_tile(rows)

    def body(part_ref, x_ref, up_ref, down_ref, *rest):
        out_ref = rest[-3] if keep else rest[-2]
        pre_ref = rest[-2]
        total = rest[-1]
        step = pl.program_id(0)
        for t in range(0, rows, tile):
            here = slice(t, t + tile)
            value = dot(x_ref[here], up_ref[...])
            if keep:
                pre_ref[here] = value.astype(bf16)
            act = (value * sigmoid(value)).astype(bf16)
            new = dot(act, down_ref[...])

            if steps == 1:
                out_ref[here] = new.astype(bf16)
                continue

            @pl.when(step == 0)
            def _(new=new, here=here):
                total[here] = new

            @pl.when(step == steps - 1)
            def _(new=new, here=here):
                out_ref[here] = (total[here] + new).astype(bf16)

    operands = [first.reshape(1), normed, weights, weights]
    specs = [
        pl.BlockSpec((rows, D), lambda f, p: (0, 0), pipeline_mode=pl.Buffered(1)),
        pl.BlockSpec((D, D), lambda f, p: (at(upper) + p[0] + f, 0)),
        pl.BlockSpec((D, D), lambda f, p: (at(lower) + p[0] + f, 0)),
    ]
    shapes = [jax.ShapeDtypeStruct((rows, D), bf16)]
    out_specs = [pl.BlockSpec((rows, D), lambda f, p: (0, 0), pipeline_mode=pl.Buffered(1))]
    aliases = {}
    if keep:
        shapes.append(jax.ShapeDtypeStruct((rows, FF), bf16))
        out_specs.append(pl.BlockSpec((rows, D), lambda f, p: (0, p[0] + f)))
        if pre is not None:
            aliases = {len(operands): 1}
            operands.append(pre)
            specs.append(ANY)
    return pl.pallas_call(
        body,
        grid_spec=pltpu.PrefetchScalarGridSpec(
            num_scalar_prefetch=1,
            grid=(steps,),
            in_specs=specs,
            out_specs=tuple(out_specs),
            scratch_shapes=[pltpu.VMEM((rows, D), f32)],
        ),
        out_shape=tuple(shapes),
        input_output_aliases=aliases,
        compiler_params=params(),
        cost_estimate=cost(4 * rows * D * D * steps, 4 * D * D * steps),
        name="ffn_part",
    )(*operands)


def join(base, products, next_gain):
    rows = base.shape[0]
    tile = row_tile(rows)
    count = len(products)

    def body(base_ref, *refs):
        gain_ref, out_ref, next_ref = refs[count:]
        both = refs[0][...].astype(f32)
        for ref in refs[1:count]:
            both = both + ref[...].astype(f32)
        y = base_ref[...].astype(f32) + 0.5 * both
        out_ref[...] = y
        next_ref[...] = norm(y, gain_ref[...]).astype(bf16)

    spec = pl.BlockSpec((tile, D), lambda t: (t, 0))
    return pl.pallas_call(
        body,
        grid=(rows // tile,),
        out_shape=(
            jax.ShapeDtypeStruct((rows, D), f32),
            jax.ShapeDtypeStruct((rows, D), bf16),
        ),
        in_specs=[spec] * (count + 1) + [const_spec((1, D))],
        out_specs=(spec, spec),
        compiler_params=params(),
        name="join",
    )(base, *products, next_gain)


def ffn_backward(
    after, after_gain, after_grads, base, stream, gain, pre, weights, upper, lower, sums, table,
    ranks, kept=None, first=0, last=None, carry=None,
):
    rows = stream.shape[0]
    tile = row_tile(rows)
    wide = 512
    steps = (FF // wide if last is None else last) - first
    whole = FF // wide
    parts = len(after_grads)
    targets = len(sums)
    with_base = base is not None
    again = kept is not None

    def body(table_ref, *refs):
        refs = list(refs)
        at_ref = 0
        if parts > 0:
            after_ref, after_gain_ref = refs[0], refs[1]
            grad_refs = refs[2 : 2 + parts]
            at_ref = 2 + parts
        base_ref = None
        if with_base:
            base_ref = refs[at_ref]
            at_ref += 1
        x_ref, gain_ref, up_ref, down_ref, pre_ref = refs[at_ref : at_ref + 5]
        kept_ref = refs[at_ref + 5]
        outs = refs[at_ref + 5 + again + (carry is not None) + aliased :]
        out_ref, gains_ref = outs[:2]
        sums_ref = outs[2 : 2 + targets]
        carry_ref = refs[at_ref + 5 + again]
        grad_sum = outs[2 + targets]
        (
            half, normed, pre_here, normed_t, pre_grad, act_t, up_part, down_part, up_sem, down_sem,
        ) = outs[3 + targets :]
        step = pl.program_id(0)

        @pl.when(step == 0)
        def _():
            gain_sum = jnp.zeros((1, D), f32)
            for t in range(0, rows, tile):
                here = slice(t, t + tile)
                if parts == 0:
                    back = base_ref[here]
                else:
                    grad = grad_refs[0][here].astype(f32)
                    for other in grad_refs[1:]:
                        grad = grad + other[here].astype(f32)
                    back, part = norm_back(after_ref[here], after_gain_ref[...], grad)
                    gain_sum = gain_sum + part
                    if with_base:
                        back = back + base_ref[here]
                out_ref[here] = back
                half[here] = (0.5 * back).astype(bf16)
                low = norm(x_ref[here].astype(f32), gain_ref[...]).astype(bf16)
                if again:
                    normed[here] = low
                normed_t[:, here] = low.T
                grad_sum[here] = jnp.zeros((tile, D), f32) if carry is None else carry_ref[here]
            gains_ref[0:1] = gain_sum

        if again:

            @pl.when((first + step) // (whole // 2) == kept_ref[0])
            def _():
                pre_here[...] = pre_ref[...]

            @pl.when((first + step) // (whole // 2) != kept_ref[0])
            def _():
                for t in range(0, rows, tile):
                    here = slice(t, t + tile)
                    pre_here[here] = dot(normed[here], up_ref[...]).astype(bf16)

        for t in range(0, rows, tile):
            here = slice(t, t + tile)
            act_grad = dot_right(half[here], down_ref[...])
            pre_act = (pre_here if again else pre_ref)[here].astype(f32)
            sigma = sigmoid(pre_act)
            act = pre_act * sigma
            act_t[:, here] = act.astype(bf16).T
            slope = sigma + act * (1.0 - sigma)
            moved = (act_grad * slope).astype(bf16)
            pre_grad[here] = moved
            grad_sum[here] += dot_right(moved, up_ref[...])

        @pl.when(step >= 1)
        def _():
            wait_blocks(up_part, up_sem)
            wait_blocks(down_part, down_sem)

        for t in range(0, D, 256):
            up_part[t : t + 256] = dot(normed_t[t : t + 256], pre_grad[...]).astype(bf16)
        for t in range(0, wide, 256):
            down_part[t : t + 256] = dot(act_t[t : t + 256], half[...]).astype(bf16)
        start_blocks(
            table_ref, sums_ref, up_part, up_sem, upper, 0, (first + step) * 4, ranks
        )
        start_blocks(
            table_ref, sums_ref, down_part, down_sem, lower, (first + step) * 4, 0, ranks
        )

        @pl.when(step == steps - 1)
        def _():
            wait_blocks(up_part, up_sem)
            wait_blocks(down_part, down_sem)
            if last is not None:
                return
            gain_sum = jnp.zeros((1, D), f32)
            for t in range(0, rows, tile):
                here = slice(t, t + tile)
                back, part = norm_back(x_ref[here].astype(f32), gain_ref[...], grad_sum[here])
                gain_sum = gain_sum + part
                out_ref[here] += back
            gains_ref[1:2] = gain_sum

    operands = [table]
    specs = [SMEM]
    if parts > 0:
        operands += [after, after_gain, *after_grads]
        specs += [const_spec((rows, D)), const_spec((1, D))] + [const_spec((rows, D))] * parts
    if with_base:
        operands.append(base)
        specs.append(const_spec((rows, D)))
    operands += [stream, gain, weights, weights]
    specs += [
        const_spec((rows, D)),
        const_spec((1, D)),
        pl.BlockSpec((D, wide), lambda f: (at(upper) + (first + f) // 2, (first + f) % 2)),
        pl.BlockSpec((wide, D), lambda f: (at(lower) * 2 + first + f, 0)),
    ]
    operands.append(pre)
    specs.append(pl.BlockSpec((rows, wide), lambda f: (0, first + f)))
    if again:
        operands.append(kept.reshape(1))
        specs.append(SMEM)
    if carry is not None:
        operands.append(carry)
        specs.append(const_spec((rows, D)))
    aliases = {}
    aliased = 0 if isinstance(sums[0], tuple) else targets
    if not isinstance(sums[0], tuple):
        for n, target in enumerate(sums):
            aliases[len(operands)] = 2 + n
            operands.append(target)
            specs.append(ANY)
        sums = [target.shape for target in sums]
    return pl.pallas_call(
        body,
        grid=(steps,),
        out_shape=(
            jax.ShapeDtypeStruct((rows, D), f32),
            jax.ShapeDtypeStruct((2, D), f32),
            *[jax.ShapeDtypeStruct(shape, bf16) for shape in sums],
        )
        + ((jax.ShapeDtypeStruct((rows, D), f32),) if last is not None else ()),
        in_specs=specs,
        out_specs=(const_spec((rows, D)), const_spec((2, D)))
        + (ANY,) * targets
        + ((const_spec((rows, D)),) if last is not None else ()),
        scratch_shapes=([pltpu.VMEM((rows, D), f32)] if last is None else [])
        + [
            pltpu.VMEM((rows, D), bf16),
            pltpu.VMEM((rows, D) if again else (16, 128), bf16),
            pltpu.VMEM((rows, wide) if again else (16, 128), bf16),
            pltpu.VMEM((D, rows), bf16),
            pltpu.VMEM((rows, wide), bf16),
            pltpu.VMEM((wide, rows), bf16),
            pltpu.VMEM((D, wide), bf16),
            pltpu.VMEM((wide, D), bf16),
            pltpu.SemaphoreType.DMA,
            pltpu.SemaphoreType.DMA,
        ],
        input_output_aliases=aliases,
        compiler_params=params(has_side_effects=True),
        cost_estimate=cost(8 * rows * D * wide * steps, 8 * D * wide * steps),
        name="ffn_backward",
    )(*operands)


def project(values, weights, first, count, part=None, parts=1, into=None):
    rows = values.shape[0]
    tile = row_tile(rows)
    wide = D

    def body(part_ref, x_ref, w_ref, *rest):
        out_ref = rest[-1]
        for t in range(0, rows, tile):
            out_ref[t : t + tile] = dot(x_ref[t : t + tile], w_ref[...]).astype(bf16)

    operands = [jnp.asarray(0 if part is None else part, jnp.int32).reshape(1), values, weights]
    specs = [
        pl.BlockSpec((rows, D), lambda f, part: (0, 0), pipeline_mode=pl.Buffered(1)),
        pl.BlockSpec((D, wide), lambda f, part: (at(first) + f, 0)),
    ]
    aliases = {}
    if into is not None:
        aliases = {3: 0}
        operands.append(into)
        specs.append(ANY)
    return pl.pallas_call(
        body,
        grid_spec=pltpu.PrefetchScalarGridSpec(
            num_scalar_prefetch=1,
            grid=(count,),
            in_specs=specs,
            out_specs=pl.BlockSpec((rows, wide), lambda f, part: (part[0], f)),
        ),
        out_shape=jax.ShapeDtypeStruct((parts * rows, count * D), bf16),
        input_output_aliases=aliases,
        compiler_params=params(),
        cost_estimate=cost(2 * rows * D * D * count, 2 * count * D * (D + rows)),
        name="project",
    )(*operands)


def project_out(values, weights, matrix, stream):
    rows = values.shape[0]
    tile = row_tile(rows)

    def body(x_ref, w_ref, s_ref, out_ref):
        out_ref[...] = s_ref[...] + dot(x_ref[...], w_ref[...])

    return pl.pallas_call(
        body,
        grid=(rows // tile,),
        out_shape=jax.ShapeDtypeStruct((rows, D), f32),
        in_specs=[
            pl.BlockSpec((tile, D), lambda t: (t, 0)),
            pl.BlockSpec((D, D), lambda t: (at(matrix), 0)),
            pl.BlockSpec((tile, D), lambda t: (t, 0)),
        ],
        out_specs=pl.BlockSpec((tile, D), lambda t: (t, 0)),
        compiler_params=params(),
        cost_estimate=cost(2 * rows * D * D, 2 * D * D + 10 * rows * D),
        name="project_out",
    )(values, weights, stream)


def project_out_back(grad, weights, matrix, attended, sums, table, ranks):
    rows = grad.shape[0]
    tile = row_tile(rows)
    wide = 512

    targets = len(sums)

    def body(table_ref, g_ref, w_ref, a_ref, *refs):
        out_ref = refs[targets]
        sums_ref = refs[targets + 1 : 2 * targets + 1]
        low, part, sem = refs[2 * targets + 1 :]
        step = pl.program_id(0)

        @pl.when(step == 0)
        def _():
            for t in range(0, rows, tile):
                low[t : t + tile] = g_ref[t : t + tile].astype(bf16)

        for t in range(0, rows, tile):
            out_ref[t : t + tile] = dot_right(low[t : t + tile], w_ref[...]).astype(bf16)
        for t in range(0, wide, 256):
            part[step, t : t + 256] = dot_left(a_ref[:, t : t + 256], low[...]).astype(bf16)
        start_blocks(table_ref, sums_ref, part.at[step], sem.at[step], matrix, step * 4, 0, ranks)

        @pl.when(step == 1)
        def _():
            for s in range(2):
                wait_blocks(part.at[s], sem.at[s])

    return pl.pallas_call(
        body,
        grid=(2,),
        out_shape=(
            jax.ShapeDtypeStruct((rows, D), bf16),
            *[jax.ShapeDtypeStruct(target.shape, bf16) for target in sums],
        ),
        in_specs=[
            SMEM,
            const_spec((rows, D)),
            pl.BlockSpec((wide, D), lambda f: (at(matrix) * 2 + f, 0)),
            pl.BlockSpec((rows, wide), lambda f: (0, f)),
        ]
        + [ANY] * targets,
        out_specs=(pl.BlockSpec((rows, wide), lambda f: (0, f)),) + (ANY,) * targets,
        scratch_shapes=[
            pltpu.VMEM((rows, D), bf16),
            pltpu.VMEM((2, wide, D), bf16),
            pltpu.SemaphoreType.DMA((2,)),
        ],
        input_output_aliases={4 + n: 1 + n for n in range(targets)},
        compiler_params=params(has_side_effects=True),
        cost_estimate=cost(4 * rows * D * D, 4 * D * D + 8 * rows * D),
        name="project_out_back",
    )(table, grad, weights, attended, *sums)


def input_gradient(key_grad, value_grad, weights, part, rows):
    tile = row_tile(rows)
    steps = rows // tile

    def body(part_ref, k_ref, v_ref, wk_ref, wv_ref, out_ref):
        out_ref[...] = (
            dot_right(k_ref[...], wk_ref[...]) + dot_right(v_ref[...], wv_ref[...])
        ).astype(bf16)

    return pl.pallas_call(
        body,
        grid_spec=pltpu.PrefetchScalarGridSpec(
            num_scalar_prefetch=1,
            grid=(steps,),
            in_specs=[
                pl.BlockSpec((tile, D), lambda t, part: (part[0] * steps + t, 0)),
                pl.BlockSpec((tile, D), lambda t, part: (part[0] * steps + t, 0)),
                pl.BlockSpec((D, D), lambda t, part: (at(KEY), 0)),
                pl.BlockSpec((D, D), lambda t, part: (at(VALUE), 0)),
            ],
            out_specs=pl.BlockSpec((tile, D), lambda t, part: (t, 0)),
        ),
        out_shape=jax.ShapeDtypeStruct((rows, D), bf16),
        compiler_params=params(),
        cost_estimate=cost(4 * rows * D * D, 4 * D * D + 6 * rows * D),
        name="input_gradient",
    )(part.reshape(1), key_grad, value_grad, weights, weights)


def projections_back(
    normed, query_grad, key_grad, value_grad, sources, own_keys, weights, sums, table, ranks
):
    rows = normed.shape[0]
    tile = row_tile(rows)
    wide = 512
    count = len(sources)
    targets = len(sums)
    lengths = [source[0].shape[0] for source in sources]

    def body(part_ref, table_ref, n_ref, q_ref, *refs):
        normed_refs = refs[:count]
        key_refs = refs[count : 2 * count]
        value_refs = refs[2 * count : 3 * count]
        w_ref = refs[3 * count]
        outs = refs[3 * count + 1 + targets :]
        out_ref, sums_ref, scratch = outs[0], outs[1 : 1 + targets], outs[1 + targets :]
        own_t = scratch[0]
        source_t = scratch[1 : 1 + count]
        part, sem = scratch[1 + count :]
        step = pl.program_id(0)
        slot = lax.rem(step, 2)

        @pl.when(step == 0)
        def _():
            for t in range(0, rows, tile):
                own_t[:, t : t + tile] = n_ref[t : t + tile].T
            for n_from, n_to, length in zip(normed_refs, source_t, lengths):
                small = row_tile(length)
                for t in range(0, length, small):
                    n_to[:, t : t + small] = n_from[t : t + small].T

        @pl.when(step >= 2)
        def _():
            wait_blocks(part.at[slot], sem.at[slot])

        @pl.when(step < 2)
        def _():
            for t in range(0, rows, tile):
                new = dot_right(q_ref[t : t + tile], w_ref[...])

                @pl.when(step == 0)
                def _():
                    out_ref[t : t + tile] = new

                @pl.when(step == 1)
                def _():
                    out_ref[t : t + tile] += new

            for t in range(0, D, 256):
                part[slot, t : t + 256] = dot(own_t[t : t + 256], q_ref[...]).astype(bf16)
            start_blocks(
                table_ref, sums_ref, part.at[slot], sem.at[slot], QUERY, 0, lax.rem(step, 2) * 4,
                ranks,
            )

        def other(grad_refs, matrix):
            if own_keys:
                for t in range(0, rows, tile):
                    out_ref[t : t + tile] += dot_right(grad_refs[0][t : t + tile], w_ref[...])
            for t in range(0, D, 256):
                total = dot(source_t[0][t : t + 256], grad_refs[0][...])
                for n_t, grad_ref in zip(source_t[1:], grad_refs[1:]):
                    total = total + dot(n_t[t : t + 256], grad_ref[...])
                part[slot, t : t + 256] = total.astype(bf16)
            start_blocks(
                table_ref, sums_ref, part.at[slot], sem.at[slot], matrix, 0, lax.rem(step, 2) * 4,
                ranks,
            )

        @pl.when((step >= 2) & (step < 4))
        def _():
            other(key_refs, KEY)

        @pl.when(step >= 4)
        def _():
            other(value_refs, VALUE)

        @pl.when(step == 5)
        def _():
            for s in range(2):
                wait_blocks(part.at[s], sem.at[s])

    parts = jnp.stack([jnp.asarray(source[1], jnp.int32) for source in sources])
    operands = [parts, table, normed, query_grad]

    def whole(shape):
        return pl.BlockSpec(shape, lambda f, part: (0, 0), pipeline_mode=pl.Buffered(1))

    specs = [
        SMEM,
        whole((rows, D)),
        pl.BlockSpec((rows, wide), lambda f, part: (0, jnp.minimum(f, 1))),
    ]
    operands += [source[0] for source in sources]
    specs += [whole((length, D)) for length in lengths]
    for grads, first in ((key_grad, 2), (value_grad, 4)):
        for n, length in enumerate(lengths):
            operands.append(grads)
            specs.append(
                pl.BlockSpec(
                    (length, wide),
                    lambda f, part, n=n, first=first: (part[n], jnp.clip(f - first, 0, 1)),
                )
            )
    operands += [weights, *sums]
    specs += [pl.BlockSpec((D, wide), lambda f, part: (at(QUERY) + f // 2, f % 2))]
    specs += [ANY] * targets
    return pl.pallas_call(
        body,
        grid_spec=pltpu.PrefetchScalarGridSpec(
            num_scalar_prefetch=1,
            grid=(6,),
            in_specs=specs,
            out_specs=(whole((rows, D)),) + (ANY,) * targets,
            scratch_shapes=[pltpu.VMEM((D, rows), bf16)]
            + [pltpu.VMEM((D, length), bf16) for length in lengths]
            + [pltpu.VMEM((2, D, wide), bf16), pltpu.SemaphoreType.DMA((2,))],
        ),
        out_shape=(
            jax.ShapeDtypeStruct((rows, D), f32),
            *[jax.ShapeDtypeStruct(target.shape, bf16) for target in sums],
        ),
        input_output_aliases={len(operands) - targets + n: 1 + n for n in range(targets)},
        compiler_params=params(has_side_effects=True),
        cost_estimate=cost(
            (4 * rows + sum(4 * length for length in lengths) + 4 * rows) * D * D, 30 * D * D
        ),
        name="projections_back",
    )(*operands)


def attention_tiles(rows):
    return (512 if rows % 512 == 0 else row_tile(rows)), 256


def key_windows(segments, rank, rows):
    tall, broad = attention_tiles(rows)
    group = segments.shape[0]
    blocks = rows // tall
    own = lax.dynamic_slice_in_dim(segments, rank * rows, rows).reshape(blocks, tall)
    low = jnp.sum(segments[None, :] < own[:, :1], axis=1)
    high = jnp.sum(segments[None, :] <= own[:, -1:], axis=1)
    start = low // 128 * 128
    steps = (high - start + broad - 1) // broad
    start = jnp.minimum(start, group - steps * broad)
    return jnp.stack([start, steps], axis=-1).reshape(-1).astype(jnp.int32)

def attention_forward(queries, keys, segments, rank, windows, slopes):
    rows = queries.shape[0]
    group = keys.shape[0]
    tall, broad = attention_tiles(rows)
    most = group // broad
    own = lax.dynamic_slice_in_dim(segments, rank * rows, rows).reshape(rows, 1)

    def body(rank_ref, window_ref, slope_ref, q_ref, own_ref, key_ref, value_ref, columns_ref, out_ref, total_ref, scores):
        head, block = pl.program_id(0), pl.program_id(1)
        slope = slope_ref[head] * LOG2E
        start = window_ref[2 * block]
        steps = window_ref[2 * block + 1]
        first = rank_ref[0] * rows + block * tall
        query = q_ref[...]
        apart = (
            lax.broadcasted_iota(jnp.int32, (tall, broad), 0)
            - lax.broadcasted_iota(jnp.int32, (tall, broad), 1)
        ).astype(f32)

        def attend(count):
            peak = jnp.full((tall, 128), MASKED, f32)
            for b in range(count):
                begin = pl.multiple_of(start + b * broad, 128)
                here = pl.ds(begin, broad)
                score = dot_right(query, key_ref[here, :]) * (SCORE_SCALE * LOG2E)
                score = score - slope * jnp.abs(apart + (first - begin).astype(f32))
                score = jnp.where(own_ref[...] == columns_ref[:, here], score, MASKED)
                scores[:, b * broad : (b + 1) * broad] = score
                for lane in range(0, broad, 128):
                    peak = jnp.maximum(peak, score[:, lane : lane + 128])
            top = jnp.max(peak, axis=-1, keepdims=True)
            total = jnp.zeros((tall, 128), f32)
            mixed = jnp.zeros((tall, HEAD_DIM), f32)
            for b in range(count):
                here = pl.ds(pl.multiple_of(start + b * broad, 128), broad)
                shifted = jnp.exp2(scores[:, b * broad : (b + 1) * broad] - top)
                for lane in range(0, broad, 128):
                    total = total + shifted[:, lane : lane + 128]
                mixed = mixed + dot(shifted.astype(bf16), value_ref[here, :])
            total = jnp.sum(total, axis=-1, keepdims=True)
            out_ref[...] = (mixed / total).astype(bf16)
            logs = jnp.broadcast_to(top + jnp.log2(total), (tall, 128))
            total_ref[...] = logs.T[0:1, :].reshape(1, 1, tall)

        for count in range(1, most + 1):
            @pl.when(steps == count)
            def _(count=count):
                attend(count)

    return pl.pallas_call(
        body,
        grid=(HEADS, rows // tall),
        out_shape=(
            jax.ShapeDtypeStruct((rows, D), bf16),
            jax.ShapeDtypeStruct((HEADS, 1, rows), f32),
        ),
        in_specs=[
            SMEM, SMEM, SMEM,
            pl.BlockSpec((tall, HEAD_DIM), lambda h, q: (q, h)),
            pl.BlockSpec((tall, 1), lambda h, q: (q, 0)),
            pl.BlockSpec((group, HEAD_DIM), lambda h, q: (0, h)),
            pl.BlockSpec((group, HEAD_DIM), lambda h, q: (0, HEADS + h)),
            const_spec((1, group)),
        ],
        out_specs=(
            pl.BlockSpec((tall, HEAD_DIM), lambda h, q: (q, h)),
            pl.BlockSpec((1, 1, tall), lambda h, q: (h, 0, q)),
        ),
        scratch_shapes=[pltpu.VMEM((tall, group), f32)],
        compiler_params=params(),
        name="attention_forward",
    )(jnp.asarray(rank,jnp.int32).reshape(1), windows, slopes, queries, own, keys, keys, segments.reshape(1, group))

def attention_backward(queries, keys, segments, rank, windows, slopes, logs, grads, attended):
    rows = queries.shape[0]
    group = keys.shape[0]
    tall, broad = attention_tiles(rows)
    most = group // broad
    own = lax.dynamic_slice_in_dim(segments, rank * rows, rows).reshape(1, rows)

    def body(rank_ref, window_ref, slope_ref, q_ref, own_ref, log_ref, grad_ref, att_ref, key_ref, value_ref, columns_ref,
             out_ref, key_out, value_out, key_sum, value_sum):
        head, block = pl.program_id(0), pl.program_id(1)
        slope = slope_ref[head] * LOG2E
        start = window_ref[2 * block]
        steps = window_ref[2 * block + 1]
        first = rank_ref[0] * rows + block * tall

        @pl.when(block == 0)
        def _():
            key_sum[...] = jnp.zeros(key_sum.shape, f32)
            value_sum[...] = jnp.zeros(value_sum.shape, f32)

        query = q_ref[...]
        grad = grad_ref[...]
        products = grad.astype(f32) * att_ref[...].astype(f32)
        delta = jnp.broadcast_to(jnp.sum(products, axis=-1, keepdims=True), (tall, 128)).T[0:1, :]
        log_row = log_ref[0]
        apart = (
            lax.broadcasted_iota(jnp.int32, (broad, tall), 1)
            - lax.broadcasted_iota(jnp.int32, (broad, tall), 0)
        ).astype(f32)

        def attend(count):
            query_sum = jnp.zeros((tall, HEAD_DIM), f32)
            for b in range(count):
                begin = pl.multiple_of(start + b * broad, 128)
                here = pl.ds(begin, broad)
                key = key_ref[here, :]
                score = dot_right(key, query) * (SCORE_SCALE * LOG2E)
                score = score - slope * jnp.abs(apart + (first - begin).astype(f32))
                score = jnp.where(own_ref[...] == columns_ref[here, :], score, MASKED)
                probs = jnp.exp2(score - log_row)
                prob_grad = dot_right(value_ref[here, :], grad)
                value_sum[here, :] += dot(probs.astype(bf16), grad)
                score_grad = (probs * (prob_grad - delta)).astype(bf16)
                key_sum[here, :] += dot(score_grad, query)
                query_sum = query_sum + dot_left(score_grad, key)
            out_ref[...] = (query_sum * SCORE_SCALE).astype(bf16)

        for count in range(1, most + 1):
            @pl.when(steps == count)
            def _(count=count):
                attend(count)

        @pl.when(block == pl.num_programs(1) - 1)
        def _():
            key_out[...] = (key_sum[...] * SCORE_SCALE).astype(bf16)
            value_out[...] = value_sum[...].astype(bf16)

    row_spec = pl.BlockSpec((tall, HEAD_DIM), lambda h, q: (q, h))
    key_spec = pl.BlockSpec((group, HEAD_DIM), lambda h, q: (0, h))
    return pl.pallas_call(
        body,
        grid=(HEADS, rows // tall),
        out_shape=(jax.ShapeDtypeStruct((rows, D), bf16),) + (jax.ShapeDtypeStruct((group, D), bf16),) * 2,
        in_specs=[
            SMEM, SMEM, SMEM,
            pl.BlockSpec((tall, HEAD_DIM), lambda h, q: (q, h)),
            pl.BlockSpec((1, tall), lambda h, q: (0, q)),
            pl.BlockSpec((1, 1, tall), lambda h, q: (h, 0, q)),
            row_spec, row_spec, key_spec,
            pl.BlockSpec((group, HEAD_DIM), lambda h, q: (0, HEADS + h)),
            const_spec((group, 1)),
        ],
        out_specs=(row_spec, key_spec, key_spec),
        scratch_shapes=[pltpu.VMEM((group, HEAD_DIM), f32)] * 2,
        compiler_params=params(),
        name="attention_backward",
    )(jnp.asarray(rank,jnp.int32).reshape(1), windows, slopes, queries, own, logs, grads, attended, keys, keys, segments.reshape(group, 1))


def conv_forward(stream, before, behind, gain, next_gain, weights, taps, masks):
    rows = stream.shape[0]
    tall = rows + 2 * HALO
    tile = row_tile(rows)
    wide = 256
    steps = D // wide

    def body(
        x_ref, before_ref, behind_ref, gain_ref, next_gain_ref, taps_ref, mask_ref, value_ref, gate_ref, out_w_ref,
        out_ref, linear_ref, gate_out_ref, next_ref, normed, glu,
    ):
        step = pl.program_id(0)

        @pl.when(step == 0)
        def _():
            gain_row = gain_ref[...]
            normed[0:HALO] = norm(before_ref[...], gain_row).astype(bf16)
            normed[rows + HALO :] = norm(behind_ref[...], gain_row).astype(bf16)
            for t in range(0, rows, tile):
                x = x_ref[t : t + tile]
                normed[HALO + t : HALO + t + tile] = norm(x, gain_row).astype(bf16)
                out_ref[t : t + tile] = x

        pieces = [(0, HALO)]
        pieces += [(HALO + t, tile) for t in range(0, rows, tile)]
        pieces += [(rows + HALO, HALO)]
        for t, size in pieces:
            here = slice(t, t + size)
            linear = dot(normed[here], value_ref[...])
            gate = dot(normed[here], gate_ref[...])
            linear_ref[here] = linear.astype(bf16)
            gate_out_ref[here] = gate.astype(bf16)
            glu[here] = linear * sigmoid(gate)
        for t in range(0, rows, tile):
            sums = []
            for half in range(0, wide, 128):
                total = jnp.zeros((tile, 128), f32)
                for k in range(KERNEL):
                    moved = glu[HALO + t + k - 2 : HALO + t + k - 2 + tile, half : half + 128]
                    if k != KERNEL // 2:
                        moved = moved * mask_ref[k, HALO + t : HALO + t + tile]
                    total = total + taps_ref[k : k + 1, half : half + 128] * moved
                sums.append(total)
            conved = jnp.concatenate(sums, axis=1)
            act = (conved * sigmoid(conved)).astype(bf16)
            out_ref[t : t + tile] += dot(act, out_w_ref[...])

        @pl.when(step == steps - 1)
        def _():
            for t in range(0, rows, tile):
                next_ref[t : t + tile] = norm(out_ref[t : t + tile], next_gain_ref[...]).astype(bf16)

    return pl.pallas_call(
        body,
        grid=(steps,),
        out_shape=(
            jax.ShapeDtypeStruct((rows, D), f32),
            jax.ShapeDtypeStruct((tall, D), bf16),
            jax.ShapeDtypeStruct((tall, D), bf16),
            jax.ShapeDtypeStruct((rows, D), bf16),
        ),
        in_specs=[
            const_spec((rows, D)),
            const_spec((HALO, D)),
            const_spec((HALO, D)),
            const_spec((1, D)),
            const_spec((1, D)),
            pl.BlockSpec((KERNEL, wide), lambda c: (0, c)),
            const_spec((KERNEL, tall, 128)),
            pl.BlockSpec((D, wide), lambda c: (at(CONV_VALUE), c)),
            pl.BlockSpec((D, wide), lambda c: (at(CONV_GATE), c)),
            pl.BlockSpec((wide, D), lambda c: (at(CONV_OUT) * 4 + c, 0)),
        ],
        out_specs=(
            const_spec((rows, D)),
            pl.BlockSpec((tall, wide), lambda c: (0, c)),
            pl.BlockSpec((tall, wide), lambda c: (0, c)),
            const_spec((rows, D)),
        ),
        scratch_shapes=[pltpu.VMEM((tall, D), bf16), pltpu.VMEM((tall, wide), f32)],
        compiler_params=params(),
        cost_estimate=cost(6 * rows * D * D, 6 * D * D + 12 * rows * D),
        name="conv_forward",
    )(stream, before, behind, gain, next_gain, taps, masks, weights, weights, weights)


def conv_backward(
    grad, before, behind, stream, gain, linear, gate, weights, taps, masks, sums, table, ranks
):
    rows = stream.shape[0]
    tall = rows + 2 * HALO
    tile = row_tile(rows)
    wide = 256
    steps = D // wide
    targets = len(sums)

    def body(
        table_ref, g_ref, before_ref, behind_ref, x_ref, gain_ref, linear_ref, gate_ref, taps_ref,
        mask_ref, value_ref, gate_w_ref, out_w_ref, *refs,
    ):
        out_ref, gain_out_ref, taps_out_ref = refs[targets : targets + 3]
        sums_ref = refs[targets + 3 : 2 * targets + 3]
        (
            low, normed_t, grad_sum, glu, conv_grad, act_t, value_grad, gate_grad, value_part,
            gate_part, out_part, value_sem, gate_sem, out_sem,
        ) = refs[2 * targets + 3 :]
        step = pl.program_id(0)
        slot = lax.rem(step, 2)

        @pl.when(step == 0)
        def _():
            low[0:HALO] = before_ref[...]
            low[rows + HALO :] = behind_ref[...]
            for t in range(0, rows, tile):
                here = slice(t, t + tile)
                low[HALO + t : HALO + t + tile] = g_ref[here].astype(bf16)
                normed_t[:, here] = norm(x_ref[here], gain_ref[...]).astype(bf16).T
                grad_sum[here] = jnp.zeros((tile, D), f32)

        pieces = [(0, HALO)]
        pieces += [(HALO + t, tile) for t in range(0, rows, tile)]
        pieces += [(rows + HALO, HALO)]
        for t, size in pieces:
            here = slice(t, t + size)
            glu[here] = linear_ref[here].astype(f32) * sigmoid(gate_ref[here].astype(f32))

        edge = 8
        pieces = [(HALO - edge, edge)]
        pieces += [(HALO + t, tile) for t in range(0, rows, tile)]
        pieces += [(rows + HALO, edge)]
        tap_sums = [[jnp.zeros((1, 128), f32) for k in range(KERNEL)] for half in range(2)]
        for t, size in pieces:
            totals, moved_rows = [], []
            for half in range(0, wide, 128):
                total = jnp.zeros((size, 128), f32)
                moved_rows.append([])
                for k in range(KERNEL):
                    moved = glu[t + k - 2 : t + k - 2 + size, half : half + 128]
                    if k != KERNEL // 2:
                        moved = moved * mask_ref[k, t : t + size]
                    moved_rows[-1].append(moved)
                    total = total + taps_ref[k : k + 1, half : half + 128] * moved
                totals.append(total)
            conved = jnp.concatenate(totals, axis=1)
            sigma = sigmoid(conved)
            act = conved * sigma
            if size == tile:
                act_t[:, t - HALO : t - HALO + size] = act.astype(bf16).T
                rows_grad = dot_right(low[t : t + size], out_w_ref[...])
            elif t < HALO:
                rows_grad = dot_right(low[0:HALO], out_w_ref[...])[edge:]
            else:
                rows_grad = dot_right(low[rows + HALO :], out_w_ref[...])[:edge]
            center = rows_grad * (sigma + act * (1.0 - sigma))
            conv_grad[t : t + size] = center
            if size == tile:
                for number in range(2):
                    lanes = center[:, number * 128 : (number + 1) * 128]
                    for k in range(KERNEL):
                        tap_sums[number][k] = tap_sums[number][k] + jnp.sum(
                            lanes * moved_rows[number][k], axis=0, keepdims=True
                        )

        for t in range(0, rows, tile):
            values, gates = [], []
            for number, half in enumerate(range(0, wide, 128)):
                lanes = slice(half, half + 128)
                start = HALO + t
                total = jnp.zeros((tile, 128), f32)
                for k in range(KERNEL):
                    moved = conv_grad[start + 2 - k : start + 2 - k + tile, lanes]
                    if k != KERNEL // 2:
                        moved = moved * mask_ref[KERNEL - 1 - k, start : start + tile]
                    total = total + taps_ref[k : k + 1, lanes] * moved
                sigma = sigmoid(gate_ref[start : start + tile, lanes].astype(f32))
                moved_value = total * sigma
                values.append(moved_value.astype(bf16))
                gates.append(
                    (
                        moved_value
                        * linear_ref[start : start + tile, lanes].astype(f32)
                        * (1.0 - sigma)
                    ).astype(bf16)
                )
            value_tile = jnp.concatenate(values, axis=1)
            gate_tile = jnp.concatenate(gates, axis=1)
            here = slice(t, t + tile)
            value_grad[here] = value_tile
            gate_grad[here] = gate_tile
            grad_sum[here] += dot_right(value_tile, value_ref[...]) + dot_right(
                gate_tile, gate_w_ref[...]
            )
        for k in range(KERNEL):
            taps_out_ref[k : k + 1] = jnp.concatenate([tap_sums[0][k], tap_sums[1][k]], axis=1)

        @pl.when(step >= 2)
        def _():
            wait_blocks(value_part.at[slot], value_sem.at[slot])
            wait_blocks(gate_part.at[slot], gate_sem.at[slot])
            wait_blocks(out_part.at[slot], out_sem.at[slot])

        for t in range(0, D, 256):
            value_part[slot, t : t + 256] = dot(normed_t[t : t + 256], value_grad[...]).astype(bf16)
            gate_part[slot, t : t + 256] = dot(normed_t[t : t + 256], gate_grad[...]).astype(bf16)
        out_part[slot] = dot(act_t[...], low[HALO : rows + HALO]).astype(bf16)
        start_blocks(
            table_ref, sums_ref, value_part.at[slot], value_sem.at[slot], CONV_VALUE, 0, step * 2,
            ranks,
        )
        start_blocks(
            table_ref, sums_ref, gate_part.at[slot], gate_sem.at[slot], CONV_GATE, 0, step * 2,
            ranks,
        )
        start_blocks(
            table_ref, sums_ref, out_part.at[slot], out_sem.at[slot], CONV_OUT, step * 2, 0, ranks
        )

        @pl.when(step == steps - 1)
        def _():
            gain_sum = jnp.zeros((1, D), f32)
            for t in range(0, rows, tile):
                here = slice(t, t + tile)
                back, part = norm_back(x_ref[here], gain_ref[...], grad_sum[here])
                gain_sum = gain_sum + part
                out_ref[here] = g_ref[here] + back
            gain_out_ref[...] = gain_sum
            for s in range(2):
                wait_blocks(value_part.at[s], value_sem.at[s])
                wait_blocks(gate_part.at[s], gate_sem.at[s])
                wait_blocks(out_part.at[s], out_sem.at[s])

    operands = [
        table, grad, before, behind, stream, gain, linear, gate, taps, masks, weights, weights,
        weights, *sums,
    ]
    return pl.pallas_call(
        body,
        grid=(steps,),
        out_shape=(
            jax.ShapeDtypeStruct((rows, D), f32),
            jax.ShapeDtypeStruct((1, D), f32),
            jax.ShapeDtypeStruct((KERNEL, D), f32),
            *[jax.ShapeDtypeStruct(target.shape, bf16) for target in sums],
        ),
        in_specs=[
            SMEM,
            const_spec((rows, D)),
            const_spec((HALO, D)),
            const_spec((HALO, D)),
            const_spec((rows, D)),
            const_spec((1, D)),
            pl.BlockSpec((tall, wide), lambda c: (0, c)),
            pl.BlockSpec((tall, wide), lambda c: (0, c)),
            pl.BlockSpec((KERNEL, wide), lambda c: (0, c)),
            const_spec((KERNEL, tall, 128)),
            pl.BlockSpec((D, wide), lambda c: (at(CONV_VALUE), c)),
            pl.BlockSpec((D, wide), lambda c: (at(CONV_GATE), c)),
            pl.BlockSpec((wide, D), lambda c: (at(CONV_OUT) * 4 + c, 0)),
        ]
        + [ANY] * targets,
        out_specs=(
            const_spec((rows, D)),
            const_spec((1, D)),
            pl.BlockSpec((KERNEL, wide), lambda c: (0, c)),
        )
        + (ANY,) * targets,
        scratch_shapes=[
            pltpu.VMEM((tall, D), bf16),
            pltpu.VMEM((D, rows), bf16),
            pltpu.VMEM((rows, D), f32),
            pltpu.VMEM((tall, wide), f32),
            pltpu.VMEM((tall, wide), f32),
            pltpu.VMEM((wide, rows), bf16),
            pltpu.VMEM((rows, wide), bf16),
            pltpu.VMEM((rows, wide), bf16),
            pltpu.VMEM((2, D, wide), bf16),
            pltpu.VMEM((2, D, wide), bf16),
            pltpu.VMEM((2, wide, D), bf16),
            pltpu.SemaphoreType.DMA((2,)),
            pltpu.SemaphoreType.DMA((2,)),
            pltpu.SemaphoreType.DMA((2,)),
        ],
        input_output_aliases={len(operands) - targets + n: 3 + n for n in range(targets)},
        compiler_params=params(has_side_effects=True),
        cost_estimate=cost(12 * rows * D * D, 12 * D * D + 16 * rows * D),
        name="conv_backward",
    )(*operands)


def shampoo(grads, arrivals, left_stats, right_stats, left_root, right_root, master, average):
    slots = master.shape[0]
    each = 8
    steps = (slots + each - 1) // each
    arrivals = jnp.pad(arrivals, (0, steps * each - slots))
    old_bias = 1.0 - DECAY_AVERAGE ** (STEP - 1)
    new_bias = 1.0 - DECAY_AVERAGE**STEP

    def body(index_ref, *refs):
        g_refs = refs[:each]
        ls_ref, rs_ref, lr_ref, rr_ref, m_ref, a_ref, go, lo, ro, mo, ao = refs[each:]
        for n in range(each):
            grad = g_refs[n][0]
            go[n] = grad.astype(f32)
            lo[n] = DECAY_STAT * ls_ref[n] + (1.0 - DECAY_STAT) * dot_right(grad, grad)
            ro[n] = DECAY_STAT * rs_ref[n] + (1.0 - DECAY_STAT) * dot_left(grad, grad)
            inner = dot(grad, rr_ref[n].astype(bf16))
            turned = dot(lr_ref[n].astype(bf16), inner.astype(bf16))
            mean_sq = jnp.mean(turned * turned, axis=(0, 1), keepdims=True)
            new = m_ref[n] - RATE_BLOCK * turned * lax.rsqrt(mean_sq + 1e-06)
            mo[n] = new
            ao[n] = (DECAY_AVERAGE * old_bias / new_bias) * a_ref[n] + (
                (1.0 - DECAY_AVERAGE) / new_bias
            ) * new

    spec = pl.BlockSpec((each, BLOCK, BLOCK), lambda s, index: (s, 0, 0))
    grad_specs = [
        pl.BlockSpec((1, BLOCK, BLOCK), lambda s, index, n=n: (index[s * each + n], 0, 0))
        for n in range(each)
    ]
    shape = jax.ShapeDtypeStruct((slots, BLOCK, BLOCK), f32)
    return pl.pallas_call(
        body,
        grid_spec=pltpu.PrefetchScalarGridSpec(
            num_scalar_prefetch=1,
            grid=(steps,),
            in_specs=grad_specs + [spec] * 6,
            out_specs=(spec,) * 5,
        ),
        out_shape=(shape,) * 5,
        compiler_params=params(),
        name="shampoo",
    )(arrivals, *[grads] * each, left_stats, right_stats, left_root, right_root, master, average)


def vector_step(values, grads):
    mean_sq = jnp.mean(grads * grads, axis=-1, keepdims=True)
    return values - RATE_VECTOR * grads * lax.rsqrt(mean_sq + 1e-06)


def round_places(number):
    place = 0
    for other, count in enumerate(ROUNDS):
        if other == number:
            break
        place = place + (32 if other == LARGE else 64) * count
    if number == LARGE:
        return place, 64 * sum(ROUNDS) - 32 * ROUNDS[LARGE]
    return place, place + 32 * ROUNDS[number]


def scatter_tables(owners_all, coords, slot_dev, blocks):
    own_rank, own_x, own_core = coords
    ranks = owners_all.shape[0]
    both = 2 * slot_dev
    chips = owners_all // both
    same = chips[:, :, None] == chips[:, None, :]
    later = jnp.arange(blocks)[None, :] > jnp.arange(blocks)[:, None]
    order = jnp.sum((same & later[None]).astype(jnp.int32), axis=-1)
    dx = (chips % 2) ^ own_x
    z_at = chips // 2
    dy = jnp.arange(ranks)[:, None] ^ own_rank
    position = jnp.zeros_like(owners_all)
    arrival = jnp.zeros_like(owners_all)
    starts, unused = offsets(ranks)
    good = jnp.array(True)
    done = 0
    for number, count in enumerate(ROUNDS):
        inside = order - 4 * done
        core = inside // (2 * count)
        kind = inside // count % 2
        slot = inside % count
        outer = jnp.where(kind == 0, dx, dy)
        inner = jnp.where(kind == 0, dy, dx)
        dc = core ^ own_core
        here = ((kind * 2 + outer) * 2 + inner) * 4 + z_at
        first, second = round_places(number)
        here = jnp.where(dc == 0, first, second) + here * count + slot
        valid = (inside >= 0) & (inside < 4 * count)
        position = jnp.where(valid, here, position)
        arrival = jnp.where(valid, dc * slot_dev + 2 * done + inside % (2 * count), arrival)
        done = done + count
        if number < len(EARLY):
            there = jnp.arange(blocks) >= starts[EARLY[number]]
            good = good & jnp.all((order >= 4 * done) | there[None])
    device = (lax.axis_index("z") * 2 + own_x) * 2 + own_core
    mine = lax.dynamic_index_in_dim(owners_all, own_rank, 0, keepdims=False)
    arrival = lax.dynamic_index_in_dim(arrival, own_rank, 0, keepdims=False)
    match = mine[None, :] == (device * slot_dev + jnp.arange(slot_dev))[:, None]
    index = jnp.sum(jnp.where(match, arrival[None, :], 0), axis=-1)
    return position.reshape(-1).astype(jnp.int32), index.astype(jnp.int32), good


def added(terms):
    return sum(term.astype(f32) for term in terms).astype(bf16)


def one_round(rounds, send, number):
    count = ROUNDS[number]
    offset = round_places(number)[0]
    (come,) = yield [(send, "core")]
    half, quarter = 16 * count, 8 * count

    def part(kind, first, length):
        start = offset + kind * half + first
        here = kind * half + first
        return [rounds.sums[start : start + length], come[here : here + length]]

    got = yield [
        (added(part(0, quarter, quarter)), "x"),
        (added(part(1, quarter, quarter)), "mp"),
    ]
    eighth = quarter // 2
    late = yield [
        (added(part(0, eighth, eighth) + [got[0][eighth:]]), "mp"),
        (added(part(1, eighth, eighth) + [got[1][eighth:]]), "x"),
    ]
    columns = [
        added(part(kind, 0, eighth) + [got[kind][:eighth], late[kind]])
        .reshape(4, count, BLOCK, BLOCK)
        for kind in range(2)
    ]
    column = jnp.concatenate(columns, axis=1)
    if number < len(ROUNDS) - 1:
        return column
    z_at = lax.axis_index("z")

    def for_z(step):
        return lax.dynamic_index_in_dim(column, jnp.clip(z_at + step, 0, 3), 0, keepdims=False)

    got = yield [(for_z(step), step) for step in (2, -2, 1, -1, 3, -3)]
    return added([for_z(0), *got])


def total_steps(values):
    for group in (("core", "x", "both"), ("mp", "near", "across"), ("far",)):
        got = yield [(values, move) for move in group]
        values = values + got[0]
        if len(got) > 1:
            values = values + (got[1] + got[2])
    return values


class Rounds:
    def __init__(self, sums, tail):
        self.running, self.waiting, self.results = {}, {}, {}
        self.sums, self.tail = sums, tail

    def add(self, name, steps):
        self.running[name] = steps
        self.waiting[name] = next(steps)

    def add_round(self, number):
        size = 32 * ROUNDS[number]
        offset = round_places(number)[1]
        send = self.tail if number == LARGE else self.sums[offset : offset + size]
        self.add(number, one_round(self, send, number))

    def beside(self, *held):
        names = list(self.waiting)
        values = [value for name in names for value, unused in self.waiting[name]]
        out = list(tied(*values, *held))
        for name in names:
            self.waiting[name] = [(out.pop(0), move) for unused, move in self.waiting[name]]
        return out

    def hold(self):
        moves = [[move for unused, move in pairs] for pairs in self.waiting.values()]
        values = [value for pairs in self.waiting.values() for value, unused in pairs]
        columns = [(name, value) for name, value in self.results.items() if isinstance(name, int)]
        out = list(tied(self.sums, *values, *[value for unused, value in columns]))
        self.sums = out.pop(0)
        for name, names in zip(self.waiting, moves):
            self.waiting[name] = [(out.pop(0), move) for move in names]
        for (name, unused), value in zip(columns, out):
            self.results[name] = value
        return self.sums, self.tail

    def step(self, names, *held, sums=None):
        names = [name for name in names if name in self.waiting]
        transfers = [pair for name in names for pair in self.waiting[name]]
        if sums is not None:
            got, held = together(transfers, *sums, *held)
            (self.sums, self.tail), held = held[:2], held[2:]
        else:
            got, held = together(transfers, *held)
        for name in names:
            count = len(self.waiting[name])
            mine, got = got[:count], got[count:]
            try:
                self.waiting[name] = self.running[name].send(mine)
            except StopIteration as end:
                self.results[name] = end.value
                del self.waiting[name]
        return held


def both_swaps(value, moves):
    arrived = []
    for move in moves:
        (value,) = yield [(value, move)]
        arrived.append(value)
    return arrived


def joined(columns):
    return jnp.concatenate(columns, axis=1).reshape(-1, BLOCK, BLOCK)


def over_z(column):
    return lax.psum_scatter(column, "z", scatter_dimension=0, tiled=True)


def finish_rounds(rounds):
    rounds.add_round(3)
    rounds.step([2, 3])
    rounds.add_round(4)
    (column,) = rounds.beside(joined([rounds.results[number] for number in range(3)]))
    early = over_z(column)
    rounds.step([3, 4, "small"])
    rounds.step([3, "small"])
    (column,) = rounds.beside(joined([rounds.results[3]]))
    late = over_z(column)
    rounds.step([4, "small"])
    rounds.step([4])
    rounds.step([4])
    mine = jnp.concatenate([early, late, rounds.results[4]], axis=0)
    return jnp.concatenate([mine, swap(mine, "core")], axis=0)


def all_rounds(sums, tail):
    rounds = Rounds(sums, tail)
    for number in range(3):
        rounds.add_round(number)
    rounds.step([0, 1, 2])
    rounds.step([0, 1, 2])
    rounds.step([0, 1])
    return finish_rounds(rounds)


def edges(first_rows, last_rows, ranks):
    before = lax.ppermute(last_rows, "mp", [(r, r + 1) for r in range(ranks - 1)])
    behind = lax.ppermute(first_rows, "mp", [(r + 1, r) for r in range(ranks - 1)])
    return before, behind


def local(fast):
    def run(
        stream, cotangent, segments, owners, master, average, left_stats, right_stats, left_root,
        right_root, gains, kernel,
    ):
        ranks = lax.axis_size("mp")
        rank = lax.axis_index("mp")
        coords = (rank, lax.axis_index("x"), lax.axis_index("core"))
        rows = stream.shape[0]
        slot_dev = master.shape[1]
        chips = lax.axis_size("z") * lax.axis_size("x") * 2
        slots = slot_dev * chips
        segment_ids = segments[0]
        group = segment_ids.shape[0]
        unused, blocks = offsets(ranks)

        if fast:
            pair = jnp.concatenate([owners, swap(owners, "mp")])
            owners_all = jnp.where(rank == 0, pair, pair[::-1])
        else:
            owners_all = lax.all_gather(owners, "mp", axis=0, tiled=True)
        places = jnp.asarray(weight_places(ranks))
        if fast:
            table, arrivals, good = scatter_tables(owners_all, coords, slot_dev, blocks)
        else:
            table = (owners_all + jnp.arange(ranks)[:, None] * slots).reshape(-1)
            arrivals = jnp.arange(slot_dev, dtype=jnp.int32)

        slopes = 2.0 ** (-8.0 * (jnp.arange(HEADS).astype(f32) + 1.0) / HEADS)
        padded = jnp.pad(segment_ids, (HALO, HALO), constant_values=-1)
        wide_ids = jnp.pad(padded, (2, 2), constant_values=-2)
        tall = rows + 2 * HALO
        here = lax.dynamic_slice_in_dim(padded, rank * rows, tall)
        masks = jnp.stack(
            [
                (lax.dynamic_slice_in_dim(wide_ids, rank * rows + k, tall) == here).astype(f32)
                for k in range(KERNEL)
            ]
        )
        masks = jnp.broadcast_to(masks[:, :, None], (KERNEL, tall, 128))
        windows = key_windows(segment_ids, rank, rows)

        def gain(n):
            return gains[n : n + 1]

        starts = [offsets(ranks)[0][first] for first, unused in GROUPS] + [blocks]
        low = master[0].astype(bf16)
        if fast:
            across = 1 - rank
            core_at = coords[2]
            own_places = places[rank]
            all_places = np.concatenate(
                [
                    part
                    for own in weight_places(ranks)
                    for part in [
                        *chunks_first(own[: starts[1]]),
                        own[starts[1] : starts[3]],
                        *chunks_first(own[starts[3] :]),
                    ]
                ]
            )
            all_places = jnp.asarray(all_places)
            column = lax.all_gather(low, ("z", "x", "core"), axis=0, tiled=True)
            normed_own = norm_rows(stream, gain(0))
            normed_other = swap(normed_own, "mp")
            column, normed_other, table, arrivals, good, windows, masks = tied(
                column, normed_other, table, arrivals, good, windows, masks
            )

            def own_part(group):
                here = slice(starts[group], starts[group + 1])
                slot, place = owners[0, here], own_places[here]
                if group in (0, 3):
                    slot = jnp.concatenate(chunks_first(slot))
                    place = jnp.concatenate(chunks_first(place))
                return unsort(column, slot, place, GROUP_CHUNKS[group], True)

            def outgoing(listed, first, count):
                half = count // 2
                return lax.dynamic_slice_in_dim(listed, first + core_at * half, half)

            def put(weights, one, two, group, first):
                base = across * blocks + starts[group] + first
                half = one.shape[0]
                return place_weights(
                    weights, [one, two],
                    [base + core_at * half, base + (1 - core_at) * half], all_places,
                )

            w_attn, list_attn = own_part(1)
            send_attn = outgoing(list_attn, 0, 96)

            def first_half():
                w_one, list_one = own_part(0)
                (product,) = ffn_part(normed_other, w_one, UP1, DOWN1, 2 * rank, 2, False)
                return w_one, list_one, product

            w_one, list_one, product = first_half()
            (come_attn,), (w_one, list_one, product) = together(
                [(send_attn, "mp")], w_one, list_one, product
            )
            own_product, pre_first = ffn_part(normed_own, w_one, UP1, DOWN1, 2 * rank, 2, True)
            w_conv, list_conv = own_part(2)
            w_two, list_two = own_part(3)
            (product, beside), (own_product, w_conv, list_conv, w_two, list_two) = together(
                [(product, "mp"), (come_attn, "core")], own_product, w_conv, list_conv, w_two,
                list_two,
            )
            after_first, normed_attn = join(stream, [own_product, product], gain(1))
            w_attn = put(w_attn, come_attn, beside, 1, 0)

            queries = project(normed_attn, w_attn, QUERY, 1)
            keys = project(normed_attn, w_attn, KEY, 2, rank, 2)
            sends = [
                outgoing(list_attn, 96, 32),
                outgoing(list_conv, 0, 96),
                outgoing(list_two, 0, 64),
                outgoing(list_two, 64, 48),
                outgoing(list_two, 112, 144),
                outgoing(list_one, 0, 128),
                outgoing(list_one, 128, 128),
            ]
            (other,), (queries, keys, *sends) = together(
                [(normed_attn, "mp")], queries, keys, *sends
            )
            keys = project(other, w_attn, KEY, 2, across, 2, keys)
            attended, logs = attention_forward(
                queries, keys, segment_ids, rank, windows, slopes
            )
            come, (attended, logs) = together([(send, "mp") for send in sends[:3]], attended, logs)
            beside, unused = together([(value, "core") for value in come])
            more_two, send_two, *send_one = sends[3:]
            more_two, *beside = tied(more_two, *beside)
            w_attn = put(w_attn, come[0], beside[0], 1, 96)
            w_conv = put(w_conv, come[1], beside[1], 2, 0)
            w_two = put(w_two, come[2], beside[2], 3, 0)
            after_attn = project_out(attended, w_attn, OUT, after_first)
            (more_two,), (after_attn, w_conv, w_two) = together(
                [(more_two, "mp")], after_attn, w_conv, w_two
            )
            before, behind = edges(after_attn[:HALO], after_attn[-HALO:], ranks)
            send_two, before, behind = tied(send_two, before, behind)
            after_conv, linear, gate, normed_two = conv_forward(
                after_attn, before, behind, gain(2), gain(3), w_conv, kernel, masks
            )
            own_product, pre_second = ffn_part(normed_two, w_two, UP2, DOWN2, 2 * rank, 2, True)
            (two, beside), (own_product, pre_second, w_two) = together(
                [(send_two, "mp"), (more_two, "core")], own_product, pre_second, w_two
            )
            w_two = put(w_two, more_two, beside, 3, 64)
            two, *send_one = tied(two, *send_one)
            (beside,), (w_two,) = together([(two, "core")], w_two)
            w_two = put(w_two, two, beside, 3, 112)
            product, pre_second = ffn_part(
                normed_two, w_two, UP2, DOWN2, 2 * across, 2, True, pre_second
            )
            after_second, output = join(after_conv, [own_product, product], gain(4))
            sources = [(normed_attn, rank), (other, across)]
        else:
            everything = lax.all_gather(low, ("mp", "z", "x", "core"), axis=0, tiled=True)
            slot_of = owners_all + jnp.arange(ranks)[:, None] * slots
            arrays = []
            for number, chunks in enumerate(GROUP_CHUNKS):
                here = slice(starts[number], starts[number + 1])
                arrays += unsort(
                    everything, slot_of[:, here].reshape(-1).astype(jnp.int32),
                    places[:, here].reshape(-1), chunks, False,
                )
            w_one, w_attn, w_conv, w_two = arrays
            after_first, pre_first, normed_attn = ffn_forward(
                stream, gain(0), gain(1), w_one, UP1, DOWN1
            )
            other = lax.all_gather(normed_attn, "mp", axis=0, tiled=True)
            queries = project(normed_attn, w_attn, QUERY, 1)
            keys = project(other, w_attn, KEY, 2)
            sources = [(other, 0)]
            attended, logs = attention_forward(
                queries, keys, segment_ids, rank, windows, slopes
            )
            after_attn = project_out(attended, w_attn, OUT, after_first)
            before, behind = edges(after_attn[:HALO], after_attn[-HALO:], ranks)
            after_conv, linear, gate, normed_two = conv_forward(
                after_attn, before, behind, gain(2), gain(3), w_conv, kernel, masks
            )
            after_second, pre_second, output = ffn_forward(
                after_conv, gain(3), gain(4), w_two, UP2, DOWN2
            )

        if fast:
            last = 32 * ROUNDS[LARGE]
            sums = ((ranks * slots - last, BLOCK, BLOCK), (last, BLOCK, BLOCK))
        else:
            sums = ((ranks * slots, BLOCK, BLOCK),)
            if slots > blocks:
                sums = (jnp.zeros(sums[0], bf16),)
        grad_conv, gains_a, *sums = ffn_backward(
            after_second, gain(4), [cotangent], None, after_conv, gain(3), pre_second, w_two,
            UP2, DOWN2, sums, table, ranks,
        )
        if fast:
            (come_one,), (grad_conv, gains_a, *sums) = together(
                [(send_one[0], "mp")], grad_conv, gains_a, *sums
            )
            rounds = Rounds(*sums)
            rounds.add_round(0)
            sums = rounds.hold()
        before, behind = edges(
            grad_conv[:HALO].astype(bf16), grad_conv[-HALO:].astype(bf16), ranks
        )
        if fast:
            send_last, before, behind = tied(send_one[1], before, behind)
        grad_attn, gains_b, tap_grads, *sums = conv_backward(
            grad_conv, before, behind, after_attn, gain(2), linear, gate, w_conv, kernel, masks,
            sums, table, ranks,
        )
        if fast:
            rounds.add("first", both_swaps(come_one, ["core"]))
            rounds.add("second", both_swaps(send_last, ["mp", "core"]))
            grad_attn, gains_b, tap_grads = rounds.step(
                [0, "first", "second"], grad_attn, gains_b, tap_grads, sums=sums
            )
            rounds.add_round(1)
            sums = rounds.hold()
        mixed_grad, *sums = project_out_back(
            grad_attn, w_attn, OUT, attended, sums, table, ranks
        )
        query_grad, key_grad, value_grad = attention_backward(
            queries, keys, segment_ids, rank, windows, slopes, logs, mixed_grad, attended
        )
        if fast:
            away = input_gradient(key_grad, value_grad, w_attn, 1 - rank, rows)
            query_grad, key_grad, value_grad, away = rounds.step(
                [0, 1, "second"], query_grad, key_grad, value_grad, away, sums=sums
            )
            sums = rounds.hold()
        else:
            away = input_gradient(key_grad, value_grad, w_attn, jnp.zeros((), jnp.int32), group)
            arrived = lax.psum_scatter(away, "mp", scatter_dimension=0, tiled=True)
        near, *sums = projections_back(
            normed_attn, query_grad, key_grad, value_grad, sources, fast, w_attn, sums, table, ranks
        )
        if fast:
            (beside,), (second, more) = rounds.results.pop("first"), rounds.results.pop("second")
            beside, more, away = tied(beside, more, away)
            w_one = put(put(w_one, come_one, beside, 0, 0), second, more, 0, 128)
            rounds.add("away", both_swaps(away, ["mp"]))
            near, w_one = rounds.step(["away"], near, w_one, sums=sums)
            (arrived,) = rounds.results.pop("away")
            rounds.add_round(2)
            sums = rounds.hold()
        first_args = (gain(0), pre_first, w_one, UP1, DOWN1)
        if fast:
            middle = FF // 512 // 2
            so_far, gains_c, *sums, carry = ffn_backward(
                after_first, gain(1), [near, arrived], grad_attn, stream, *first_args, sums, table,
                ranks, rank, 0, middle,
            )
            so_far, gains_c, carry = rounds.step([0, 1, 2], so_far, gains_c, carry, sums=sums)
            sums = rounds.hold()
            stream_grad, gains_d, *sums = ffn_backward(
                None, None, [], so_far, stream, *first_args, sums, table, ranks, rank, middle,
                carry=carry,
            )
            stream_grad, gains_d = rounds.step([1, 2], stream_grad, gains_d, sums=sums)
            gains_c = jnp.concatenate([gains_c[0:1], gains_d[1:2]])
        else:
            stream_grad, gains_c, *sums = ffn_backward(
                after_first, gain(1), [near, arrived], grad_attn, stream, *first_args, sums, table,
                ranks,
            )
        small = jnp.concatenate(
            [gains_c[1:2], gains_c[0:1], gains_b, gains_a[1:2], gains_a[0:1], tap_grads]
        )
        everywhere = ("mp", "z", "x", "core")
        if fast:
            rounds.add("small", total_steps(small))
            sums = (rounds.sums, rounds.tail)
            own_grads = finish_rounds(rounds)
            small = rounds.results["small"]
            own_grads = lax.cond(
                good,
                lambda sums, tail, own: own,
                lambda sums, tail, own: all_rounds(sums, tail),
                *sums,
                own_grads,
            )
        else:
            own_grads = lax.psum_scatter(sums[0], everywhere, scatter_dimension=0, tiled=True)
            small = lax.psum(small, everywhere)
        gain_grads, kernel_grads = small[:5], small[5:]
        block_grads, left_new, right_new, master_new, average_new = shampoo(
            own_grads, arrivals, left_stats[0], right_stats[0], left_root[0], right_root[0], master[0],
            average[0],
        )
        return (
            output,
            stream_grad,
            block_grads[None],
            left_new[None],
            right_new[None],
            master_new[None],
            average_new[None],
            gain_grads,
            vector_step(gains, gain_grads),
            kernel_grads,
            vector_step(kernel, kernel_grads),
        )

    return run


def solution(mesh):
    ranks, pieces = mesh.shape["mp"], mesh.shape["dp"]
    fast = ranks == 2 and pieces == 16
    xs = 2 if fast else 1
    grid = Mesh(
        np.asarray(mesh.devices).reshape(ranks, pieces // (2 * xs), xs, 2), ("mp", "z", "x", "core")
    )
    dp = ("z", "x", "core")
    rows = P((*dp, "mp"), None)
    slots = P("mp", dp, None, None)
    return jax.shard_map(
        local(fast),
        mesh=grid,
        in_specs=(
            rows, rows, P(dp, None), P("mp", None), slots, slots, slots, slots, slots, slots, P(),
            P(),
        ),
        out_specs=(rows, rows, slots, slots, slots, slots, slots, P(), P(), P(), P()),
        check_vma=False,
    )
```

```python
import math

import jax
import jax.numpy as jnp
import numpy as np
from jax import lax
from jax.experimental import pallas as pl
from jax.experimental.pallas import tpu as pltpu
from jax.sharding import Mesh
from jax.sharding import PartitionSpec as P

D = 1024
FF = 4096
HEADS = 8
HEAD_DIM = 128
KERNEL = 5
STEP = 4
BLOCK = 128
HALO = 16
WIDE = 8

EPSILON = 1e-05
DECAY_STAT = 0.95
RATE_BLOCK = 0.02
RATE_VECTOR = 0.2
DECAY_AVERAGE = 0.9999
MASKED = -1e30
LOG2E = math.log2(math.e)
SCORE_SCALE = 1.0 / math.sqrt(HEAD_DIM)

f32 = jnp.float32
bf16 = jnp.bfloat16
ANY = pl.BlockSpec(memory_space=pl.ANY)
SMEM = pl.BlockSpec(memory_space=pltpu.SMEM)

MATRICES = [
    (0, 0, D, FF, True),
    (0, 4, FF, D, False),
    (1, 0, D, D, True),
    (1, 1, D, D, True),
    (1, 2, D, D, True),
    (1, 3, D, D, False),
    (2, 0, D, D, True),
    (2, 1, D, D, True),
    (2, 2, D, D, False),
    (3, 0, D, FF, True),
    (3, 4, FF, D, False),
]
UP1, DOWN1, QUERY, KEY, VALUE, OUT, CONV_VALUE, CONV_GATE, CONV_OUT, UP2, DOWN2 = range(11)
GROUPS = [(0, 2), (2, 6), (6, 9), (9, 11)]
GROUP_CHUNKS = [8, 4, 3, 8]


def at(matrix):
    return MATRICES[matrix][1]


ROUNDS = [4, 3, 4, 9, 3]
LARGE = 3
EARLY = [9, 6, 2]


def params(**kw):
    return pltpu.CompilerParams(vmem_limit_bytes=58 * 2**20, **kw)


def const_spec(shape):
    return pl.BlockSpec(shape, lambda *ids: (0,) * len(shape), pipeline_mode=pl.Buffered(1))


def row_tile(rows):
    return 256 if rows % 256 == 0 else 128


def cost(flops, moved):
    return pl.CostEstimate(flops=int(flops), bytes_accessed=int(moved), transcendentals=0)


def offsets(ranks):
    out = []
    offset = 0
    for unused, unused_chunk, height, breadth, by_columns in MATRICES:
        out.append(offset)
        offset = offset + height * breadth // (BLOCK * BLOCK * ranks)
    return out, offset


def block_number(matrix, row_block, column_block, ranks):
    starts, total = offsets(ranks)
    unused, unused_chunk, height, breadth, by_columns = MATRICES[matrix]
    if by_columns:
        part = breadth // BLOCK // ranks
        return (
            (column_block // part) * total + starts[matrix] + row_block * part + column_block % part
        )
    part = height // BLOCK // ranks
    breadth_blocks = breadth // BLOCK
    return (
        (row_block // part) * total
        + starts[matrix]
        + (row_block % part) * breadth_blocks
        + column_block
    )


def weight_places(ranks):
    unused, total = offsets(ranks)
    places = np.zeros((ranks * total,), np.int32)
    for matrix, (unused, chunk, height, breadth, by_columns) in enumerate(MATRICES):
        for row in range(height // BLOCK):
            for column in range(breadth // BLOCK):
                place = ((chunk + column // WIDE) * 8 + row) * WIDE + column % WIDE
                places[block_number(matrix, row, column, ranks)] = place
    return places.reshape(ranks, total)


def copy_in_place(out, source, place, sem):
    row = pl.multiple_of((place // WIDE) * BLOCK, BLOCK)
    column = pl.multiple_of((place % WIDE) * BLOCK, BLOCK)
    pltpu.make_async_copy(
        source, out.at[pl.ds(row, BLOCK), pl.ds(column, BLOCK)], sem
    ).start()


def unsort(slots, sources, places, chunks, into=None):
    count = sources.shape[0]
    each = max(n for n in range(1, 65) if count % n == 0)
    steps = count // each

    def body(source_ref, place_ref, slots_ref, *rest):
        out, held, read_sem, write_sem = rest[-4:]
        step = pl.program_id(0)
        slot = lax.rem(step, 2)

        def read(number, into):
            def one(n, unused):
                pltpu.make_async_copy(
                    slots_ref.at[source_ref[number * each + n]], held.at[into, n], read_sem.at[into]
                ).start()
                return unused

            lax.fori_loop(0, each, one, 0)

        def written(number, into):
            pltpu.make_async_copy(held.at[into], held.at[into], write_sem.at[into]).wait()

        @pl.when(step == 0)
        def _():
            read(0, 0)

        @pl.when(step >= 1)
        def _():
            written(step - 1, 1 - slot)

        @pl.when(step + 1 < steps)
        def _():
            read(step + 1, 1 - slot)

        pltpu.make_async_copy(held.at[slot], held.at[slot], read_sem.at[slot]).wait()

        def one(n, unused):
            copy_in_place(out, held.at[slot, n], place_ref[step * each + n], write_sem.at[slot])
            return unused

        lax.fori_loop(0, each, one, 0)

        @pl.when(step == steps - 1)
        def _():
            written(step, slot)

    operands = [sources, places, slots]
    if into is not None:
        operands.append(into)
    return pl.pallas_call(
        body,
        grid=(steps,),
        out_shape=jax.ShapeDtypeStruct((chunks * D, D), bf16),
        in_specs=[SMEM, SMEM] + [ANY] * (len(operands) - 2),
        out_specs=ANY,
        scratch_shapes=[
            pltpu.VMEM((2, each, BLOCK, BLOCK), bf16),
            pltpu.SemaphoreType.DMA((2,)),
            pltpu.SemaphoreType.DMA((2,)),
        ],
        input_output_aliases={} if into is None else {3: 0},
        compiler_params=params(has_side_effects=True),
        cost_estimate=cost(0, 2 * count * BLOCK * BLOCK * 2),
        name="unsort",
    )(*operands)


PAIR = [(0, 1), (1, 0)]
MOVES = {
    "x": ("x", PAIR),
    "mp": ("mp", PAIR),
    "core": ("core", PAIR),
    "near": ("z", [(0, 1), (1, 0), (2, 3), (3, 2)]),
    "far": ("z", [(0, 2), (2, 0), (1, 3), (3, 1)]),
    "both": (("x", "core"), [(n, 3 - n) for n in range(4)]),
    "across": (("mp", "z"), [(n, (n // 4 * 4) ^ 4 | (n % 4) ^ 1) for n in range(8)]),
}
for _step in (-3, -2, -1, 1, 2, 3):
    MOVES[_step] = ("z", [(z, z + _step) for z in range(4) if 0 <= z + _step < 4])


def swap(value, move):
    axis, pairs = MOVES[move]
    return lax.ppermute(value, axis, pairs)


def tied(*values):
    return lax.optimization_barrier(values)


def together(transfers, *held):
    values = tied(*[value for value, unused in transfers])
    arrived = [swap(value, move) for value, (unused, move) in zip(values, transfers)]
    out = tied(*arrived, *held)
    return list(out[: len(arrived)]), out[len(arrived) :]


def sigmoid(values):
    return 0.5 * jnp.tanh(0.5 * values) + 0.5


def norm_parts(values):
    center = values - jnp.mean(values, axis=-1, keepdims=True)
    spread = jnp.mean(center * center, axis=-1, keepdims=True)
    scale = lax.rsqrt(spread + EPSILON)
    return center * scale, scale


def norm(values, gain):
    return norm_parts(values)[0] * gain


def norm_back(values, gain, grad):
    hat, scale = norm_parts(values)
    inner = grad * gain
    mean_inner = jnp.mean(inner, axis=-1, keepdims=True)
    mean_hat = jnp.mean(inner * hat, axis=-1, keepdims=True)
    return (
        scale * (inner - mean_inner - hat * mean_hat),
        jnp.sum(grad * hat, axis=0, keepdims=True),
    )


def dot(a, b):
    return jnp.dot(a, b, preferred_element_type=f32)


def dot_right(a, b):
    return lax.dot_general(a, b, (((1,), (1,)), ((), ())), preferred_element_type=f32)


def dot_left(a, b):
    return lax.dot_general(a, b, (((0,), (0,)), ((), ())), preferred_element_type=f32)


def start_blocks(table, targets, source, sem, matrix, row_block, column_block, ranks):
    height, breadth = source.shape
    for i in range(height // BLOCK):
        for j in range(breadth // BLOCK):
            place = table[block_number(matrix, row_block + i, column_block + j, ranks)]
            block = source.at[pl.ds(i * BLOCK, BLOCK), pl.ds(j * BLOCK, BLOCK)]
            if len(targets) == 1:
                pltpu.make_async_copy(block, targets[0].at[place], sem).start()
                continue
            limit = targets[0].shape[0]

            @pl.when(place < limit)
            def _(place=place, block=block):
                pltpu.make_async_copy(block, targets[0].at[place], sem).start()

            @pl.when(place >= limit)
            def _(place=place, block=block):
                pltpu.make_async_copy(block, targets[1].at[place - limit], sem).start()


def wait_blocks(source, sem):
    pltpu.make_async_copy(source, source, sem).wait()


def ffn_forward(stream, gain, next_gain, weights, upper, lower):
    rows = stream.shape[0]
    tile = row_tile(rows)
    wide = D
    steps = FF // wide

    def body(x_ref, gain_ref, next_gain_ref, up_ref, down_ref, out_ref, pre_ref, next_ref, normed):
        step = pl.program_id(0)

        @pl.when(step == 0)
        def _():
            for t in range(0, rows, tile):
                x = x_ref[t : t + tile].astype(f32)
                normed[t : t + tile] = norm(x, gain_ref[...]).astype(bf16)
                out_ref[t : t + tile] = jnp.zeros((tile, D), f32)

        for t in range(0, rows, tile):
            pre = dot(normed[t : t + tile], up_ref[...])
            pre_ref[t : t + tile] = pre.astype(bf16)
            act = (pre * sigmoid(pre)).astype(bf16)
            out_ref[t : t + tile] += dot(act, down_ref[...])

        @pl.when(step == steps - 1)
        def _():
            for t in range(0, rows, tile):
                y = x_ref[t : t + tile].astype(f32) + 0.5 * out_ref[t : t + tile]
                out_ref[t : t + tile] = y
                next_ref[t : t + tile] = norm(y, next_gain_ref[...]).astype(bf16)

    return pl.pallas_call(
        body,
        grid=(steps,),
        out_shape=(
            jax.ShapeDtypeStruct((rows, D), f32),
            jax.ShapeDtypeStruct((rows, FF), bf16),
            jax.ShapeDtypeStruct((rows, D), bf16),
        ),
        in_specs=[
            const_spec((rows, D)),
            const_spec((1, D)),
            const_spec((1, D)),
            pl.BlockSpec((D, wide), lambda f: (at(upper) + f, 0)),
            pl.BlockSpec((wide, D), lambda f: (at(lower) + f, 0)),
        ],
        out_specs=(
            const_spec((rows, D)),
            pl.BlockSpec((rows, wide), lambda f: (0, f)),
            const_spec((rows, D)),
        ),
        scratch_shapes=[pltpu.VMEM((rows, D), bf16)],
        compiler_params=params(),
        cost_estimate=cost(4 * rows * D * FF, 4 * D * FF + 2 * rows * FF),
        name="ffn_forward",
    )(stream, gain, next_gain, weights, weights)


def norm_rows(values, gain):
    rows = values.shape[0]
    tile = row_tile(rows)

    def body(x_ref, gain_ref, out_ref):
        out_ref[...] = norm(x_ref[...].astype(f32), gain_ref[...]).astype(bf16)

    spec = pl.BlockSpec((tile, D), lambda t: (t, 0))
    return pl.pallas_call(
        body,
        grid=(rows // tile,),
        out_shape=jax.ShapeDtypeStruct((rows, D), bf16),
        in_specs=[spec, const_spec((1, D))],
        out_specs=spec,
        compiler_params=params(),
        name="norm_rows",
    )(values, gain)


def ffn_part(normed, weights, upper, lower, first, steps, keep, pre=None):
    rows = normed.shape[0]
    tile = row_tile(rows)

    def body(part_ref, x_ref, up_ref, down_ref, *rest):
        out_ref = rest[-3] if keep else rest[-2]
        pre_ref = rest[-2]
        total = rest[-1]
        step = pl.program_id(0)
        for t in range(0, rows, tile):
            here = slice(t, t + tile)
            value = dot(x_ref[here], up_ref[...])
            if keep:
                pre_ref[here] = value.astype(bf16)
            act = (value * sigmoid(value)).astype(bf16)
            new = dot(act, down_ref[...])

            if steps == 1:
                out_ref[here] = new.astype(bf16)
                continue

            @pl.when(step == 0)
            def _(new=new, here=here):
                total[here] = new

            @pl.when((step > 0) & (step < steps - 1))
            def _(new=new, here=here):
                total[here] += new

            @pl.when(step == steps - 1)
            def _(new=new, here=here):
                out_ref[here] = (total[here] + new).astype(bf16)

    operands = [first.reshape(1), normed, weights, weights]
    specs = [
        pl.BlockSpec((rows, D), lambda f, p: (0, 0), pipeline_mode=pl.Buffered(1)),
        pl.BlockSpec((D, D), lambda f, p: (at(upper) + p[0] + f, 0)),
        pl.BlockSpec((D, D), lambda f, p: (at(lower) + p[0] + f, 0)),
    ]
    shapes = [jax.ShapeDtypeStruct((rows, D), bf16)]
    out_specs = [pl.BlockSpec((rows, D), lambda f, p: (0, 0), pipeline_mode=pl.Buffered(1))]
    aliases = {}
    if keep:
        shapes.append(jax.ShapeDtypeStruct((rows, FF), bf16))
        out_specs.append(pl.BlockSpec((rows, D), lambda f, p: (0, p[0] + f)))
        if pre is not None:
            aliases = {len(operands): 1}
            operands.append(pre)
            specs.append(ANY)
    return pl.pallas_call(
        body,
        grid_spec=pltpu.PrefetchScalarGridSpec(
            num_scalar_prefetch=1,
            grid=(steps,),
            in_specs=specs,
            out_specs=tuple(out_specs),
            scratch_shapes=[pltpu.VMEM((rows, D), f32)],
        ),
        out_shape=tuple(shapes),
        input_output_aliases=aliases,
        compiler_params=params(),
        cost_estimate=cost(4 * rows * D * D * steps, 4 * D * D * steps),
        name="ffn_part",
    )(*operands)


def join(base, products, next_gain):
    rows = base.shape[0]
    tile = row_tile(rows)
    count = len(products)

    def body(base_ref, *refs):
        gain_ref, out_ref, next_ref = refs[count:]
        both = refs[0][...].astype(f32)
        for ref in refs[1:count]:
            both = both + ref[...].astype(f32)
        y = base_ref[...].astype(f32) + 0.5 * both
        out_ref[...] = y
        next_ref[...] = norm(y, gain_ref[...]).astype(bf16)

    spec = pl.BlockSpec((tile, D), lambda t: (t, 0))
    return pl.pallas_call(
        body,
        grid=(rows // tile,),
        out_shape=(
            jax.ShapeDtypeStruct((rows, D), f32),
            jax.ShapeDtypeStruct((rows, D), bf16),
        ),
        in_specs=[spec] * (count + 1) + [const_spec((1, D))],
        out_specs=(spec, spec),
        compiler_params=params(),
        name="join",
    )(base, *products, next_gain)


def ffn_backward(
    after, after_gain, after_grads, base, stream, gain, pre, weights, upper, lower, sums, table,
    ranks, kept=None, first=0, last=None, carry=None,
):
    rows = stream.shape[0]
    tile = row_tile(rows)
    wide = 512
    steps = (FF // wide if last is None else last) - first
    whole = FF // wide
    parts = len(after_grads)
    targets = len(sums)
    with_base = base is not None
    again = kept is not None

    def body(table_ref, *refs):
        refs = list(refs)
        at_ref = 0
        if parts > 0:
            after_ref, after_gain_ref = refs[0], refs[1]
            grad_refs = refs[2 : 2 + parts]
            at_ref = 2 + parts
        base_ref = None
        if with_base:
            base_ref = refs[at_ref]
            at_ref += 1
        x_ref, gain_ref, up_ref, down_ref, pre_ref = refs[at_ref : at_ref + 5]
        kept_ref = refs[at_ref + 5]
        outs = refs[at_ref + 5 + again + (carry is not None) + aliased :]
        out_ref, gains_ref = outs[:2]
        sums_ref = outs[2 : 2 + targets]
        carry_ref = refs[at_ref + 5 + again]
        grad_sum = outs[2 + targets]
        (
            half, normed, pre_here, normed_t, pre_grad, act_t, up_part, down_part, up_sem, down_sem,
        ) = outs[3 + targets :]
        step = pl.program_id(0)

        @pl.when(step == 0)
        def _():
            gain_sum = jnp.zeros((1, D), f32)
            for t in range(0, rows, tile):
                here = slice(t, t + tile)
                if parts == 0:
                    back = base_ref[here]
                else:
                    grad = grad_refs[0][here].astype(f32)
                    for other in grad_refs[1:]:
                        grad = grad + other[here].astype(f32)
                    back, part = norm_back(after_ref[here], after_gain_ref[...], grad)
                    gain_sum = gain_sum + part
                    if with_base:
                        back = back + base_ref[here]
                out_ref[here] = back
                half[here] = (0.5 * back).astype(bf16)
                low = norm(x_ref[here].astype(f32), gain_ref[...]).astype(bf16)
                if again:
                    normed[here] = low
                normed_t[:, here] = low.T
                grad_sum[here] = jnp.zeros((tile, D), f32) if carry is None else carry_ref[here]
            gains_ref[0:1] = gain_sum

        if again:

            @pl.when((first + step) // (whole // 2) == kept_ref[0])
            def _():
                pre_here[...] = pre_ref[...]

            @pl.when((first + step) // (whole // 2) != kept_ref[0])
            def _():
                for t in range(0, rows, tile):
                    here = slice(t, t + tile)
                    pre_here[here] = dot(normed[here], up_ref[...]).astype(bf16)

        for t in range(0, rows, tile):
            here = slice(t, t + tile)
            act_grad = dot_right(half[here], down_ref[...])
            pre_act = (pre_here if again else pre_ref)[here].astype(f32)
            sigma = sigmoid(pre_act)
            act = pre_act * sigma
            act_t[:, here] = act.astype(bf16).T
            slope = sigma + act * (1.0 - sigma)
            moved = (act_grad * slope).astype(bf16)
            pre_grad[here] = moved
            grad_sum[here] += dot_right(moved, up_ref[...])

        @pl.when(step >= 1)
        def _():
            wait_blocks(up_part, up_sem)
            wait_blocks(down_part, down_sem)

        for t in range(0, D, 256):
            up_part[t : t + 256] = dot(normed_t[t : t + 256], pre_grad[...]).astype(bf16)
        for t in range(0, wide, 256):
            down_part[t : t + 256] = dot(act_t[t : t + 256], half[...]).astype(bf16)
        start_blocks(
            table_ref, sums_ref, up_part, up_sem, upper, 0, (first + step) * 4, ranks
        )
        start_blocks(
            table_ref, sums_ref, down_part, down_sem, lower, (first + step) * 4, 0, ranks
        )

        @pl.when(step == steps - 1)
        def _():
            wait_blocks(up_part, up_sem)
            wait_blocks(down_part, down_sem)
            if last is not None:
                return
            gain_sum = jnp.zeros((1, D), f32)
            for t in range(0, rows, tile):
                here = slice(t, t + tile)
                back, part = norm_back(x_ref[here].astype(f32), gain_ref[...], grad_sum[here])
                gain_sum = gain_sum + part
                out_ref[here] += back
            gains_ref[1:2] = gain_sum

    operands = [table]
    specs = [SMEM]
    if parts > 0:
        operands += [after, after_gain, *after_grads]
        specs += [const_spec((rows, D)), const_spec((1, D))] + [const_spec((rows, D))] * parts
    if with_base:
        operands.append(base)
        specs.append(const_spec((rows, D)))
    operands += [stream, gain, weights, weights]
    specs += [
        const_spec((rows, D)),
        const_spec((1, D)),
        pl.BlockSpec((D, wide), lambda f: (at(upper) + (first + f) // 2, (first + f) % 2)),
        pl.BlockSpec((wide, D), lambda f: (at(lower) * 2 + first + f, 0)),
    ]
    operands.append(pre)
    specs.append(pl.BlockSpec((rows, wide), lambda f: (0, first + f)))
    if again:
        operands.append(kept.reshape(1))
        specs.append(SMEM)
    if carry is not None:
        operands.append(carry)
        specs.append(const_spec((rows, D)))
    aliases = {}
    aliased = 0 if isinstance(sums[0], tuple) else targets
    if not isinstance(sums[0], tuple):
        for n, target in enumerate(sums):
            aliases[len(operands)] = 2 + n
            operands.append(target)
            specs.append(ANY)
        sums = [target.shape for target in sums]
    return pl.pallas_call(
        body,
        grid=(steps,),
        out_shape=(
            jax.ShapeDtypeStruct((rows, D), f32),
            jax.ShapeDtypeStruct((2, D), f32),
            *[jax.ShapeDtypeStruct(shape, bf16) for shape in sums],
        )
        + ((jax.ShapeDtypeStruct((rows, D), f32),) if last is not None else ()),
        in_specs=specs,
        out_specs=(const_spec((rows, D)), const_spec((2, D)))
        + (ANY,) * targets
        + ((const_spec((rows, D)),) if last is not None else ()),
        scratch_shapes=([pltpu.VMEM((rows, D), f32)] if last is None else [])
        + [
            pltpu.VMEM((rows, D), bf16),
            pltpu.VMEM((rows, D) if again else (16, 128), bf16),
            pltpu.VMEM((rows, wide) if again else (16, 128), bf16),
            pltpu.VMEM((D, rows), bf16),
            pltpu.VMEM((rows, wide), bf16),
            pltpu.VMEM((wide, rows), bf16),
            pltpu.VMEM((D, wide), bf16),
            pltpu.VMEM((wide, D), bf16),
            pltpu.SemaphoreType.DMA,
            pltpu.SemaphoreType.DMA,
        ],
        input_output_aliases=aliases,
        compiler_params=params(has_side_effects=True),
        cost_estimate=cost(8 * rows * D * wide * steps, 8 * D * wide * steps),
        name="ffn_backward",
    )(*operands)


def project(values, weights, first, count, part=None, parts=1, into=None):
    rows = values.shape[0]
    tile = row_tile(rows)
    wide = D

    def body(part_ref, x_ref, w_ref, *rest):
        out_ref = rest[-1]
        for t in range(0, rows, tile):
            out_ref[t : t + tile] = dot(x_ref[t : t + tile], w_ref[...]).astype(bf16)

    operands = [jnp.asarray(0 if part is None else part, jnp.int32).reshape(1), values, weights]
    specs = [
        pl.BlockSpec((rows, D), lambda f, part: (0, 0), pipeline_mode=pl.Buffered(1)),
        pl.BlockSpec((D, wide), lambda f, part: (at(first) + f, 0)),
    ]
    aliases = {}
    if into is not None:
        aliases = {3: 0}
        operands.append(into)
        specs.append(ANY)
    return pl.pallas_call(
        body,
        grid_spec=pltpu.PrefetchScalarGridSpec(
            num_scalar_prefetch=1,
            grid=(count,),
            in_specs=specs,
            out_specs=pl.BlockSpec((rows, wide), lambda f, part: (part[0], f)),
        ),
        out_shape=jax.ShapeDtypeStruct((parts * rows, count * D), bf16),
        input_output_aliases=aliases,
        compiler_params=params(),
        cost_estimate=cost(2 * rows * D * D * count, 2 * count * D * (D + rows)),
        name="project",
    )(*operands)


def project_out(values, weights, matrix, stream):
    rows = values.shape[0]
    tile = row_tile(rows)

    def body(x_ref, w_ref, s_ref, out_ref):
        out_ref[...] = s_ref[...] + dot(x_ref[...], w_ref[...])

    return pl.pallas_call(
        body,
        grid=(rows // tile,),
        out_shape=jax.ShapeDtypeStruct((rows, D), f32),
        in_specs=[
            pl.BlockSpec((tile, D), lambda t: (t, 0)),
            pl.BlockSpec((D, D), lambda t: (at(matrix), 0)),
            pl.BlockSpec((tile, D), lambda t: (t, 0)),
        ],
        out_specs=pl.BlockSpec((tile, D), lambda t: (t, 0)),
        compiler_params=params(),
        cost_estimate=cost(2 * rows * D * D, 2 * D * D + 10 * rows * D),
        name="project_out",
    )(values, weights, stream)


def project_out_back(grad, weights, matrix, attended, sums, table, ranks):
    rows = grad.shape[0]
    tile = row_tile(rows)
    wide = 512

    targets = len(sums)

    def body(table_ref, g_ref, w_ref, a_ref, *refs):
        out_ref = refs[targets]
        sums_ref = refs[targets + 1 : 2 * targets + 1]
        low, part, sem = refs[2 * targets + 1 :]
        step = pl.program_id(0)

        @pl.when(step == 0)
        def _():
            for t in range(0, rows, tile):
                low[t : t + tile] = g_ref[t : t + tile].astype(bf16)

        for t in range(0, rows, tile):
            out_ref[t : t + tile] = dot_right(low[t : t + tile], w_ref[...]).astype(bf16)
        for t in range(0, wide, 256):
            part[step, t : t + 256] = dot_left(a_ref[:, t : t + 256], low[...]).astype(bf16)
        start_blocks(table_ref, sums_ref, part.at[step], sem.at[step], matrix, step * 4, 0, ranks)

        @pl.when(step == 1)
        def _():
            for s in range(2):
                wait_blocks(part.at[s], sem.at[s])

    return pl.pallas_call(
        body,
        grid=(2,),
        out_shape=(
            jax.ShapeDtypeStruct((rows, D), bf16),
            *[jax.ShapeDtypeStruct(target.shape, bf16) for target in sums],
        ),
        in_specs=[
            SMEM,
            const_spec((rows, D)),
            pl.BlockSpec((wide, D), lambda f: (at(matrix) * 2 + f, 0)),
            pl.BlockSpec((rows, wide), lambda f: (0, f)),
        ]
        + [ANY] * targets,
        out_specs=(pl.BlockSpec((rows, wide), lambda f: (0, f)),) + (ANY,) * targets,
        scratch_shapes=[
            pltpu.VMEM((rows, D), bf16),
            pltpu.VMEM((2, wide, D), bf16),
            pltpu.SemaphoreType.DMA((2,)),
        ],
        input_output_aliases={4 + n: 1 + n for n in range(targets)},
        compiler_params=params(has_side_effects=True),
        cost_estimate=cost(4 * rows * D * D, 4 * D * D + 8 * rows * D),
        name="project_out_back",
    )(table, grad, weights, attended, *sums)


def input_gradient(key_grad, value_grad, weights, part, rows):
    tile = row_tile(rows)
    steps = rows // tile

    def body(part_ref, k_ref, v_ref, wk_ref, wv_ref, out_ref):
        out_ref[...] = (
            dot_right(k_ref[...], wk_ref[...]) + dot_right(v_ref[...], wv_ref[...])
        ).astype(bf16)

    return pl.pallas_call(
        body,
        grid_spec=pltpu.PrefetchScalarGridSpec(
            num_scalar_prefetch=1,
            grid=(steps,),
            in_specs=[
                pl.BlockSpec((tile, D), lambda t, part: (part[0] * steps + t, 0)),
                pl.BlockSpec((tile, D), lambda t, part: (part[0] * steps + t, 0)),
                pl.BlockSpec((D, D), lambda t, part: (at(KEY), 0)),
                pl.BlockSpec((D, D), lambda t, part: (at(VALUE), 0)),
            ],
            out_specs=pl.BlockSpec((tile, D), lambda t, part: (t, 0)),
        ),
        out_shape=jax.ShapeDtypeStruct((rows, D), bf16),
        compiler_params=params(),
        cost_estimate=cost(4 * rows * D * D, 4 * D * D + 6 * rows * D),
        name="input_gradient",
    )(part.reshape(1), key_grad, value_grad, weights, weights)


def projections_back(
    normed, query_grad, key_grad, value_grad, sources, own_keys, weights, sums, table, ranks
):
    rows = normed.shape[0]
    tile = row_tile(rows)
    wide = 512
    count = len(sources)
    targets = len(sums)
    lengths = [source[0].shape[0] for source in sources]

    def body(part_ref, table_ref, n_ref, q_ref, *refs):
        normed_refs = refs[:count]
        key_refs = refs[count : 2 * count]
        value_refs = refs[2 * count : 3 * count]
        w_ref = refs[3 * count]
        outs = refs[3 * count + 1 + targets :]
        out_ref, sums_ref, scratch = outs[0], outs[1 : 1 + targets], outs[1 + targets :]
        own_t = scratch[0]
        source_t = scratch[1 : 1 + count]
        part, sem = scratch[1 + count :]
        step = pl.program_id(0)
        slot = lax.rem(step, 2)

        @pl.when(step == 0)
        def _():
            for t in range(0, rows, tile):
                own_t[:, t : t + tile] = n_ref[t : t + tile].T
            for n_from, n_to, length in zip(normed_refs, source_t, lengths):
                small = row_tile(length)
                for t in range(0, length, small):
                    n_to[:, t : t + small] = n_from[t : t + small].T

        @pl.when(step >= 2)
        def _():
            wait_blocks(part.at[slot], sem.at[slot])

        @pl.when(step < 2)
        def _():
            for t in range(0, rows, tile):
                new = dot_right(q_ref[t : t + tile], w_ref[...])

                @pl.when(step == 0)
                def _():
                    out_ref[t : t + tile] = new

                @pl.when(step == 1)
                def _():
                    out_ref[t : t + tile] += new

            for t in range(0, D, 256):
                part[slot, t : t + 256] = dot(own_t[t : t + 256], q_ref[...]).astype(bf16)
            start_blocks(
                table_ref, sums_ref, part.at[slot], sem.at[slot], QUERY, 0, lax.rem(step, 2) * 4,
                ranks,
            )

        def other(grad_refs, matrix):
            if own_keys:
                for t in range(0, rows, tile):
                    out_ref[t : t + tile] += dot_right(grad_refs[0][t : t + tile], w_ref[...])
            for t in range(0, D, 256):
                total = dot(source_t[0][t : t + 256], grad_refs[0][...])
                for n_t, grad_ref in zip(source_t[1:], grad_refs[1:]):
                    total = total + dot(n_t[t : t + 256], grad_ref[...])
                part[slot, t : t + 256] = total.astype(bf16)
            start_blocks(
                table_ref, sums_ref, part.at[slot], sem.at[slot], matrix, 0, lax.rem(step, 2) * 4,
                ranks,
            )

        @pl.when((step >= 2) & (step < 4))
        def _():
            other(key_refs, KEY)

        @pl.when(step >= 4)
        def _():
            other(value_refs, VALUE)

        @pl.when(step == 5)
        def _():
            for s in range(2):
                wait_blocks(part.at[s], sem.at[s])

    parts = jnp.stack([jnp.asarray(source[1], jnp.int32) for source in sources])
    operands = [parts, table, normed, query_grad]

    def whole(shape):
        return pl.BlockSpec(shape, lambda f, part: (0, 0), pipeline_mode=pl.Buffered(1))

    specs = [
        SMEM,
        whole((rows, D)),
        pl.BlockSpec((rows, wide), lambda f, part: (0, jnp.minimum(f, 1))),
    ]
    operands += [source[0] for source in sources]
    specs += [whole((length, D)) for length in lengths]
    for grads, first in ((key_grad, 2), (value_grad, 4)):
        for n, length in enumerate(lengths):
            operands.append(grads)
            specs.append(
                pl.BlockSpec(
                    (length, wide),
                    lambda f, part, n=n, first=first: (part[n], jnp.clip(f - first, 0, 1)),
                )
            )
    operands += [weights, *sums]
    specs += [pl.BlockSpec((D, wide), lambda f, part: (at(QUERY) + f // 2, f % 2))]
    specs += [ANY] * targets
    return pl.pallas_call(
        body,
        grid_spec=pltpu.PrefetchScalarGridSpec(
            num_scalar_prefetch=1,
            grid=(6,),
            in_specs=specs,
            out_specs=(whole((rows, D)),) + (ANY,) * targets,
            scratch_shapes=[pltpu.VMEM((D, rows), bf16)]
            + [pltpu.VMEM((D, length), bf16) for length in lengths]
            + [pltpu.VMEM((2, D, wide), bf16), pltpu.SemaphoreType.DMA((2,))],
        ),
        out_shape=(
            jax.ShapeDtypeStruct((rows, D), f32),
            *[jax.ShapeDtypeStruct(target.shape, bf16) for target in sums],
        ),
        input_output_aliases={len(operands) - targets + n: 1 + n for n in range(targets)},
        compiler_params=params(has_side_effects=True),
        cost_estimate=cost(
            (4 * rows + sum(4 * length for length in lengths) + 4 * rows) * D * D, 30 * D * D
        ),
        name="projections_back",
    )(*operands)


def attention_tiles(rows):
    return (512 if rows % 512 == 0 else row_tile(rows)), 256


def key_windows(segments, rank, rows):
    tall, broad = attention_tiles(rows)
    group = segments.shape[0]
    blocks = rows // tall
    own = lax.dynamic_slice_in_dim(segments, rank * rows, rows).reshape(blocks, tall)
    low = jnp.sum(segments[None, :] < own[:, :1], axis=1)
    high = jnp.sum(segments[None, :] <= own[:, -1:], axis=1)
    start = low // 128 * 128
    steps = (high - start + broad - 1) // broad
    start = jnp.minimum(start, group - steps * broad)
    return jnp.stack([start, steps], axis=-1).reshape(-1).astype(jnp.int32)

def attention_forward(queries, keys, segments, rank, windows, slopes):
    rows = queries.shape[0]
    group = keys.shape[0]
    tall, broad = attention_tiles(rows)
    most = group // broad
    own = lax.dynamic_slice_in_dim(segments, rank * rows, rows).reshape(rows, 1)

    def body(rank_ref, window_ref, slope_ref, q_ref, own_ref, key_ref, value_ref, columns_ref, out_ref, total_ref, scores):
        head, block = pl.program_id(0), pl.program_id(1)
        slope = slope_ref[head] * LOG2E
        start = window_ref[2 * block]
        steps = window_ref[2 * block + 1]
        first = rank_ref[0] * rows + block * tall
        query = q_ref[...]
        apart = (
            lax.broadcasted_iota(jnp.int32, (tall, broad), 0)
            - lax.broadcasted_iota(jnp.int32, (tall, broad), 1)
        ).astype(f32)

        def attend(count):
            peak = jnp.full((tall, 128), MASKED, f32)
            for b in range(count):
                begin = pl.multiple_of(start + b * broad, 128)
                here = pl.ds(begin, broad)
                score = dot_right(query, key_ref[here, :]) * (SCORE_SCALE * LOG2E)
                score = score - slope * jnp.abs(apart + (first - begin).astype(f32))
                score = jnp.where(own_ref[...] == columns_ref[:, here], score, MASKED)
                scores[:, b * broad : (b + 1) * broad] = score
                for lane in range(0, broad, 128):
                    peak = jnp.maximum(peak, score[:, lane : lane + 128])
            top = jnp.max(peak, axis=-1, keepdims=True)
            total = jnp.zeros((tall, 128), f32)
            mixed = jnp.zeros((tall, HEAD_DIM), f32)
            for b in range(count):
                here = pl.ds(pl.multiple_of(start + b * broad, 128), broad)
                shifted = jnp.exp2(scores[:, b * broad : (b + 1) * broad] - top)
                for lane in range(0, broad, 128):
                    total = total + shifted[:, lane : lane + 128]
                mixed = mixed + dot(shifted.astype(bf16), value_ref[here, :])
            total = jnp.sum(total, axis=-1, keepdims=True)
            out_ref[...] = (mixed / total).astype(bf16)
            logs = jnp.broadcast_to(top + jnp.log2(total), (tall, 128))
            total_ref[...] = logs.T[0:1, :].reshape(1, 1, tall)

        for count in range(1, most + 1):
            @pl.when(steps == count)
            def _(count=count):
                attend(count)

    return pl.pallas_call(
        body,
        grid=(HEADS, rows // tall),
        out_shape=(
            jax.ShapeDtypeStruct((rows, D), bf16),
            jax.ShapeDtypeStruct((HEADS, 1, rows), f32),
        ),
        in_specs=[
            SMEM, SMEM, SMEM,
            pl.BlockSpec((tall, HEAD_DIM), lambda h, q: (q, h)),
            pl.BlockSpec((tall, 1), lambda h, q: (q, 0)),
            pl.BlockSpec((group, HEAD_DIM), lambda h, q: (0, h)),
            pl.BlockSpec((group, HEAD_DIM), lambda h, q: (0, HEADS + h)),
            const_spec((1, group)),
        ],
        out_specs=(
            pl.BlockSpec((tall, HEAD_DIM), lambda h, q: (q, h)),
            pl.BlockSpec((1, 1, tall), lambda h, q: (h, 0, q)),
        ),
        scratch_shapes=[pltpu.VMEM((tall, group), f32)],
        compiler_params=params(),
        name="attention_forward",
    )(jnp.asarray(rank,jnp.int32).reshape(1), windows, slopes, queries, own, keys, keys, segments.reshape(1, group))

def attention_backward(queries, keys, segments, rank, windows, slopes, logs, grads, attended):
    rows = queries.shape[0]
    group = keys.shape[0]
    tall, broad = attention_tiles(rows)
    most = group // broad
    own = lax.dynamic_slice_in_dim(segments, rank * rows, rows).reshape(1, rows)

    def body(rank_ref, window_ref, slope_ref, q_ref, own_ref, log_ref, grad_ref, att_ref, key_ref, value_ref, columns_ref,
             out_ref, key_out, value_out, key_sum, value_sum):
        head, block = pl.program_id(0), pl.program_id(1)
        slope = slope_ref[head] * LOG2E
        start = window_ref[2 * block]
        steps = window_ref[2 * block + 1]
        first = rank_ref[0] * rows + block * tall

        @pl.when(block == 0)
        def _():
            key_sum[...] = jnp.zeros(key_sum.shape, f32)
            value_sum[...] = jnp.zeros(value_sum.shape, f32)

        query = q_ref[...]
        grad = grad_ref[...]
        products = grad.astype(f32) * att_ref[...].astype(f32)
        delta = jnp.broadcast_to(jnp.sum(products, axis=-1, keepdims=True), (tall, 128)).T[0:1, :]
        log_row = log_ref[0]
        apart = (
            lax.broadcasted_iota(jnp.int32, (broad, tall), 1)
            - lax.broadcasted_iota(jnp.int32, (broad, tall), 0)
        ).astype(f32)

        def attend(count):
            query_sum = jnp.zeros((tall, HEAD_DIM), f32)
            for b in range(count):
                begin = pl.multiple_of(start + b * broad, 128)
                here = pl.ds(begin, broad)
                key = key_ref[here, :]
                score = dot_right(key, query) * (SCORE_SCALE * LOG2E)
                score = score - slope * jnp.abs(apart + (first - begin).astype(f32))
                score = jnp.where(own_ref[...] == columns_ref[here, :], score, MASKED)
                probs = jnp.exp2(score - log_row)
                prob_grad = dot_right(value_ref[here, :], grad)
                value_sum[here, :] += dot(probs.astype(bf16), grad)
                score_grad = (probs * (prob_grad - delta)).astype(bf16)
                key_sum[here, :] += dot(score_grad, query)
                query_sum = query_sum + dot_left(score_grad, key)
            out_ref[...] = (query_sum * SCORE_SCALE).astype(bf16)

        for count in range(1, most + 1):
            @pl.when(steps == count)
            def _(count=count):
                attend(count)

        @pl.when(block == pl.num_programs(1) - 1)
        def _():
            key_out[...] = (key_sum[...] * SCORE_SCALE).astype(bf16)
            value_out[...] = value_sum[...].astype(bf16)

    row_spec = pl.BlockSpec((tall, HEAD_DIM), lambda h, q: (q, h))
    key_spec = pl.BlockSpec((group, HEAD_DIM), lambda h, q: (0, h))
    return pl.pallas_call(
        body,
        grid=(HEADS, rows // tall),
        out_shape=(jax.ShapeDtypeStruct((rows, D), bf16),) + (jax.ShapeDtypeStruct((group, D), bf16),) * 2,
        in_specs=[
            SMEM, SMEM, SMEM,
            pl.BlockSpec((tall, HEAD_DIM), lambda h, q: (q, h)),
            pl.BlockSpec((1, tall), lambda h, q: (0, q)),
            pl.BlockSpec((1, 1, tall), lambda h, q: (h, 0, q)),
            row_spec, row_spec, key_spec,
            pl.BlockSpec((group, HEAD_DIM), lambda h, q: (0, HEADS + h)),
            const_spec((group, 1)),
        ],
        out_specs=(row_spec, key_spec, key_spec),
        scratch_shapes=[pltpu.VMEM((group, HEAD_DIM), f32)] * 2,
        compiler_params=params(),
        name="attention_backward",
    )(jnp.asarray(rank,jnp.int32).reshape(1), windows, slopes, queries, own, logs, grads, attended, keys, keys, segments.reshape(group, 1))


def conv_forward(stream, before, behind, gain, next_gain, weights, taps, masks):
    rows = stream.shape[0]
    tall = rows + 2 * HALO
    tile = row_tile(rows)
    wide = 256
    steps = D // wide

    def body(
        x_ref, before_ref, behind_ref, gain_ref, next_gain_ref, taps_ref, mask_ref, value_ref, gate_ref, out_w_ref,
        out_ref, linear_ref, gate_out_ref, next_ref, normed, glu,
    ):
        step = pl.program_id(0)

        @pl.when(step == 0)
        def _():
            gain_row = gain_ref[...]
            normed[0:HALO] = norm(before_ref[...], gain_row).astype(bf16)
            normed[rows + HALO :] = norm(behind_ref[...], gain_row).astype(bf16)
            for t in range(0, rows, tile):
                x = x_ref[t : t + tile]
                normed[HALO + t : HALO + t + tile] = norm(x, gain_row).astype(bf16)
                out_ref[t : t + tile] = x

        pieces = [(0, HALO)]
        pieces += [(HALO + t, tile) for t in range(0, rows, tile)]
        pieces += [(rows + HALO, HALO)]
        for t, size in pieces:
            here = slice(t, t + size)
            linear = dot(normed[here], value_ref[...])
            gate = dot(normed[here], gate_ref[...])
            linear_ref[here] = linear.astype(bf16)
            gate_out_ref[here] = gate.astype(bf16)
            glu[here] = linear * sigmoid(gate)
        for t in range(0, rows, tile):
            sums = []
            for half in range(0, wide, 128):
                total = jnp.zeros((tile, 128), f32)
                for k in range(KERNEL):
                    moved = glu[HALO + t + k - 2 : HALO + t + k - 2 + tile, half : half + 128]
                    if k != KERNEL // 2:
                        moved = moved * mask_ref[k, HALO + t : HALO + t + tile]
                    total = total + taps_ref[k : k + 1, half : half + 128] * moved
                sums.append(total)
            conved = jnp.concatenate(sums, axis=1)
            act = (conved * sigmoid(conved)).astype(bf16)
            out_ref[t : t + tile] += dot(act, out_w_ref[...])

        @pl.when(step == steps - 1)
        def _():
            for t in range(0, rows, tile):
                next_ref[t : t + tile] = norm(out_ref[t : t + tile], next_gain_ref[...]).astype(bf16)

    return pl.pallas_call(
        body,
        grid=(steps,),
        out_shape=(
            jax.ShapeDtypeStruct((rows, D), f32),
            jax.ShapeDtypeStruct((tall, D), bf16),
            jax.ShapeDtypeStruct((tall, D), bf16),
            jax.ShapeDtypeStruct((rows, D), bf16),
        ),
        in_specs=[
            const_spec((rows, D)),
            const_spec((HALO, D)),
            const_spec((HALO, D)),
            const_spec((1, D)),
            const_spec((1, D)),
            pl.BlockSpec((KERNEL, wide), lambda c: (0, c)),
            const_spec((KERNEL, tall, 128)),
            pl.BlockSpec((D, wide), lambda c: (at(CONV_VALUE), c)),
            pl.BlockSpec((D, wide), lambda c: (at(CONV_GATE), c)),
            pl.BlockSpec((wide, D), lambda c: (at(CONV_OUT) * 4 + c, 0)),
        ],
        out_specs=(
            const_spec((rows, D)),
            pl.BlockSpec((tall, wide), lambda c: (0, c)),
            pl.BlockSpec((tall, wide), lambda c: (0, c)),
            const_spec((rows, D)),
        ),
        scratch_shapes=[pltpu.VMEM((tall, D), bf16), pltpu.VMEM((tall, wide), f32)],
        compiler_params=params(),
        cost_estimate=cost(6 * rows * D * D, 6 * D * D + 12 * rows * D),
        name="conv_forward",
    )(stream, before, behind, gain, next_gain, taps, masks, weights, weights, weights)


def conv_backward(
    grad, before, behind, stream, gain, linear, gate, weights, taps, masks, sums, table, ranks
):
    rows = stream.shape[0]
    tall = rows + 2 * HALO
    tile = row_tile(rows)
    wide = 256
    steps = D // wide
    targets = len(sums)

    def body(
        table_ref, g_ref, before_ref, behind_ref, x_ref, gain_ref, linear_ref, gate_ref, taps_ref,
        mask_ref, value_ref, gate_w_ref, out_w_ref, *refs,
    ):
        out_ref, gain_out_ref, taps_out_ref = refs[targets : targets + 3]
        sums_ref = refs[targets + 3 : 2 * targets + 3]
        (
            low, normed_t, grad_sum, glu, conv_grad, act_t, value_grad, gate_grad, value_part,
            gate_part, out_part, value_sem, gate_sem, out_sem,
        ) = refs[2 * targets + 3 :]
        step = pl.program_id(0)
        slot = lax.rem(step, 2)

        @pl.when(step == 0)
        def _():
            low[0:HALO] = before_ref[...]
            low[rows + HALO :] = behind_ref[...]
            for t in range(0, rows, tile):
                here = slice(t, t + tile)
                low[HALO + t : HALO + t + tile] = g_ref[here].astype(bf16)
                normed_t[:, here] = norm(x_ref[here], gain_ref[...]).astype(bf16).T
                grad_sum[here] = jnp.zeros((tile, D), f32)

        pieces = [(0, HALO)]
        pieces += [(HALO + t, tile) for t in range(0, rows, tile)]
        pieces += [(rows + HALO, HALO)]
        for t, size in pieces:
            here = slice(t, t + size)
            glu[here] = linear_ref[here].astype(f32) * sigmoid(gate_ref[here].astype(f32))

        edge = 8
        pieces = [(HALO - edge, edge)]
        pieces += [(HALO + t, tile) for t in range(0, rows, tile)]
        pieces += [(rows + HALO, edge)]
        tap_sums = [[jnp.zeros((1, 128), f32) for k in range(KERNEL)] for half in range(2)]
        for t, size in pieces:
            totals, moved_rows = [], []
            for half in range(0, wide, 128):
                total = jnp.zeros((size, 128), f32)
                moved_rows.append([])
                for k in range(KERNEL):
                    moved = glu[t + k - 2 : t + k - 2 + size, half : half + 128]
                    if k != KERNEL // 2:
                        moved = moved * mask_ref[k, t : t + size]
                    moved_rows[-1].append(moved)
                    total = total + taps_ref[k : k + 1, half : half + 128] * moved
                totals.append(total)
            conved = jnp.concatenate(totals, axis=1)
            sigma = sigmoid(conved)
            act = conved * sigma
            if size == tile:
                act_t[:, t - HALO : t - HALO + size] = act.astype(bf16).T
                rows_grad = dot_right(low[t : t + size], out_w_ref[...])
            elif t < HALO:
                rows_grad = dot_right(low[0:HALO], out_w_ref[...])[edge:]
            else:
                rows_grad = dot_right(low[rows + HALO :], out_w_ref[...])[:edge]
            center = rows_grad * (sigma + act * (1.0 - sigma))
            conv_grad[t : t + size] = center
            if size == tile:
                for number in range(2):
                    lanes = center[:, number * 128 : (number + 1) * 128]
                    for k in range(KERNEL):
                        tap_sums[number][k] = tap_sums[number][k] + jnp.sum(
                            lanes * moved_rows[number][k], axis=0, keepdims=True
                        )

        for t in range(0, rows, tile):
            values, gates = [], []
            for number, half in enumerate(range(0, wide, 128)):
                lanes = slice(half, half + 128)
                start = HALO + t
                total = jnp.zeros((tile, 128), f32)
                for k in range(KERNEL):
                    moved = conv_grad[start + 2 - k : start + 2 - k + tile, lanes]
                    if k != KERNEL // 2:
                        moved = moved * mask_ref[KERNEL - 1 - k, start : start + tile]
                    total = total + taps_ref[k : k + 1, lanes] * moved
                sigma = sigmoid(gate_ref[start : start + tile, lanes].astype(f32))
                moved_value = total * sigma
                values.append(moved_value.astype(bf16))
                gates.append(
                    (
                        moved_value
                        * linear_ref[start : start + tile, lanes].astype(f32)
                        * (1.0 - sigma)
                    ).astype(bf16)
                )
            value_tile = jnp.concatenate(values, axis=1)
            gate_tile = jnp.concatenate(gates, axis=1)
            here = slice(t, t + tile)
            value_grad[here] = value_tile
            gate_grad[here] = gate_tile
            grad_sum[here] += dot_right(value_tile, value_ref[...]) + dot_right(
                gate_tile, gate_w_ref[...]
            )
        for k in range(KERNEL):
            taps_out_ref[k : k + 1] = jnp.concatenate([tap_sums[0][k], tap_sums[1][k]], axis=1)

        @pl.when(step >= 2)
        def _():
            wait_blocks(value_part.at[slot], value_sem.at[slot])
            wait_blocks(gate_part.at[slot], gate_sem.at[slot])
            wait_blocks(out_part.at[slot], out_sem.at[slot])

        for t in range(0, D, 256):
            value_part[slot, t : t + 256] = dot(normed_t[t : t + 256], value_grad[...]).astype(bf16)
            gate_part[slot, t : t + 256] = dot(normed_t[t : t + 256], gate_grad[...]).astype(bf16)
        out_part[slot] = dot(act_t[...], low[HALO : rows + HALO]).astype(bf16)
        start_blocks(
            table_ref, sums_ref, value_part.at[slot], value_sem.at[slot], CONV_VALUE, 0, step * 2,
            ranks,
        )
        start_blocks(
            table_ref, sums_ref, gate_part.at[slot], gate_sem.at[slot], CONV_GATE, 0, step * 2,
            ranks,
        )
        start_blocks(
            table_ref, sums_ref, out_part.at[slot], out_sem.at[slot], CONV_OUT, step * 2, 0, ranks
        )

        @pl.when(step == steps - 1)
        def _():
            gain_sum = jnp.zeros((1, D), f32)
            for t in range(0, rows, tile):
                here = slice(t, t + tile)
                back, part = norm_back(x_ref[here], gain_ref[...], grad_sum[here])
                gain_sum = gain_sum + part
                out_ref[here] = g_ref[here] + back
            gain_out_ref[...] = gain_sum
            for s in range(2):
                wait_blocks(value_part.at[s], value_sem.at[s])
                wait_blocks(gate_part.at[s], gate_sem.at[s])
                wait_blocks(out_part.at[s], out_sem.at[s])

    operands = [
        table, grad, before, behind, stream, gain, linear, gate, taps, masks, weights, weights,
        weights, *sums,
    ]
    return pl.pallas_call(
        body,
        grid=(steps,),
        out_shape=(
            jax.ShapeDtypeStruct((rows, D), f32),
            jax.ShapeDtypeStruct((1, D), f32),
            jax.ShapeDtypeStruct((KERNEL, D), f32),
            *[jax.ShapeDtypeStruct(target.shape, bf16) for target in sums],
        ),
        in_specs=[
            SMEM,
            const_spec((rows, D)),
            const_spec((HALO, D)),
            const_spec((HALO, D)),
            const_spec((rows, D)),
            const_spec((1, D)),
            pl.BlockSpec((tall, wide), lambda c: (0, c)),
            pl.BlockSpec((tall, wide), lambda c: (0, c)),
            pl.BlockSpec((KERNEL, wide), lambda c: (0, c)),
            const_spec((KERNEL, tall, 128)),
            pl.BlockSpec((D, wide), lambda c: (at(CONV_VALUE), c)),
            pl.BlockSpec((D, wide), lambda c: (at(CONV_GATE), c)),
            pl.BlockSpec((wide, D), lambda c: (at(CONV_OUT) * 4 + c, 0)),
        ]
        + [ANY] * targets,
        out_specs=(
            const_spec((rows, D)),
            const_spec((1, D)),
            pl.BlockSpec((KERNEL, wide), lambda c: (0, c)),
        )
        + (ANY,) * targets,
        scratch_shapes=[
            pltpu.VMEM((tall, D), bf16),
            pltpu.VMEM((D, rows), bf16),
            pltpu.VMEM((rows, D), f32),
            pltpu.VMEM((tall, wide), f32),
            pltpu.VMEM((tall, wide), f32),
            pltpu.VMEM((wide, rows), bf16),
            pltpu.VMEM((rows, wide), bf16),
            pltpu.VMEM((rows, wide), bf16),
            pltpu.VMEM((2, D, wide), bf16),
            pltpu.VMEM((2, D, wide), bf16),
            pltpu.VMEM((2, wide, D), bf16),
            pltpu.SemaphoreType.DMA((2,)),
            pltpu.SemaphoreType.DMA((2,)),
            pltpu.SemaphoreType.DMA((2,)),
        ],
        input_output_aliases={len(operands) - targets + n: 3 + n for n in range(targets)},
        compiler_params=params(has_side_effects=True),
        cost_estimate=cost(12 * rows * D * D, 12 * D * D + 16 * rows * D),
        name="conv_backward",
    )(*operands)


def shampoo(grads, arrivals, left_stats, right_stats, left_root, right_root, master, average):
    slots = master.shape[0]
    each = 8
    steps = (slots + each - 1) // each
    arrivals = jnp.pad(arrivals, (0, steps * each - slots))
    old_bias = 1.0 - DECAY_AVERAGE ** (STEP - 1)
    new_bias = 1.0 - DECAY_AVERAGE**STEP

    def body(index_ref, *refs):
        g_refs = refs[:each]
        ls_ref, rs_ref, lr_ref, rr_ref, m_ref, a_ref, go, lo, ro, mo, ao = refs[each:]
        for n in range(each):
            grad = g_refs[n][0]
            go[n] = grad.astype(f32)
            lo[n] = DECAY_STAT * ls_ref[n] + (1.0 - DECAY_STAT) * dot_right(grad, grad)
            ro[n] = DECAY_STAT * rs_ref[n] + (1.0 - DECAY_STAT) * dot_left(grad, grad)
            inner = dot(grad, rr_ref[n].astype(bf16))
            turned = dot(lr_ref[n].astype(bf16), inner.astype(bf16))
            mean_sq = jnp.mean(turned * turned, axis=(0, 1), keepdims=True)
            new = m_ref[n] - RATE_BLOCK * turned * lax.rsqrt(mean_sq + 1e-06)
            mo[n] = new
            ao[n] = (DECAY_AVERAGE * old_bias / new_bias) * a_ref[n] + (
                (1.0 - DECAY_AVERAGE) / new_bias
            ) * new

    spec = pl.BlockSpec((each, BLOCK, BLOCK), lambda s, index: (s, 0, 0))
    grad_specs = [
        pl.BlockSpec((1, BLOCK, BLOCK), lambda s, index, n=n: (index[s * each + n], 0, 0))
        for n in range(each)
    ]
    shape = jax.ShapeDtypeStruct((slots, BLOCK, BLOCK), f32)
    return pl.pallas_call(
        body,
        grid_spec=pltpu.PrefetchScalarGridSpec(
            num_scalar_prefetch=1,
            grid=(steps,),
            in_specs=grad_specs + [spec] * 6,
            out_specs=(spec,) * 5,
        ),
        out_shape=(shape,) * 5,
        compiler_params=params(),
        name="shampoo",
    )(arrivals, *[grads] * each, left_stats, right_stats, left_root, right_root, master, average)


def vector_step(values, grads):
    mean_sq = jnp.mean(grads * grads, axis=-1, keepdims=True)
    return values - RATE_VECTOR * grads * lax.rsqrt(mean_sq + 1e-06)


def round_places(number):
    place = 0
    for other, count in enumerate(ROUNDS):
        if other == number:
            break
        place = place + (32 if other == LARGE else 64) * count
    if number == LARGE:
        return place, 64 * sum(ROUNDS) - 32 * ROUNDS[LARGE]
    return place, place + 32 * ROUNDS[number]


def scatter_tables(owners_all, coords, slot_dev, blocks):
    own_rank, own_x, own_core = coords
    ranks = owners_all.shape[0]
    both = 2 * slot_dev
    chips = owners_all // both
    same = chips[:, :, None] == chips[:, None, :]
    later = jnp.arange(blocks)[None, :] > jnp.arange(blocks)[:, None]
    order = jnp.sum((same & later[None]).astype(jnp.int32), axis=-1)
    dx = (chips % 2) ^ own_x
    z_at = chips // 2
    dy = jnp.arange(ranks)[:, None] ^ own_rank
    position = jnp.zeros_like(owners_all)
    arrival = jnp.zeros_like(owners_all)
    starts, unused = offsets(ranks)
    good = jnp.array(True)
    done = 0
    for number, count in enumerate(ROUNDS):
        inside = order - 4 * done
        core = inside // (2 * count)
        kind = inside // count % 2
        slot = inside % count
        outer = jnp.where(kind == 0, dx, dy)
        inner = jnp.where(kind == 0, dy, dx)
        dc = core ^ own_core
        here = ((kind * 2 + outer) * 2 + inner) * 4 + z_at
        first, second = round_places(number)
        here = jnp.where(dc == 0, first, second) + here * count + slot
        valid = (inside >= 0) & (inside < 4 * count)
        position = jnp.where(valid, here, position)
        arrival = jnp.where(valid, dc * slot_dev + 2 * done + inside % (2 * count), arrival)
        done = done + count
        if number < len(EARLY):
            there = jnp.arange(blocks) >= starts[EARLY[number]]
            good = good & jnp.all((order >= 4 * done) | there[None])
    device = (lax.axis_index("z") * 2 + own_x) * 2 + own_core
    mine = lax.dynamic_index_in_dim(owners_all, own_rank, 0, keepdims=False)
    arrival = lax.dynamic_index_in_dim(arrival, own_rank, 0, keepdims=False)
    match = mine[None, :] == (device * slot_dev + jnp.arange(slot_dev))[:, None]
    index = jnp.sum(jnp.where(match, arrival[None, :], 0), axis=-1)
    return position.reshape(-1).astype(jnp.int32), index.astype(jnp.int32), good


def added(terms):
    return sum(term.astype(f32) for term in terms).astype(bf16)


def one_round(rounds, send, number):
    count = ROUNDS[number]
    offset = round_places(number)[0]
    (come,) = yield [(send, "core")]
    half, quarter = 16 * count, 8 * count

    def part(kind, first, length):
        start = offset + kind * half + first
        here = kind * half + first
        return [rounds.sums[start : start + length], come[here : here + length]]

    got = yield [
        (added(part(0, quarter, quarter)), "x"),
        (added(part(1, quarter, quarter)), "mp"),
    ]
    eighth = quarter // 2
    late = yield [
        (added(part(0, eighth, eighth) + [got[0][eighth:]]), "mp"),
        (added(part(1, eighth, eighth) + [got[1][eighth:]]), "x"),
    ]
    columns = [
        added(part(kind, 0, eighth) + [got[kind][:eighth], late[kind]])
        .reshape(4, count, BLOCK, BLOCK)
        for kind in range(2)
    ]
    column = jnp.concatenate(columns, axis=1)
    if number < len(ROUNDS) - 1:
        return column
    z_at = lax.axis_index("z")

    def for_z(step):
        return lax.dynamic_index_in_dim(column, jnp.clip(z_at + step, 0, 3), 0, keepdims=False)

    got = yield [(for_z(step), step) for step in (2, -2, 1, -1, 3, -3)]
    return added([for_z(0), *got])


def total_steps(values):
    for group in (("core", "x", "both"), ("mp", "near", "across"), ("far",)):
        got = yield [(values, move) for move in group]
        values = values + got[0]
        if len(got) > 1:
            values = values + (got[1] + got[2])
    return values


class Rounds:
    def __init__(self, sums, tail):
        self.running, self.waiting, self.results = {}, {}, {}
        self.sums, self.tail = sums, tail

    def add(self, name, steps):
        self.running[name] = steps
        self.waiting[name] = next(steps)

    def add_round(self, number):
        size = 32 * ROUNDS[number]
        offset = round_places(number)[1]
        send = self.tail if number == LARGE else self.sums[offset : offset + size]
        self.add(number, one_round(self, send, number))

    def beside(self, *held):
        names = list(self.waiting)
        values = [value for name in names for value, unused in self.waiting[name]]
        out = list(tied(*values, *held))
        for name in names:
            self.waiting[name] = [(out.pop(0), move) for unused, move in self.waiting[name]]
        return out

    def hold(self):
        moves = [[move for unused, move in pairs] for pairs in self.waiting.values()]
        values = [value for pairs in self.waiting.values() for value, unused in pairs]
        columns = [(name, value) for name, value in self.results.items() if isinstance(name, int)]
        out = list(tied(self.sums, *values, *[value for unused, value in columns]))
        self.sums = out.pop(0)
        for name, names in zip(self.waiting, moves):
            self.waiting[name] = [(out.pop(0), move) for move in names]
        for (name, unused), value in zip(columns, out):
            self.results[name] = value
        return self.sums, self.tail

    def step(self, names, *held, sums=None):
        names = [name for name in names if name in self.waiting]
        transfers = [pair for name in names for pair in self.waiting[name]]
        if sums is not None:
            got, held = together(transfers, *sums, *held)
            (self.sums, self.tail), held = held[:2], held[2:]
        else:
            got, held = together(transfers, *held)
        for name in names:
            count = len(self.waiting[name])
            mine, got = got[:count], got[count:]
            try:
                self.waiting[name] = self.running[name].send(mine)
            except StopIteration as end:
                self.results[name] = end.value
                del self.waiting[name]
        return held


def both_swaps(value, moves):
    arrived = []
    for move in moves:
        (value,) = yield [(value, move)]
        arrived.append(value)
    return arrived


def joined(columns):
    return jnp.concatenate(columns, axis=1).reshape(-1, BLOCK, BLOCK)


def over_z(column):
    return lax.psum_scatter(column, "z", scatter_dimension=0, tiled=True)


def finish_rounds(rounds):
    rounds.add_round(3)
    rounds.step([2, 3])
    rounds.add_round(4)
    (column,) = rounds.beside(joined([rounds.results[number] for number in range(3)]))
    early = over_z(column)
    rounds.step([3, 4, "small"])
    rounds.step([3, "small"])
    (column,) = rounds.beside(joined([rounds.results[3]]))
    late = over_z(column)
    rounds.step([4, "small"])
    rounds.step([4])
    rounds.step([4])
    mine = jnp.concatenate([early, late, rounds.results[4]], axis=0)
    return jnp.concatenate([mine, swap(mine, "core")], axis=0)


def all_rounds(sums, tail):
    rounds = Rounds(sums, tail)
    for number in range(3):
        rounds.add_round(number)
    rounds.step([0, 1, 2])
    rounds.step([0, 1, 2])
    rounds.step([0, 1])
    return finish_rounds(rounds)


def edges(first_rows, last_rows, ranks):
    before = lax.ppermute(last_rows, "mp", [(r, r + 1) for r in range(ranks - 1)])
    behind = lax.ppermute(first_rows, "mp", [(r + 1, r) for r in range(ranks - 1)])
    return before, behind


def local(fast):
    def run(
        stream, cotangent, segments, owners, master, average, left_stats, right_stats, left_root,
        right_root, gains, kernel,
    ):
        ranks = lax.axis_size("mp")
        rank = lax.axis_index("mp")
        coords = (rank, lax.axis_index("x"), lax.axis_index("core"))
        rows = stream.shape[0]
        slot_dev = master.shape[1]
        chips = lax.axis_size("z") * lax.axis_size("x") * 2
        slots = slot_dev * chips
        segment_ids = segments[0]
        group = segment_ids.shape[0]
        unused, blocks = offsets(ranks)

        if fast:
            pair = jnp.concatenate([owners, swap(owners, "mp")])
            owners_all = jnp.where(rank == 0, pair, pair[::-1])
        else:
            owners_all = lax.all_gather(owners, "mp", axis=0, tiled=True)
        places = jnp.asarray(weight_places(ranks))
        if fast:
            table, arrivals, good = scatter_tables(owners_all, coords, slot_dev, blocks)
        else:
            table = (owners_all + jnp.arange(ranks)[:, None] * slots).reshape(-1)
            arrivals = jnp.arange(slot_dev, dtype=jnp.int32)

        slopes = 2.0 ** (-8.0 * (jnp.arange(HEADS).astype(f32) + 1.0) / HEADS)
        padded = jnp.pad(segment_ids, (HALO, HALO), constant_values=-1)
        wide_ids = jnp.pad(padded, (2, 2), constant_values=-2)
        tall = rows + 2 * HALO
        here = lax.dynamic_slice_in_dim(padded, rank * rows, tall)
        masks = jnp.stack(
            [
                (lax.dynamic_slice_in_dim(wide_ids, rank * rows + k, tall) == here).astype(f32)
                for k in range(KERNEL)
            ]
        )
        masks = jnp.broadcast_to(masks[:, :, None], (KERNEL, tall, 128))
        windows = key_windows(segment_ids, rank, rows)

        def gain(n):
            return gains[n : n + 1]

        starts = [offsets(ranks)[0][first] for first, unused in GROUPS] + [blocks]
        low = master[0].astype(bf16)
        if fast:
            across = 1 - rank
            dp = ("z", "x", "core")
            normed_own = norm_rows(stream, gain(0))
            low_other, normed_other = swap(low, "mp"), swap(normed_own, "mp")
            column = lax.all_gather(low, dp, axis=0, tiled=True)
            column, normed_other, table, arrivals, good, windows, masks = tied(
                column, normed_other, table, arrivals, good, windows, masks
            )
            low_other, column = tied(low_other, column)
            column_other = lax.all_gather(low_other, dp, axis=0, tiled=True)

            def of_index(slots, index, number, into=None):
                here = slice(starts[number], starts[number + 1])
                return unsort(
                    slots, owners_all[index, here], places[index, here], GROUP_CHUNKS[number], into
                )

            w_one = of_index(column, rank, 0)
            (product,) = ffn_part(normed_other, w_one, UP1, DOWN1, 2 * rank, 2, False)
            own_product, pre_first = ffn_part(normed_own, w_one, UP1, DOWN1, 2 * rank, 2, True)
            w_attn, w_conv, w_two = [of_index(column, rank, number) for number in (1, 2, 3)]
            (product,), (own_product, w_attn, w_conv, w_two) = together(
                [(product, "mp")], own_product, w_attn, w_conv, w_two
            )
            after_first, normed_attn = join(stream, [own_product, product], gain(1))
            (other,), unused = together([(normed_attn, "mp")])
            column_other, other = tied(column_other, other)

            w_attn = of_index(column_other, across, 1, w_attn)
            queries = project(normed_attn, w_attn, QUERY, 1)
            keys = project(normed_attn, w_attn, KEY, 2, rank, 2)
            keys = project(other, w_attn, KEY, 2, across, 2, keys)
            attended, logs = attention_forward(
                queries, keys, segment_ids, rank, windows, slopes
            )
            after_attn = project_out(attended, w_attn, OUT, after_first)
            w_conv = of_index(column_other, across, 2, w_conv)
            w_two = of_index(column_other, across, 3, w_two)
            w_one = of_index(column_other, across, 0, tied(w_one, own_product)[0])
            before, behind = edges(after_attn[:HALO], after_attn[-HALO:], ranks)
            after_conv, linear, gate, normed_two = conv_forward(
                after_attn, before, behind, gain(2), gain(3), w_conv, kernel, masks
            )
            product, pre_second = ffn_part(
                normed_two, w_two, UP2, DOWN2, jnp.zeros((), jnp.int32), 4, True
            )
            after_second, output = join(after_conv, [product], gain(4))
            sources = [(normed_attn, rank), (other, across)]
        else:
            everything = lax.all_gather(low, ("mp", "z", "x", "core"), axis=0, tiled=True)
            slot_of = owners_all + jnp.arange(ranks)[:, None] * slots
            arrays = []
            for number, chunks in enumerate(GROUP_CHUNKS):
                here = slice(starts[number], starts[number + 1])
                array = unsort(
                    everything, slot_of[:, here].reshape(-1).astype(jnp.int32),
                    places[:, here].reshape(-1), chunks,
                )
                arrays.append(array)
            w_one, w_attn, w_conv, w_two = arrays
            after_first, pre_first, normed_attn = ffn_forward(
                stream, gain(0), gain(1), w_one, UP1, DOWN1
            )
            other = lax.all_gather(normed_attn, "mp", axis=0, tiled=True)
            queries = project(normed_attn, w_attn, QUERY, 1)
            keys = project(other, w_attn, KEY, 2)
            sources = [(other, 0)]
            attended, logs = attention_forward(
                queries, keys, segment_ids, rank, windows, slopes
            )
            after_attn = project_out(attended, w_attn, OUT, after_first)
            before, behind = edges(after_attn[:HALO], after_attn[-HALO:], ranks)
            after_conv, linear, gate, normed_two = conv_forward(
                after_attn, before, behind, gain(2), gain(3), w_conv, kernel, masks
            )
            after_second, pre_second, output = ffn_forward(
                after_conv, gain(3), gain(4), w_two, UP2, DOWN2
            )

        if fast:
            last = 32 * ROUNDS[LARGE]
            sums = ((ranks * slots - last, BLOCK, BLOCK), (last, BLOCK, BLOCK))
        else:
            sums = ((ranks * slots, BLOCK, BLOCK),)
            if slots > blocks:
                sums = (jnp.zeros(sums[0], bf16),)
        grad_conv, gains_a, *sums = ffn_backward(
            after_second, gain(4), [cotangent], None, after_conv, gain(3), pre_second, w_two,
            UP2, DOWN2, sums, table, ranks,
        )
        if fast:
            rounds = Rounds(*sums)
            rounds.add_round(0)
            sums = rounds.hold()
        before, behind = edges(
            grad_conv[:HALO].astype(bf16), grad_conv[-HALO:].astype(bf16), ranks
        )
        grad_attn, gains_b, tap_grads, *sums = conv_backward(
            grad_conv, before, behind, after_attn, gain(2), linear, gate, w_conv, kernel, masks,
            sums, table, ranks,
        )
        if fast:
            grad_attn, gains_b, tap_grads = rounds.step(
                [0], grad_attn, gains_b, tap_grads, sums=sums
            )
            rounds.add_round(1)
            sums = rounds.hold()
        mixed_grad, *sums = project_out_back(
            grad_attn, w_attn, OUT, attended, sums, table, ranks
        )
        query_grad, key_grad, value_grad = attention_backward(
            queries, keys, segment_ids, rank, windows, slopes, logs, mixed_grad, attended
        )
        if fast:
            away = input_gradient(key_grad, value_grad, w_attn, 1 - rank, rows)
            query_grad, key_grad, value_grad, away = rounds.step(
                [0, 1], query_grad, key_grad, value_grad, away, sums=sums
            )
            sums = rounds.hold()
        else:
            away = input_gradient(key_grad, value_grad, w_attn, jnp.zeros((), jnp.int32), group)
            arrived = lax.psum_scatter(away, "mp", scatter_dimension=0, tiled=True)
        near, *sums = projections_back(
            normed_attn, query_grad, key_grad, value_grad, sources, fast, w_attn, sums, table, ranks
        )
        if fast:
            rounds.add("away", both_swaps(away, ["mp"]))
            (near,) = rounds.step(["away"], near, sums=sums)
            (arrived,) = rounds.results.pop("away")
            rounds.add_round(2)
            sums = rounds.hold()
        first_args = (gain(0), pre_first, w_one, UP1, DOWN1)
        if fast:
            middle = FF // 512 // 2
            so_far, gains_c, *sums, carry = ffn_backward(
                after_first, gain(1), [near, arrived], grad_attn, stream, *first_args, sums, table,
                ranks, rank, 0, middle,
            )
            so_far, gains_c, carry = rounds.step([0, 1, 2], so_far, gains_c, carry, sums=sums)
            sums = rounds.hold()
            stream_grad, gains_d, *sums = ffn_backward(
                None, None, [], so_far, stream, *first_args, sums, table, ranks, rank, middle,
                carry=carry,
            )
            stream_grad, gains_d = rounds.step([1, 2], stream_grad, gains_d, sums=sums)
            gains_c = jnp.concatenate([gains_c[0:1], gains_d[1:2]])
        else:
            stream_grad, gains_c, *sums = ffn_backward(
                after_first, gain(1), [near, arrived], grad_attn, stream, *first_args, sums, table,
                ranks,
            )
        small = jnp.concatenate(
            [gains_c[1:2], gains_c[0:1], gains_b, gains_a[1:2], gains_a[0:1], tap_grads]
        )
        everywhere = ("mp", "z", "x", "core")
        if fast:
            rounds.add("small", total_steps(small))
            sums = (rounds.sums, rounds.tail)
            own_grads = finish_rounds(rounds)
            small = rounds.results["small"]
            own_grads = lax.cond(
                good,
                lambda sums, tail, own: own,
                lambda sums, tail, own: all_rounds(sums, tail),
                *sums,
                own_grads,
            )
        else:
            own_grads = lax.psum_scatter(sums[0], everywhere, scatter_dimension=0, tiled=True)
            small = lax.psum(small, everywhere)
        gain_grads, kernel_grads = small[:5], small[5:]
        block_grads, left_new, right_new, master_new, average_new = shampoo(
            own_grads, arrivals, left_stats[0], right_stats[0], left_root[0], right_root[0], master[0],
            average[0],
        )
        return (
            output,
            stream_grad,
            block_grads[None],
            left_new[None],
            right_new[None],
            master_new[None],
            average_new[None],
            gain_grads,
            vector_step(gains, gain_grads),
            kernel_grads,
            vector_step(kernel, kernel_grads),
        )

    return run


def solution(mesh):
    ranks, pieces = mesh.shape["mp"], mesh.shape["dp"]
    fast = ranks == 2 and pieces == 16
    xs = 2 if fast else 1
    grid = Mesh(
        np.asarray(mesh.devices).reshape(ranks, pieces // (2 * xs), xs, 2), ("mp", "z", "x", "core")
    )
    dp = ("z", "x", "core")
    rows = P((*dp, "mp"), None)
    slots = P("mp", dp, None, None)
    return jax.shard_map(
        local(fast),
        mesh=grid,
        in_specs=(
            rows, rows, P(dp, None), P("mp", None), slots, slots, slots, slots, slots, slots, P(),
            P(),
        ),
        out_specs=(rows, rows, slots, slots, slots, slots, slots, P(), P(), P(), P()),
        check_vma=False,
    )
```

```python
import math

import jax
import jax.numpy as jnp
import numpy as np
from jax import lax
from jax.experimental import pallas as pl
from jax.experimental.pallas import tpu as pltpu
from jax.sharding import Mesh
from jax.sharding import PartitionSpec as P

D = 1024
FF = 4096
HEADS = 8
HEAD_DIM = 128
KERNEL = 5
STEP = 4
BLOCK = 128
HALO = 16
WIDE = 8

EPSILON = 1e-05
DECAY_STAT = 0.95
RATE_BLOCK = 0.02
RATE_VECTOR = 0.2
DECAY_AVERAGE = 0.9999
MASKED = -1e30
LOG2E = math.log2(math.e)
SCORE_SCALE = 1.0 / math.sqrt(HEAD_DIM)

f32 = jnp.float32
bf16 = jnp.bfloat16
ANY = pl.BlockSpec(memory_space=pl.ANY)
SMEM = pl.BlockSpec(memory_space=pltpu.SMEM)

MATRICES = [
    (0, 0, D, FF, True),
    (0, 4, FF, D, False),
    (1, 0, D, D, True),
    (1, 1, D, D, True),
    (1, 2, D, D, True),
    (1, 3, D, D, False),
    (2, 0, D, D, True),
    (2, 1, D, D, True),
    (2, 2, D, D, False),
    (3, 0, D, FF, True),
    (3, 4, FF, D, False),
]
UP1, DOWN1, QUERY, KEY, VALUE, OUT, CONV_VALUE, CONV_GATE, CONV_OUT, UP2, DOWN2 = range(11)
GROUPS = [(0, 2), (2, 6), (6, 9), (9, 11)]
GROUP_CHUNKS = [8, 4, 3, 8]


def at(matrix):
    return MATRICES[matrix][1]


ROUNDS = [4, 3, 4, 9, 3]
LARGE = 3
EARLY = [9, 6, 2]


def params(**kw):
    return pltpu.CompilerParams(vmem_limit_bytes=58 * 2**20, **kw)


def const_spec(shape):
    return pl.BlockSpec(shape, lambda *ids: (0,) * len(shape), pipeline_mode=pl.Buffered(1))


def row_tile(rows):
    return 256 if rows % 256 == 0 else 128


def cost(flops, moved):
    return pl.CostEstimate(flops=int(flops), bytes_accessed=int(moved), transcendentals=0)


def offsets(ranks):
    out = []
    offset = 0
    for unused, unused_chunk, height, breadth, by_columns in MATRICES:
        out.append(offset)
        offset = offset + height * breadth // (BLOCK * BLOCK * ranks)
    return out, offset


def block_number(matrix, row_block, column_block, ranks):
    starts, total = offsets(ranks)
    unused, unused_chunk, height, breadth, by_columns = MATRICES[matrix]
    if by_columns:
        part = breadth // BLOCK // ranks
        return (
            (column_block // part) * total + starts[matrix] + row_block * part + column_block % part
        )
    part = height // BLOCK // ranks
    breadth_blocks = breadth // BLOCK
    return (
        (row_block // part) * total
        + starts[matrix]
        + (row_block % part) * breadth_blocks
        + column_block
    )


def weight_places(ranks):
    unused, total = offsets(ranks)
    places = np.zeros((ranks * total,), np.int32)
    for matrix, (unused, chunk, height, breadth, by_columns) in enumerate(MATRICES):
        for row in range(height // BLOCK):
            for column in range(breadth // BLOCK):
                place = ((chunk + column // WIDE) * 8 + row) * WIDE + column % WIDE
                places[block_number(matrix, row, column, ranks)] = place
    return places.reshape(ranks, total)


def copy_in_place(out, source, place, sem):
    row = pl.multiple_of((place // WIDE) * BLOCK, BLOCK)
    column = pl.multiple_of((place % WIDE) * BLOCK, BLOCK)
    pltpu.make_async_copy(
        source, out.at[pl.ds(row, BLOCK), pl.ds(column, BLOCK)], sem
    ).start()


def unsort(slots, sources, places, chunks, into=None):
    count = sources.shape[0]
    each = max(n for n in range(1, 65) if count % n == 0)
    steps = count // each

    def body(source_ref, place_ref, slots_ref, *rest):
        out, held, read_sem, write_sem = rest[-4:]
        step = pl.program_id(0)
        slot = lax.rem(step, 2)

        def read(number, into):
            def one(n, unused):
                pltpu.make_async_copy(
                    slots_ref.at[source_ref[number * each + n]], held.at[into, n], read_sem.at[into]
                ).start()
                return unused

            lax.fori_loop(0, each, one, 0)

        def written(number, into):
            pltpu.make_async_copy(held.at[into], held.at[into], write_sem.at[into]).wait()

        @pl.when(step == 0)
        def _():
            read(0, 0)

        @pl.when(step >= 1)
        def _():
            written(step - 1, 1 - slot)

        @pl.when(step + 1 < steps)
        def _():
            read(step + 1, 1 - slot)

        pltpu.make_async_copy(held.at[slot], held.at[slot], read_sem.at[slot]).wait()

        def one(n, unused):
            copy_in_place(out, held.at[slot, n], place_ref[step * each + n], write_sem.at[slot])
            return unused

        lax.fori_loop(0, each, one, 0)

        @pl.when(step == steps - 1)
        def _():
            written(step, slot)

    operands = [sources, places, slots]
    if into is not None:
        operands.append(into)
    return pl.pallas_call(
        body,
        grid=(steps,),
        out_shape=jax.ShapeDtypeStruct((chunks * D, D), bf16),
        in_specs=[SMEM, SMEM] + [ANY] * (len(operands) - 2),
        out_specs=ANY,
        scratch_shapes=[
            pltpu.VMEM((2, each, BLOCK, BLOCK), bf16),
            pltpu.SemaphoreType.DMA((2,)),
            pltpu.SemaphoreType.DMA((2,)),
        ],
        input_output_aliases={} if into is None else {3: 0},
        compiler_params=params(has_side_effects=True),
        cost_estimate=cost(0, 2 * count * BLOCK * BLOCK * 2),
        name="unsort",
    )(*operands)


PAIR = [(0, 1), (1, 0)]
MOVES = {
    "x": ("x", PAIR),
    "mp": ("mp", PAIR),
    "core": ("core", PAIR),
    "near": ("z", [(0, 1), (1, 0), (2, 3), (3, 2)]),
    "far": ("z", [(0, 2), (2, 0), (1, 3), (3, 1)]),
    "both": (("x", "core"), [(n, 3 - n) for n in range(4)]),
    "across": (("mp", "z"), [(n, (n // 4 * 4) ^ 4 | (n % 4) ^ 1) for n in range(8)]),
}
for _step in (-3, -2, -1, 1, 2, 3):
    MOVES[_step] = ("z", [(z, z + _step) for z in range(4) if 0 <= z + _step < 4])


def swap(value, move):
    axis, pairs = MOVES[move]
    return lax.ppermute(value, axis, pairs)


def tied(*values):
    return lax.optimization_barrier(values)


def together(transfers, *held):
    values = tied(*[value for value, unused in transfers])
    arrived = [swap(value, move) for value, (unused, move) in zip(values, transfers)]
    out = tied(*arrived, *held)
    return list(out[: len(arrived)]), out[len(arrived) :]


def sigmoid(values):
    return 0.5 * jnp.tanh(0.5 * values) + 0.5


def norm_parts(values):
    center = values - jnp.mean(values, axis=-1, keepdims=True)
    spread = jnp.mean(center * center, axis=-1, keepdims=True)
    scale = lax.rsqrt(spread + EPSILON)
    return center * scale, scale


def norm(values, gain):
    return norm_parts(values)[0] * gain


def norm_back(values, gain, grad):
    hat, scale = norm_parts(values)
    inner = grad * gain
    mean_inner = jnp.mean(inner, axis=-1, keepdims=True)
    mean_hat = jnp.mean(inner * hat, axis=-1, keepdims=True)
    return (
        scale * (inner - mean_inner - hat * mean_hat),
        jnp.sum(grad * hat, axis=0, keepdims=True),
    )


def dot(a, b):
    return jnp.dot(a, b, preferred_element_type=f32)


def dot_right(a, b):
    return lax.dot_general(a, b, (((1,), (1,)), ((), ())), preferred_element_type=f32)


def dot_left(a, b):
    return lax.dot_general(a, b, (((0,), (0,)), ((), ())), preferred_element_type=f32)


def start_blocks(table, targets, source, sem, matrix, row_block, column_block, ranks):
    height, breadth = source.shape
    for i in range(height // BLOCK):
        for j in range(breadth // BLOCK):
            place = table[block_number(matrix, row_block + i, column_block + j, ranks)]
            block = source.at[pl.ds(i * BLOCK, BLOCK), pl.ds(j * BLOCK, BLOCK)]
            if len(targets) == 1:
                pltpu.make_async_copy(block, targets[0].at[place], sem).start()
                continue
            limit = targets[0].shape[0]

            @pl.when(place < limit)
            def _(place=place, block=block):
                pltpu.make_async_copy(block, targets[0].at[place], sem).start()

            @pl.when(place >= limit)
            def _(place=place, block=block):
                pltpu.make_async_copy(block, targets[1].at[place - limit], sem).start()


def wait_blocks(source, sem):
    pltpu.make_async_copy(source, source, sem).wait()


def ffn_forward(stream, gain, next_gain, weights, upper, lower):
    rows = stream.shape[0]
    tile = row_tile(rows)
    wide = D
    steps = FF // wide

    def body(x_ref, gain_ref, next_gain_ref, up_ref, down_ref, out_ref, pre_ref, next_ref, normed):
        step = pl.program_id(0)

        @pl.when(step == 0)
        def _():
            for t in range(0, rows, tile):
                x = x_ref[t : t + tile].astype(f32)
                normed[t : t + tile] = norm(x, gain_ref[...]).astype(bf16)
                out_ref[t : t + tile] = jnp.zeros((tile, D), f32)

        for t in range(0, rows, tile):
            pre = dot(normed[t : t + tile], up_ref[...])
            pre_ref[t : t + tile] = pre.astype(bf16)
            act = (pre * sigmoid(pre)).astype(bf16)
            out_ref[t : t + tile] += dot(act, down_ref[...])

        @pl.when(step == steps - 1)
        def _():
            for t in range(0, rows, tile):
                y = x_ref[t : t + tile].astype(f32) + 0.5 * out_ref[t : t + tile]
                out_ref[t : t + tile] = y
                next_ref[t : t + tile] = norm(y, next_gain_ref[...]).astype(bf16)

    return pl.pallas_call(
        body,
        grid=(steps,),
        out_shape=(
            jax.ShapeDtypeStruct((rows, D), f32),
            jax.ShapeDtypeStruct((rows, FF), bf16),
            jax.ShapeDtypeStruct((rows, D), bf16),
        ),
        in_specs=[
            const_spec((rows, D)),
            const_spec((1, D)),
            const_spec((1, D)),
            pl.BlockSpec((D, wide), lambda f: (at(upper) + f, 0)),
            pl.BlockSpec((wide, D), lambda f: (at(lower) + f, 0)),
        ],
        out_specs=(
            const_spec((rows, D)),
            pl.BlockSpec((rows, wide), lambda f: (0, f)),
            const_spec((rows, D)),
        ),
        scratch_shapes=[pltpu.VMEM((rows, D), bf16)],
        compiler_params=params(),
        cost_estimate=cost(4 * rows * D * FF, 4 * D * FF + 2 * rows * FF),
        name="ffn_forward",
    )(stream, gain, next_gain, weights, weights)


def norm_rows(values, gain):
    rows = values.shape[0]
    tile = row_tile(rows)

    def body(x_ref, gain_ref, out_ref):
        out_ref[...] = norm(x_ref[...].astype(f32), gain_ref[...]).astype(bf16)

    spec = pl.BlockSpec((tile, D), lambda t: (t, 0))
    return pl.pallas_call(
        body,
        grid=(rows // tile,),
        out_shape=jax.ShapeDtypeStruct((rows, D), bf16),
        in_specs=[spec, const_spec((1, D))],
        out_specs=spec,
        compiler_params=params(),
        name="norm_rows",
    )(values, gain)


def ffn_part(normed, weights, upper, lower, first, steps, keep, pre=None):
    rows = normed.shape[0]
    tile = row_tile(rows)

    def body(part_ref, x_ref, up_ref, down_ref, *rest):
        out_ref = rest[-3] if keep else rest[-2]
        pre_ref = rest[-2]
        total = rest[-1]
        step = pl.program_id(0)
        for t in range(0, rows, tile):
            here = slice(t, t + tile)
            value = dot(x_ref[here], up_ref[...])
            if keep:
                pre_ref[here] = value.astype(bf16)
            act = (value * sigmoid(value)).astype(bf16)
            new = dot(act, down_ref[...])

            if steps == 1:
                out_ref[here] = new.astype(bf16)
                continue

            @pl.when(step == 0)
            def _(new=new, here=here):
                total[here] = new

            @pl.when((step > 0) & (step < steps - 1))
            def _(new=new, here=here):
                total[here] += new

            @pl.when(step == steps - 1)
            def _(new=new, here=here):
                out_ref[here] = (total[here] + new).astype(bf16)

    operands = [first.reshape(1), normed, weights, weights]
    specs = [
        pl.BlockSpec((rows, D), lambda f, p: (0, 0), pipeline_mode=pl.Buffered(1)),
        pl.BlockSpec((D, D), lambda f, p: (at(upper) + p[0] + f, 0)),
        pl.BlockSpec((D, D), lambda f, p: (at(lower) + p[0] + f, 0)),
    ]
    shapes = [jax.ShapeDtypeStruct((rows, D), bf16)]
    out_specs = [pl.BlockSpec((rows, D), lambda f, p: (0, 0), pipeline_mode=pl.Buffered(1))]
    aliases = {}
    if keep:
        shapes.append(jax.ShapeDtypeStruct((rows, FF), bf16))
        out_specs.append(pl.BlockSpec((rows, D), lambda f, p: (0, p[0] + f)))
        if pre is not None:
            aliases = {len(operands): 1}
            operands.append(pre)
            specs.append(ANY)
    return pl.pallas_call(
        body,
        grid_spec=pltpu.PrefetchScalarGridSpec(
            num_scalar_prefetch=1,
            grid=(steps,),
            in_specs=specs,
            out_specs=tuple(out_specs),
            scratch_shapes=[pltpu.VMEM((rows, D), f32)],
        ),
        out_shape=tuple(shapes),
        input_output_aliases=aliases,
        compiler_params=params(),
        cost_estimate=cost(4 * rows * D * D * steps, 4 * D * D * steps),
        name="ffn_part",
    )(*operands)


def join(base, products, next_gain):
    rows = base.shape[0]
    tile = row_tile(rows)
    count = len(products)

    def body(base_ref, *refs):
        gain_ref, out_ref, next_ref = refs[count:]
        both = refs[0][...].astype(f32)
        for ref in refs[1:count]:
            both = both + ref[...].astype(f32)
        y = base_ref[...].astype(f32) + 0.5 * both
        out_ref[...] = y
        next_ref[...] = norm(y, gain_ref[...]).astype(bf16)

    spec = pl.BlockSpec((tile, D), lambda t: (t, 0))
    return pl.pallas_call(
        body,
        grid=(rows // tile,),
        out_shape=(
            jax.ShapeDtypeStruct((rows, D), f32),
            jax.ShapeDtypeStruct((rows, D), bf16),
        ),
        in_specs=[spec] * (count + 1) + [const_spec((1, D))],
        out_specs=(spec, spec),
        compiler_params=params(),
        name="join",
    )(base, *products, next_gain)


def ffn_backward(
    after, after_gain, after_grads, base, stream, gain, pre, weights, upper, lower, sums, table,
    ranks, kept=None, first=0, last=None, carry=None,
):
    rows = stream.shape[0]
    tile = row_tile(rows)
    wide = 512
    steps = (FF // wide if last is None else last) - first
    whole = FF // wide
    parts = len(after_grads)
    targets = len(sums)
    with_base = base is not None
    again = kept is not None

    def body(table_ref, *refs):
        refs = list(refs)
        at_ref = 0
        if parts > 0:
            after_ref, after_gain_ref = refs[0], refs[1]
            grad_refs = refs[2 : 2 + parts]
            at_ref = 2 + parts
        base_ref = None
        if with_base:
            base_ref = refs[at_ref]
            at_ref += 1
        x_ref, gain_ref, up_ref, down_ref, pre_ref = refs[at_ref : at_ref + 5]
        kept_ref = refs[at_ref + 5]
        outs = refs[at_ref + 5 + again + (carry is not None) + aliased :]
        out_ref, gains_ref = outs[:2]
        sums_ref = outs[2 : 2 + targets]
        carry_ref = refs[at_ref + 5 + again]
        grad_sum = outs[2 + targets]
        (
            half, normed, pre_here, normed_t, pre_grad, act_t, up_part, down_part, up_sem, down_sem,
        ) = outs[3 + targets :]
        step = pl.program_id(0)

        @pl.when(step == 0)
        def _():
            gain_sum = jnp.zeros((1, D), f32)
            for t in range(0, rows, tile):
                here = slice(t, t + tile)
                if parts == 0:
                    back = base_ref[here]
                else:
                    grad = grad_refs[0][here].astype(f32)
                    for other in grad_refs[1:]:
                        grad = grad + other[here].astype(f32)
                    back, part = norm_back(after_ref[here], after_gain_ref[...], grad)
                    gain_sum = gain_sum + part
                    if with_base:
                        back = back + base_ref[here]
                out_ref[here] = back
                half[here] = (0.5 * back).astype(bf16)
                low = norm(x_ref[here].astype(f32), gain_ref[...]).astype(bf16)
                if again:
                    normed[here] = low
                normed_t[:, here] = low.T
                grad_sum[here] = jnp.zeros((tile, D), f32) if carry is None else carry_ref[here]
            gains_ref[0:1] = gain_sum

        if again:

            @pl.when((first + step) // (whole // 2) == kept_ref[0])
            def _():
                pre_here[...] = pre_ref[...]

            @pl.when((first + step) // (whole // 2) != kept_ref[0])
            def _():
                for t in range(0, rows, tile):
                    here = slice(t, t + tile)
                    pre_here[here] = dot(normed[here], up_ref[...]).astype(bf16)

        for t in range(0, rows, tile):
            here = slice(t, t + tile)
            act_grad = dot_right(half[here], down_ref[...])
            pre_act = (pre_here if again else pre_ref)[here].astype(f32)
            sigma = sigmoid(pre_act)
            act = pre_act * sigma
            act_t[:, here] = act.astype(bf16).T
            slope = sigma + act * (1.0 - sigma)
            moved = (act_grad * slope).astype(bf16)
            pre_grad[here] = moved
            grad_sum[here] += dot_right(moved, up_ref[...])

        @pl.when(step >= 1)
        def _():
            wait_blocks(up_part, up_sem)
            wait_blocks(down_part, down_sem)

        for t in range(0, D, 256):
            up_part[t : t + 256] = dot(normed_t[t : t + 256], pre_grad[...]).astype(bf16)
        for t in range(0, wide, 256):
            down_part[t : t + 256] = dot(act_t[t : t + 256], half[...]).astype(bf16)
        start_blocks(
            table_ref, sums_ref, up_part, up_sem, upper, 0, (first + step) * 4, ranks
        )
        start_blocks(
            table_ref, sums_ref, down_part, down_sem, lower, (first + step) * 4, 0, ranks
        )

        @pl.when(step == steps - 1)
        def _():
            wait_blocks(up_part, up_sem)
            wait_blocks(down_part, down_sem)
            if last is not None:
                return
            gain_sum = jnp.zeros((1, D), f32)
            for t in range(0, rows, tile):
                here = slice(t, t + tile)
                back, part = norm_back(x_ref[here].astype(f32), gain_ref[...], grad_sum[here])
                gain_sum = gain_sum + part
                out_ref[here] += back
            gains_ref[1:2] = gain_sum

    operands = [table]
    specs = [SMEM]
    if parts > 0:
        operands += [after, after_gain, *after_grads]
        specs += [const_spec((rows, D)), const_spec((1, D))] + [const_spec((rows, D))] * parts
    if with_base:
        operands.append(base)
        specs.append(const_spec((rows, D)))
    operands += [stream, gain, weights, weights]
    specs += [
        const_spec((rows, D)),
        const_spec((1, D)),
        pl.BlockSpec((D, wide), lambda f: (at(upper) + (first + f) // 2, (first + f) % 2)),
        pl.BlockSpec((wide, D), lambda f: (at(lower) * 2 + first + f, 0)),
    ]
    operands.append(pre)
    specs.append(pl.BlockSpec((rows, wide), lambda f: (0, first + f)))
    if again:
        operands.append(kept.reshape(1))
        specs.append(SMEM)
    if carry is not None:
        operands.append(carry)
        specs.append(const_spec((rows, D)))
    aliases = {}
    aliased = 0 if isinstance(sums[0], tuple) else targets
    if not isinstance(sums[0], tuple):
        for n, target in enumerate(sums):
            aliases[len(operands)] = 2 + n
            operands.append(target)
            specs.append(ANY)
        sums = [target.shape for target in sums]
    return pl.pallas_call(
        body,
        grid=(steps,),
        out_shape=(
            jax.ShapeDtypeStruct((rows, D), f32),
            jax.ShapeDtypeStruct((2, D), f32),
            *[jax.ShapeDtypeStruct(shape, bf16) for shape in sums],
        )
        + ((jax.ShapeDtypeStruct((rows, D), f32),) if last is not None else ()),
        in_specs=specs,
        out_specs=(const_spec((rows, D)), const_spec((2, D)))
        + (ANY,) * targets
        + ((const_spec((rows, D)),) if last is not None else ()),
        scratch_shapes=([pltpu.VMEM((rows, D), f32)] if last is None else [])
        + [
            pltpu.VMEM((rows, D), bf16),
            pltpu.VMEM((rows, D) if again else (16, 128), bf16),
            pltpu.VMEM((rows, wide) if again else (16, 128), bf16),
            pltpu.VMEM((D, rows), bf16),
            pltpu.VMEM((rows, wide), bf16),
            pltpu.VMEM((wide, rows), bf16),
            pltpu.VMEM((D, wide), bf16),
            pltpu.VMEM((wide, D), bf16),
            pltpu.SemaphoreType.DMA,
            pltpu.SemaphoreType.DMA,
        ],
        input_output_aliases=aliases,
        compiler_params=params(has_side_effects=True),
        cost_estimate=cost(8 * rows * D * wide * steps, 8 * D * wide * steps),
        name="ffn_backward",
    )(*operands)


def project(values, weights, first, count, part=None, parts=1, into=None):
    rows = values.shape[0]
    tile = row_tile(rows)
    wide = D

    def body(part_ref, x_ref, w_ref, *rest):
        out_ref = rest[-1]
        for t in range(0, rows, tile):
            out_ref[t : t + tile] = dot(x_ref[t : t + tile], w_ref[...]).astype(bf16)

    operands = [jnp.asarray(0 if part is None else part, jnp.int32).reshape(1), values, weights]
    specs = [
        pl.BlockSpec((rows, D), lambda f, part: (0, 0), pipeline_mode=pl.Buffered(1)),
        pl.BlockSpec((D, wide), lambda f, part: (at(first) + f, 0)),
    ]
    aliases = {}
    if into is not None:
        aliases = {3: 0}
        operands.append(into)
        specs.append(ANY)
    return pl.pallas_call(
        body,
        grid_spec=pltpu.PrefetchScalarGridSpec(
            num_scalar_prefetch=1,
            grid=(count,),
            in_specs=specs,
            out_specs=pl.BlockSpec((rows, wide), lambda f, part: (part[0], f)),
        ),
        out_shape=jax.ShapeDtypeStruct((parts * rows, count * D), bf16),
        input_output_aliases=aliases,
        compiler_params=params(),
        cost_estimate=cost(2 * rows * D * D * count, 2 * count * D * (D + rows)),
        name="project",
    )(*operands)


def project_out(values, weights, matrix, stream):
    rows = values.shape[0]
    tile = 512 if rows % 512 == 0 else row_tile(rows)

    def body(x_ref, w_ref, s_ref, out_ref):
        out_ref[...] = s_ref[...] + dot(x_ref[...], w_ref[...])

    return pl.pallas_call(
        body,
        grid=(rows // tile,),
        out_shape=jax.ShapeDtypeStruct((rows, D), f32),
        in_specs=[
            pl.BlockSpec((tile, D), lambda t: (t, 0)),
            pl.BlockSpec((D, D), lambda t: (at(matrix), 0)),
            pl.BlockSpec((tile, D), lambda t: (t, 0)),
        ],
        out_specs=pl.BlockSpec((tile, D), lambda t: (t, 0)),
        compiler_params=params(),
        cost_estimate=cost(2 * rows * D * D, 2 * D * D + 10 * rows * D),
        name="project_out",
    )(values, weights, stream)


def project_out_back(grad, weights, matrix, attended, sums, table, ranks):
    rows = grad.shape[0]
    tile = row_tile(rows)
    wide = 512

    targets = len(sums)

    def body(table_ref, g_ref, w_ref, a_ref, *refs):
        out_ref = refs[targets]
        sums_ref = refs[targets + 1 : 2 * targets + 1]
        low, part, sem = refs[2 * targets + 1 :]
        step = pl.program_id(0)

        @pl.when(step == 0)
        def _():
            for t in range(0, rows, tile):
                low[t : t + tile] = g_ref[t : t + tile].astype(bf16)

        for t in range(0, rows, tile):
            out_ref[t : t + tile] = dot_right(low[t : t + tile], w_ref[...]).astype(bf16)
        for t in range(0, wide, 256):
            part[step, t : t + 256] = dot_left(a_ref[:, t : t + 256], low[...]).astype(bf16)
        start_blocks(table_ref, sums_ref, part.at[step], sem.at[step], matrix, step * 4, 0, ranks)

        @pl.when(step == 1)
        def _():
            for s in range(2):
                wait_blocks(part.at[s], sem.at[s])

    return pl.pallas_call(
        body,
        grid=(2,),
        out_shape=(
            jax.ShapeDtypeStruct((rows, D), bf16),
            *[jax.ShapeDtypeStruct(target.shape, bf16) for target in sums],
        ),
        in_specs=[
            SMEM,
            const_spec((rows, D)),
            pl.BlockSpec((wide, D), lambda f: (at(matrix) * 2 + f, 0)),
            pl.BlockSpec((rows, wide), lambda f: (0, f)),
        ]
        + [ANY] * targets,
        out_specs=(pl.BlockSpec((rows, wide), lambda f: (0, f)),) + (ANY,) * targets,
        scratch_shapes=[
            pltpu.VMEM((rows, D), bf16),
            pltpu.VMEM((2, wide, D), bf16),
            pltpu.SemaphoreType.DMA((2,)),
        ],
        input_output_aliases={4 + n: 1 + n for n in range(targets)},
        compiler_params=params(has_side_effects=True),
        cost_estimate=cost(4 * rows * D * D, 4 * D * D + 8 * rows * D),
        name="project_out_back",
    )(table, grad, weights, attended, *sums)


def input_gradient(key_grad, value_grad, weights, part, rows):
    tile = row_tile(rows)
    steps = rows // tile

    def body(part_ref, k_ref, v_ref, wk_ref, wv_ref, out_ref):
        out_ref[...] = (
            dot_right(k_ref[...], wk_ref[...]) + dot_right(v_ref[...], wv_ref[...])
        ).astype(bf16)

    return pl.pallas_call(
        body,
        grid_spec=pltpu.PrefetchScalarGridSpec(
            num_scalar_prefetch=1,
            grid=(steps,),
            in_specs=[
                pl.BlockSpec((tile, D), lambda t, part: (part[0] * steps + t, 0)),
                pl.BlockSpec((tile, D), lambda t, part: (part[0] * steps + t, 0)),
                pl.BlockSpec((D, D), lambda t, part: (at(KEY), 0)),
                pl.BlockSpec((D, D), lambda t, part: (at(VALUE), 0)),
            ],
            out_specs=pl.BlockSpec((tile, D), lambda t, part: (t, 0)),
        ),
        out_shape=jax.ShapeDtypeStruct((rows, D), bf16),
        compiler_params=params(),
        cost_estimate=cost(4 * rows * D * D, 4 * D * D + 6 * rows * D),
        name="input_gradient",
    )(part.reshape(1), key_grad, value_grad, weights, weights)


def projections_back(
    normed, query_grad, key_grad, value_grad, sources, own_keys, weights, sums, table, ranks
):
    rows = normed.shape[0]
    tile = row_tile(rows)
    wide = 512
    count = len(sources)
    targets = len(sums)
    lengths = [source[0].shape[0] for source in sources]

    def body(part_ref, table_ref, n_ref, q_ref, *refs):
        normed_refs = refs[:count]
        key_refs = refs[count : 2 * count]
        value_refs = refs[2 * count : 3 * count]
        w_ref = refs[3 * count]
        outs = refs[3 * count + 1 + targets :]
        out_ref, sums_ref, scratch = outs[0], outs[1 : 1 + targets], outs[1 + targets :]
        own_t = scratch[0]
        source_t = scratch[1 : 1 + count]
        part, sem = scratch[1 + count :]
        step = pl.program_id(0)
        slot = lax.rem(step, 2)

        @pl.when(step == 0)
        def _():
            for t in range(0, rows, tile):
                own_t[:, t : t + tile] = n_ref[t : t + tile].T
            for n_from, n_to, length in zip(normed_refs, source_t, lengths):
                small = row_tile(length)
                for t in range(0, length, small):
                    n_to[:, t : t + small] = n_from[t : t + small].T

        @pl.when(step >= 2)
        def _():
            wait_blocks(part.at[slot], sem.at[slot])

        @pl.when(step < 2)
        def _():
            for t in range(0, rows, tile):
                new = dot_right(q_ref[t : t + tile], w_ref[...])

                @pl.when(step == 0)
                def _():
                    out_ref[t : t + tile] = new

                @pl.when(step == 1)
                def _():
                    out_ref[t : t + tile] += new

            for t in range(0, D, 256):
                part[slot, t : t + 256] = dot(own_t[t : t + 256], q_ref[...]).astype(bf16)
            start_blocks(
                table_ref, sums_ref, part.at[slot], sem.at[slot], QUERY, 0, lax.rem(step, 2) * 4,
                ranks,
            )

        def other(grad_refs, matrix):
            if own_keys:
                for t in range(0, rows, tile):
                    out_ref[t : t + tile] += dot_right(grad_refs[0][t : t + tile], w_ref[...])
            for t in range(0, D, 256):
                total = dot(source_t[0][t : t + 256], grad_refs[0][...])
                for n_t, grad_ref in zip(source_t[1:], grad_refs[1:]):
                    total = total + dot(n_t[t : t + 256], grad_ref[...])
                part[slot, t : t + 256] = total.astype(bf16)
            start_blocks(
                table_ref, sums_ref, part.at[slot], sem.at[slot], matrix, 0, lax.rem(step, 2) * 4,
                ranks,
            )

        @pl.when((step >= 2) & (step < 4))
        def _():
            other(key_refs, KEY)

        @pl.when(step >= 4)
        def _():
            other(value_refs, VALUE)

        @pl.when(step == 5)
        def _():
            for s in range(2):
                wait_blocks(part.at[s], sem.at[s])

    parts = jnp.stack([jnp.asarray(source[1], jnp.int32) for source in sources])
    operands = [parts, table, normed, query_grad]

    def whole(shape):
        return pl.BlockSpec(shape, lambda f, part: (0, 0), pipeline_mode=pl.Buffered(1))

    specs = [
        SMEM,
        whole((rows, D)),
        pl.BlockSpec((rows, wide), lambda f, part: (0, jnp.minimum(f, 1))),
    ]
    operands += [source[0] for source in sources]
    specs += [whole((length, D)) for length in lengths]
    for grads, first in ((key_grad, 2), (value_grad, 4)):
        for n, length in enumerate(lengths):
            operands.append(grads)
            specs.append(
                pl.BlockSpec(
                    (length, wide),
                    lambda f, part, n=n, first=first: (part[n], jnp.clip(f - first, 0, 1)),
                )
            )
    operands += [weights, *sums]
    specs += [pl.BlockSpec((D, wide), lambda f, part: (at(QUERY) + f // 2, f % 2))]
    specs += [ANY] * targets
    return pl.pallas_call(
        body,
        grid_spec=pltpu.PrefetchScalarGridSpec(
            num_scalar_prefetch=1,
            grid=(6,),
            in_specs=specs,
            out_specs=(whole((rows, D)),) + (ANY,) * targets,
            scratch_shapes=[pltpu.VMEM((D, rows), bf16)]
            + [pltpu.VMEM((D, length), bf16) for length in lengths]
            + [pltpu.VMEM((2, D, wide), bf16), pltpu.SemaphoreType.DMA((2,))],
        ),
        out_shape=(
            jax.ShapeDtypeStruct((rows, D), f32),
            *[jax.ShapeDtypeStruct(target.shape, bf16) for target in sums],
        ),
        input_output_aliases={len(operands) - targets + n: 1 + n for n in range(targets)},
        compiler_params=params(has_side_effects=True),
        cost_estimate=cost(
            (4 * rows + sum(4 * length for length in lengths) + 4 * rows) * D * D, 30 * D * D
        ),
        name="projections_back",
    )(*operands)


def attention_tiles(rows):
    return (512 if rows % 512 == 0 else row_tile(rows)), 256


def key_windows(segments, rank, rows):
    tall, broad = attention_tiles(rows)
    group = segments.shape[0]
    blocks = rows // tall
    own = lax.dynamic_slice_in_dim(segments, rank * rows, rows).reshape(blocks, tall)
    low = jnp.sum(segments[None, :] < own[:, :1], axis=1)
    high = jnp.sum(segments[None, :] <= own[:, -1:], axis=1)
    start = low // 128 * 128
    steps = (high - start + broad - 1) // broad
    start = jnp.minimum(start, group - steps * broad)
    return jnp.stack([start, steps], axis=-1).reshape(-1).astype(jnp.int32)

def attention_forward(queries, keys, segments, rank, windows, slopes):
    rows = queries.shape[0]
    group = keys.shape[0]
    tall, broad = attention_tiles(rows)
    most = group // broad
    own = lax.dynamic_slice_in_dim(segments, rank * rows, rows).reshape(rows, 1)

    def body(rank_ref, window_ref, slope_ref, q_ref, own_ref, key_ref, value_ref, columns_ref, out_ref, total_ref, scores):
        head, block = pl.program_id(0), pl.program_id(1)
        slope = slope_ref[head] * LOG2E
        start = window_ref[2 * block]
        steps = window_ref[2 * block + 1]
        first = rank_ref[0] * rows + block * tall
        query = q_ref[...]
        apart = (
            lax.broadcasted_iota(jnp.int32, (tall, broad), 0)
            - lax.broadcasted_iota(jnp.int32, (tall, broad), 1)
        ).astype(f32)

        def attend(count):
            peak = jnp.full((tall, 128), MASKED, f32)
            for b in range(count):
                begin = pl.multiple_of(start + b * broad, 128)
                here = pl.ds(begin, broad)
                score = dot_right(query, key_ref[here, :]) * (SCORE_SCALE * LOG2E)
                score = score - slope * jnp.abs(apart + (first - begin).astype(f32))
                score = jnp.where(own_ref[...] == columns_ref[:, here], score, MASKED)
                scores[:, b * broad : (b + 1) * broad] = score
                for lane in range(0, broad, 128):
                    peak = jnp.maximum(peak, score[:, lane : lane + 128])
            top = jnp.max(peak, axis=-1, keepdims=True)
            total = jnp.zeros((tall, 128), f32)
            mixed = jnp.zeros((tall, HEAD_DIM), f32)
            for b in range(count):
                here = pl.ds(pl.multiple_of(start + b * broad, 128), broad)
                shifted = jnp.exp2(scores[:, b * broad : (b + 1) * broad] - top)
                for lane in range(0, broad, 128):
                    total = total + shifted[:, lane : lane + 128]
                mixed = mixed + dot(shifted.astype(bf16), value_ref[here, :])
            total = jnp.sum(total, axis=-1, keepdims=True)
            out_ref[...] = (mixed / total).astype(bf16)
            logs = jnp.broadcast_to(top + jnp.log2(total), (tall, 128))
            total_ref[...] = logs.T[0:1, :].reshape(1, 1, tall)

        for count in range(1, most + 1):
            @pl.when(steps == count)
            def _(count=count):
                attend(count)

    return pl.pallas_call(
        body,
        grid=(HEADS, rows // tall),
        out_shape=(
            jax.ShapeDtypeStruct((rows, D), bf16),
            jax.ShapeDtypeStruct((HEADS, 1, rows), f32),
        ),
        in_specs=[
            SMEM, SMEM, SMEM,
            pl.BlockSpec((tall, HEAD_DIM), lambda h, q: (q, h)),
            pl.BlockSpec((tall, 1), lambda h, q: (q, 0)),
            pl.BlockSpec((group, HEAD_DIM), lambda h, q: (0, h)),
            pl.BlockSpec((group, HEAD_DIM), lambda h, q: (0, HEADS + h)),
            const_spec((1, group)),
        ],
        out_specs=(
            pl.BlockSpec((tall, HEAD_DIM), lambda h, q: (q, h)),
            pl.BlockSpec((1, 1, tall), lambda h, q: (h, 0, q)),
        ),
        scratch_shapes=[pltpu.VMEM((tall, group), f32)],
        compiler_params=params(),
        name="attention_forward",
    )(jnp.asarray(rank,jnp.int32).reshape(1), windows, slopes, queries, own, keys, keys, segments.reshape(1, group))

def attention_backward(queries, keys, segments, rank, windows, slopes, logs, grads, attended):
    rows = queries.shape[0]
    group = keys.shape[0]
    tall, broad = attention_tiles(rows)
    most = group // broad
    own = lax.dynamic_slice_in_dim(segments, rank * rows, rows).reshape(1, rows)

    def body(rank_ref, window_ref, slope_ref, q_ref, own_ref, log_ref, grad_ref, att_ref, key_ref, value_ref, columns_ref,
             out_ref, key_out, value_out, key_sum, value_sum):
        head, block = pl.program_id(0), pl.program_id(1)
        slope = slope_ref[head] * LOG2E
        start = window_ref[2 * block]
        steps = window_ref[2 * block + 1]
        first = rank_ref[0] * rows + block * tall

        @pl.when(block == 0)
        def _():
            key_sum[...] = jnp.zeros(key_sum.shape, f32)
            value_sum[...] = jnp.zeros(value_sum.shape, f32)

        query = q_ref[...]
        grad = grad_ref[...]
        products = grad.astype(f32) * att_ref[...].astype(f32)
        delta = jnp.broadcast_to(jnp.sum(products, axis=-1, keepdims=True), (tall, 128)).T[0:1, :]
        log_row = log_ref[0]
        apart = (
            lax.broadcasted_iota(jnp.int32, (broad, tall), 1)
            - lax.broadcasted_iota(jnp.int32, (broad, tall), 0)
        ).astype(f32)

        def attend(count):
            query_sum = jnp.zeros((tall, HEAD_DIM), f32)
            for b in range(count):
                begin = pl.multiple_of(start + b * broad, 128)
                here = pl.ds(begin, broad)
                key = key_ref[here, :]
                score = dot_right(key, query) * (SCORE_SCALE * LOG2E)
                score = score - slope * jnp.abs(apart + (first - begin).astype(f32))
                score = jnp.where(own_ref[...] == columns_ref[here, :], score, MASKED)
                probs = jnp.exp2(score - log_row)
                prob_grad = dot_right(value_ref[here, :], grad)
                value_sum[here, :] += dot(probs.astype(bf16), grad)
                score_grad = (probs * (prob_grad - delta)).astype(bf16)
                key_sum[here, :] += dot(score_grad, query)
                query_sum = query_sum + dot_left(score_grad, key)
            out_ref[...] = (query_sum * SCORE_SCALE).astype(bf16)

        for count in range(1, most + 1):
            @pl.when(steps == count)
            def _(count=count):
                attend(count)

        @pl.when(block == pl.num_programs(1) - 1)
        def _():
            key_out[...] = (key_sum[...] * SCORE_SCALE).astype(bf16)
            value_out[...] = value_sum[...].astype(bf16)

    row_spec = pl.BlockSpec((tall, HEAD_DIM), lambda h, q: (q, h))
    key_spec = pl.BlockSpec((group, HEAD_DIM), lambda h, q: (0, h))
    return pl.pallas_call(
        body,
        grid=(HEADS, rows // tall),
        out_shape=(jax.ShapeDtypeStruct((rows, D), bf16),) + (jax.ShapeDtypeStruct((group, D), bf16),) * 2,
        in_specs=[
            SMEM, SMEM, SMEM,
            pl.BlockSpec((tall, HEAD_DIM), lambda h, q: (q, h)),
            pl.BlockSpec((1, tall), lambda h, q: (0, q)),
            pl.BlockSpec((1, 1, tall), lambda h, q: (h, 0, q)),
            row_spec, row_spec, key_spec,
            pl.BlockSpec((group, HEAD_DIM), lambda h, q: (0, HEADS + h)),
            const_spec((group, 1)),
        ],
        out_specs=(row_spec, key_spec, key_spec),
        scratch_shapes=[pltpu.VMEM((group, HEAD_DIM), f32)] * 2,
        compiler_params=params(),
        name="attention_backward",
    )(jnp.asarray(rank,jnp.int32).reshape(1), windows, slopes, queries, own, logs, grads, attended, keys, keys, segments.reshape(group, 1))


def conv_forward(stream, before, behind, gain, next_gain, weights, taps, masks):
    rows = stream.shape[0]
    tall = rows + 2 * HALO
    tile = row_tile(rows)
    wide = 256
    steps = D // wide

    def body(
        x_ref, before_ref, behind_ref, gain_ref, next_gain_ref, taps_ref, mask_ref, value_ref, gate_ref, out_w_ref,
        out_ref, linear_ref, gate_out_ref, next_ref, normed, glu,
    ):
        step = pl.program_id(0)

        @pl.when(step == 0)
        def _():
            gain_row = gain_ref[...]
            normed[0:HALO] = norm(before_ref[...], gain_row).astype(bf16)
            normed[rows + HALO :] = norm(behind_ref[...], gain_row).astype(bf16)
            for t in range(0, rows, tile):
                x = x_ref[t : t + tile]
                normed[HALO + t : HALO + t + tile] = norm(x, gain_row).astype(bf16)
                out_ref[t : t + tile] = x

        pieces = [(0, HALO)]
        pieces += [(HALO + t, tile) for t in range(0, rows, tile)]
        pieces += [(rows + HALO, HALO)]
        for t, size in pieces:
            here = slice(t, t + size)
            linear = dot(normed[here], value_ref[...])
            gate = dot(normed[here], gate_ref[...])
            linear_ref[here] = linear.astype(bf16)
            gate_out_ref[here] = gate.astype(bf16)
            glu[here] = linear * sigmoid(gate)
        for t in range(0, rows, tile):
            sums = []
            for half in range(0, wide, 128):
                total = jnp.zeros((tile, 128), f32)
                for k in range(KERNEL):
                    moved = glu[HALO + t + k - 2 : HALO + t + k - 2 + tile, half : half + 128]
                    if k != KERNEL // 2:
                        moved = moved * mask_ref[k, HALO + t : HALO + t + tile]
                    total = total + taps_ref[k : k + 1, half : half + 128] * moved
                sums.append(total)
            conved = jnp.concatenate(sums, axis=1)
            act = (conved * sigmoid(conved)).astype(bf16)
            out_ref[t : t + tile] += dot(act, out_w_ref[...])

        @pl.when(step == steps - 1)
        def _():
            for t in range(0, rows, tile):
                next_ref[t : t + tile] = norm(out_ref[t : t + tile], next_gain_ref[...]).astype(bf16)

    return pl.pallas_call(
        body,
        grid=(steps,),
        out_shape=(
            jax.ShapeDtypeStruct((rows, D), f32),
            jax.ShapeDtypeStruct((tall, D), bf16),
            jax.ShapeDtypeStruct((tall, D), bf16),
            jax.ShapeDtypeStruct((rows, D), bf16),
        ),
        in_specs=[
            const_spec((rows, D)),
            const_spec((HALO, D)),
            const_spec((HALO, D)),
            const_spec((1, D)),
            const_spec((1, D)),
            pl.BlockSpec((KERNEL, wide), lambda c: (0, c)),
            const_spec((KERNEL, tall, 128)),
            pl.BlockSpec((D, wide), lambda c: (at(CONV_VALUE), c)),
            pl.BlockSpec((D, wide), lambda c: (at(CONV_GATE), c)),
            pl.BlockSpec((wide, D), lambda c: (at(CONV_OUT) * 4 + c, 0)),
        ],
        out_specs=(
            const_spec((rows, D)),
            pl.BlockSpec((tall, wide), lambda c: (0, c)),
            pl.BlockSpec((tall, wide), lambda c: (0, c)),
            const_spec((rows, D)),
        ),
        scratch_shapes=[pltpu.VMEM((tall, D), bf16), pltpu.VMEM((tall, wide), f32)],
        compiler_params=params(),
        cost_estimate=cost(6 * rows * D * D, 6 * D * D + 12 * rows * D),
        name="conv_forward",
    )(stream, before, behind, gain, next_gain, taps, masks, weights, weights, weights)


def conv_backward(
    grad, before, behind, stream, gain, linear, gate, weights, taps, masks, sums, table, ranks
):
    rows = stream.shape[0]
    tall = rows + 2 * HALO
    tile = row_tile(rows)
    wide = 256
    steps = D // wide
    targets = len(sums)

    def body(
        table_ref, g_ref, before_ref, behind_ref, x_ref, gain_ref, linear_ref, gate_ref, taps_ref,
        mask_ref, value_ref, gate_w_ref, out_w_ref, *refs,
    ):
        out_ref, gain_out_ref, taps_out_ref = refs[targets : targets + 3]
        sums_ref = refs[targets + 3 : 2 * targets + 3]
        (
            low, normed_t, grad_sum, glu, conv_grad, act_t, value_grad, gate_grad, value_part,
            gate_part, out_part, value_sem, gate_sem, out_sem,
        ) = refs[2 * targets + 3 :]
        step = pl.program_id(0)
        slot = lax.rem(step, 2)

        @pl.when(step == 0)
        def _():
            low[0:HALO] = before_ref[...]
            low[rows + HALO :] = behind_ref[...]
            for t in range(0, rows, tile):
                here = slice(t, t + tile)
                low[HALO + t : HALO + t + tile] = g_ref[here].astype(bf16)
                normed_t[:, here] = norm(x_ref[here], gain_ref[...]).astype(bf16).T
                grad_sum[here] = jnp.zeros((tile, D), f32)

        pieces = [(0, HALO)]
        pieces += [(HALO + t, tile) for t in range(0, rows, tile)]
        pieces += [(rows + HALO, HALO)]
        for t, size in pieces:
            here = slice(t, t + size)
            glu[here] = linear_ref[here].astype(f32) * sigmoid(gate_ref[here].astype(f32))

        edge = 8
        pieces = [(HALO - edge, edge)]
        pieces += [(HALO + t, tile) for t in range(0, rows, tile)]
        pieces += [(rows + HALO, edge)]
        tap_sums = [[jnp.zeros((1, 128), f32) for k in range(KERNEL)] for half in range(2)]
        for t, size in pieces:
            totals, moved_rows = [], []
            for half in range(0, wide, 128):
                total = jnp.zeros((size, 128), f32)
                moved_rows.append([])
                for k in range(KERNEL):
                    moved = glu[t + k - 2 : t + k - 2 + size, half : half + 128]
                    if k != KERNEL // 2:
                        moved = moved * mask_ref[k, t : t + size]
                    moved_rows[-1].append(moved)
                    total = total + taps_ref[k : k + 1, half : half + 128] * moved
                totals.append(total)
            conved = jnp.concatenate(totals, axis=1)
            sigma = sigmoid(conved)
            act = conved * sigma
            if size == tile:
                act_t[:, t - HALO : t - HALO + size] = act.astype(bf16).T
                rows_grad = dot_right(low[t : t + size], out_w_ref[...])
            elif t < HALO:
                rows_grad = dot_right(low[0:HALO], out_w_ref[...])[edge:]
            else:
                rows_grad = dot_right(low[rows + HALO :], out_w_ref[...])[:edge]
            center = rows_grad * (sigma + act * (1.0 - sigma))
            conv_grad[t : t + size] = center
            if size == tile:
                for number in range(2):
                    lanes = center[:, number * 128 : (number + 1) * 128]
                    for k in range(KERNEL):
                        tap_sums[number][k] = tap_sums[number][k] + jnp.sum(
                            lanes * moved_rows[number][k], axis=0, keepdims=True
                        )

        for t in range(0, rows, tile):
            values, gates = [], []
            for number, half in enumerate(range(0, wide, 128)):
                lanes = slice(half, half + 128)
                start = HALO + t
                total = jnp.zeros((tile, 128), f32)
                for k in range(KERNEL):
                    moved = conv_grad[start + 2 - k : start + 2 - k + tile, lanes]
                    if k != KERNEL // 2:
                        moved = moved * mask_ref[KERNEL - 1 - k, start : start + tile]
                    total = total + taps_ref[k : k + 1, lanes] * moved
                sigma = sigmoid(gate_ref[start : start + tile, lanes].astype(f32))
                moved_value = total * sigma
                values.append(moved_value.astype(bf16))
                gates.append(
                    (
                        moved_value
                        * linear_ref[start : start + tile, lanes].astype(f32)
                        * (1.0 - sigma)
                    ).astype(bf16)
                )
            value_tile = jnp.concatenate(values, axis=1)
            gate_tile = jnp.concatenate(gates, axis=1)
            here = slice(t, t + tile)
            value_grad[here] = value_tile
            gate_grad[here] = gate_tile
            grad_sum[here] += dot_right(value_tile, value_ref[...]) + dot_right(
                gate_tile, gate_w_ref[...]
            )
        for k in range(KERNEL):
            taps_out_ref[k : k + 1] = jnp.concatenate([tap_sums[0][k], tap_sums[1][k]], axis=1)

        @pl.when(step >= 2)
        def _():
            wait_blocks(value_part.at[slot], value_sem.at[slot])
            wait_blocks(gate_part.at[slot], gate_sem.at[slot])
            wait_blocks(out_part.at[slot], out_sem.at[slot])

        for t in range(0, D, 256):
            value_part[slot, t : t + 256] = dot(normed_t[t : t + 256], value_grad[...]).astype(bf16)
            gate_part[slot, t : t + 256] = dot(normed_t[t : t + 256], gate_grad[...]).astype(bf16)
        out_part[slot] = dot(act_t[...], low[HALO : rows + HALO]).astype(bf16)
        start_blocks(
            table_ref, sums_ref, value_part.at[slot], value_sem.at[slot], CONV_VALUE, 0, step * 2,
            ranks,
        )
        start_blocks(
            table_ref, sums_ref, gate_part.at[slot], gate_sem.at[slot], CONV_GATE, 0, step * 2,
            ranks,
        )
        start_blocks(
            table_ref, sums_ref, out_part.at[slot], out_sem.at[slot], CONV_OUT, step * 2, 0, ranks
        )

        @pl.when(step == steps - 1)
        def _():
            gain_sum = jnp.zeros((1, D), f32)
            for t in range(0, rows, tile):
                here = slice(t, t + tile)
                back, part = norm_back(x_ref[here], gain_ref[...], grad_sum[here])
                gain_sum = gain_sum + part
                out_ref[here] = g_ref[here] + back
            gain_out_ref[...] = gain_sum
            for s in range(2):
                wait_blocks(value_part.at[s], value_sem.at[s])
                wait_blocks(gate_part.at[s], gate_sem.at[s])
                wait_blocks(out_part.at[s], out_sem.at[s])

    operands = [
        table, grad, before, behind, stream, gain, linear, gate, taps, masks, weights, weights,
        weights, *sums,
    ]
    return pl.pallas_call(
        body,
        grid=(steps,),
        out_shape=(
            jax.ShapeDtypeStruct((rows, D), f32),
            jax.ShapeDtypeStruct((1, D), f32),
            jax.ShapeDtypeStruct((KERNEL, D), f32),
            *[jax.ShapeDtypeStruct(target.shape, bf16) for target in sums],
        ),
        in_specs=[
            SMEM,
            const_spec((rows, D)),
            const_spec((HALO, D)),
            const_spec((HALO, D)),
            const_spec((rows, D)),
            const_spec((1, D)),
            pl.BlockSpec((tall, wide), lambda c: (0, c)),
            pl.BlockSpec((tall, wide), lambda c: (0, c)),
            pl.BlockSpec((KERNEL, wide), lambda c: (0, c)),
            const_spec((KERNEL, tall, 128)),
            pl.BlockSpec((D, wide), lambda c: (at(CONV_VALUE), c)),
            pl.BlockSpec((D, wide), lambda c: (at(CONV_GATE), c)),
            pl.BlockSpec((wide, D), lambda c: (at(CONV_OUT) * 4 + c, 0)),
        ]
        + [ANY] * targets,
        out_specs=(
            const_spec((rows, D)),
            const_spec((1, D)),
            pl.BlockSpec((KERNEL, wide), lambda c: (0, c)),
        )
        + (ANY,) * targets,
        scratch_shapes=[
            pltpu.VMEM((tall, D), bf16),
            pltpu.VMEM((D, rows), bf16),
            pltpu.VMEM((rows, D), f32),
            pltpu.VMEM((tall, wide), f32),
            pltpu.VMEM((tall, wide), f32),
            pltpu.VMEM((wide, rows), bf16),
            pltpu.VMEM((rows, wide), bf16),
            pltpu.VMEM((rows, wide), bf16),
            pltpu.VMEM((2, D, wide), bf16),
            pltpu.VMEM((2, D, wide), bf16),
            pltpu.VMEM((2, wide, D), bf16),
            pltpu.SemaphoreType.DMA((2,)),
            pltpu.SemaphoreType.DMA((2,)),
            pltpu.SemaphoreType.DMA((2,)),
        ],
        input_output_aliases={len(operands) - targets + n: 3 + n for n in range(targets)},
        compiler_params=params(has_side_effects=True),
        cost_estimate=cost(12 * rows * D * D, 12 * D * D + 16 * rows * D),
        name="conv_backward",
    )(*operands)


def shampoo(grads, arrivals, left_stats, right_stats, left_root, right_root, master, average):
    slots = master.shape[0]
    each = 8
    steps = (slots + each - 1) // each
    arrivals = jnp.pad(arrivals, (0, steps * each - slots))
    old_bias = 1.0 - DECAY_AVERAGE ** (STEP - 1)
    new_bias = 1.0 - DECAY_AVERAGE**STEP

    def body(index_ref, *refs):
        g_refs = refs[:each]
        ls_ref, rs_ref, lr_ref, rr_ref, m_ref, a_ref, go, lo, ro, mo, ao = refs[each:]
        for n in range(each):
            grad = g_refs[n][0]
            go[n] = grad.astype(f32)
            lo[n] = DECAY_STAT * ls_ref[n] + (1.0 - DECAY_STAT) * dot_right(grad, grad)
            ro[n] = DECAY_STAT * rs_ref[n] + (1.0 - DECAY_STAT) * dot_left(grad, grad)
            inner = dot(grad, rr_ref[n].astype(bf16))
            turned = dot(lr_ref[n].astype(bf16), inner.astype(bf16))
            mean_sq = jnp.mean(turned * turned, axis=(0, 1), keepdims=True)
            new = m_ref[n] - RATE_BLOCK * turned * lax.rsqrt(mean_sq + 1e-06)
            mo[n] = new
            ao[n] = (DECAY_AVERAGE * old_bias / new_bias) * a_ref[n] + (
                (1.0 - DECAY_AVERAGE) / new_bias
            ) * new

    spec = pl.BlockSpec((each, BLOCK, BLOCK), lambda s, index: (s, 0, 0))
    grad_specs = [
        pl.BlockSpec((1, BLOCK, BLOCK), lambda s, index, n=n: (index[s * each + n], 0, 0))
        for n in range(each)
    ]
    shape = jax.ShapeDtypeStruct((slots, BLOCK, BLOCK), f32)
    return pl.pallas_call(
        body,
        grid_spec=pltpu.PrefetchScalarGridSpec(
            num_scalar_prefetch=1,
            grid=(steps,),
            in_specs=grad_specs + [spec] * 6,
            out_specs=(spec,) * 5,
        ),
        out_shape=(shape,) * 5,
        compiler_params=params(),
        name="shampoo",
    )(arrivals, *[grads] * each, left_stats, right_stats, left_root, right_root, master, average)


def vector_step(values, grads):
    mean_sq = jnp.mean(grads * grads, axis=-1, keepdims=True)
    return values - RATE_VECTOR * grads * lax.rsqrt(mean_sq + 1e-06)


def round_places(number):
    place = 0
    for other, count in enumerate(ROUNDS):
        if other == number:
            break
        place = place + (32 if other == LARGE else 64) * count
    if number == LARGE:
        return place, 64 * sum(ROUNDS) - 32 * ROUNDS[LARGE]
    return place, place + 32 * ROUNDS[number]


def scatter_tables(owners_all, coords, slot_dev, blocks):
    own_rank, own_x, own_core = coords
    ranks = owners_all.shape[0]
    both = 2 * slot_dev
    chips = owners_all // both
    same = chips[:, :, None] == chips[:, None, :]
    later = jnp.arange(blocks)[None, :] > jnp.arange(blocks)[:, None]
    order = jnp.sum((same & later[None]).astype(jnp.int32), axis=-1)
    dx = (chips % 2) ^ own_x
    z_at = chips // 2
    dy = jnp.arange(ranks)[:, None] ^ own_rank
    position = jnp.zeros_like(owners_all)
    arrival = jnp.zeros_like(owners_all)
    starts, unused = offsets(ranks)
    good = jnp.array(True)
    done = 0
    for number, count in enumerate(ROUNDS):
        inside = order - 4 * done
        core = inside // (2 * count)
        kind = inside // count % 2
        slot = inside % count
        outer = jnp.where(kind == 0, dx, dy)
        inner = jnp.where(kind == 0, dy, dx)
        dc = core ^ own_core
        here = ((kind * 2 + outer) * 2 + inner) * 4 + z_at
        first, second = round_places(number)
        here = jnp.where(dc == 0, first, second) + here * count + slot
        valid = (inside >= 0) & (inside < 4 * count)
        position = jnp.where(valid, here, position)
        arrival = jnp.where(valid, dc * slot_dev + 2 * done + inside % (2 * count), arrival)
        done = done + count
        if number < len(EARLY):
            there = jnp.arange(blocks) >= starts[EARLY[number]]
            good = good & jnp.all((order >= 4 * done) | there[None])
    device = (lax.axis_index("z") * 2 + own_x) * 2 + own_core
    mine = lax.dynamic_index_in_dim(owners_all, own_rank, 0, keepdims=False)
    arrival = lax.dynamic_index_in_dim(arrival, own_rank, 0, keepdims=False)
    match = mine[None, :] == (device * slot_dev + jnp.arange(slot_dev))[:, None]
    index = jnp.sum(jnp.where(match, arrival[None, :], 0), axis=-1)
    return position.reshape(-1).astype(jnp.int32), index.astype(jnp.int32), good


def added(terms):
    return sum(term.astype(f32) for term in terms).astype(bf16)


def one_round(rounds, send, number):
    count = ROUNDS[number]
    offset = round_places(number)[0]
    (come,) = yield [(send, "core")]
    half, quarter = 16 * count, 8 * count

    def part(kind, first, length):
        start = offset + kind * half + first
        here = kind * half + first
        return [rounds.sums[start : start + length], come[here : here + length]]

    got = yield [
        (added(part(0, quarter, quarter)), "x"),
        (added(part(1, quarter, quarter)), "mp"),
    ]
    eighth = quarter // 2
    late = yield [
        (added(part(0, eighth, eighth) + [got[0][eighth:]]), "mp"),
        (added(part(1, eighth, eighth) + [got[1][eighth:]]), "x"),
    ]
    columns = [
        added(part(kind, 0, eighth) + [got[kind][:eighth], late[kind]])
        .reshape(4, count, BLOCK, BLOCK)
        for kind in range(2)
    ]
    column = jnp.concatenate(columns, axis=1)
    if number < len(ROUNDS) - 1:
        return column
    z_at = lax.axis_index("z")

    def for_z(step):
        return lax.dynamic_index_in_dim(column, jnp.clip(z_at + step, 0, 3), 0, keepdims=False)

    got = yield [(for_z(step), step) for step in (2, -2, 1, -1, 3, -3)]
    return added([for_z(0), *got])


def total_steps(values):
    for group in (("core", "x", "both"), ("mp", "near", "across"), ("far",)):
        got = yield [(values, move) for move in group]
        values = values + got[0]
        if len(got) > 1:
            values = values + (got[1] + got[2])
    return values


class Rounds:
    def __init__(self, sums, tail):
        self.running, self.waiting, self.results = {}, {}, {}
        self.sums, self.tail = sums, tail

    def add(self, name, steps):
        self.running[name] = steps
        self.waiting[name] = next(steps)

    def add_round(self, number):
        size = 32 * ROUNDS[number]
        offset = round_places(number)[1]
        send = self.tail if number == LARGE else self.sums[offset : offset + size]
        self.add(number, one_round(self, send, number))

    def beside(self, *held):
        names = list(self.waiting)
        values = [value for name in names for value, unused in self.waiting[name]]
        out = list(tied(*values, *held))
        for name in names:
            self.waiting[name] = [(out.pop(0), move) for unused, move in self.waiting[name]]
        return out

    def hold(self):
        moves = [[move for unused, move in pairs] for pairs in self.waiting.values()]
        values = [value for pairs in self.waiting.values() for value, unused in pairs]
        columns = [(name, value) for name, value in self.results.items() if isinstance(name, int)]
        out = list(tied(self.sums, *values, *[value for unused, value in columns]))
        self.sums = out.pop(0)
        for name, names in zip(self.waiting, moves):
            self.waiting[name] = [(out.pop(0), move) for move in names]
        for (name, unused), value in zip(columns, out):
            self.results[name] = value
        return self.sums, self.tail

    def step(self, names, *held, sums=None):
        names = [name for name in names if name in self.waiting]
        transfers = [pair for name in names for pair in self.waiting[name]]
        if sums is not None:
            got, held = together(transfers, *sums, *held)
            (self.sums, self.tail), held = held[:2], held[2:]
        else:
            got, held = together(transfers, *held)
        for name in names:
            count = len(self.waiting[name])
            mine, got = got[:count], got[count:]
            try:
                self.waiting[name] = self.running[name].send(mine)
            except StopIteration as end:
                self.results[name] = end.value
                del self.waiting[name]
        return held


def both_swaps(value, moves):
    arrived = []
    for move in moves:
        (value,) = yield [(value, move)]
        arrived.append(value)
    return arrived


def joined(columns):
    return jnp.concatenate(columns, axis=1).reshape(-1, BLOCK, BLOCK)


def over_z(column):
    return lax.psum_scatter(column, "z", scatter_dimension=0, tiled=True)


def finish_rounds(rounds):
    rounds.add_round(3)
    rounds.step([2, 3])
    rounds.add_round(4)
    (column,) = rounds.beside(joined([rounds.results[number] for number in range(3)]))
    early = over_z(column)
    rounds.step([3, 4, "small"])
    rounds.step([3, "small"])
    (column,) = rounds.beside(joined([rounds.results[3]]))
    late = over_z(column)
    rounds.step([4, "small"])
    rounds.step([4])
    rounds.step([4])
    mine = jnp.concatenate([early, late, rounds.results[4]], axis=0)
    return jnp.concatenate([mine, swap(mine, "core")], axis=0)


def all_rounds(sums, tail):
    rounds = Rounds(sums, tail)
    for number in range(3):
        rounds.add_round(number)
    rounds.step([0, 1, 2])
    rounds.step([0, 1, 2])
    rounds.step([0, 1])
    return finish_rounds(rounds)


def edges(first_rows, last_rows, ranks):
    before = lax.ppermute(last_rows, "mp", [(r, r + 1) for r in range(ranks - 1)])
    behind = lax.ppermute(first_rows, "mp", [(r + 1, r) for r in range(ranks - 1)])
    return before, behind


def local(fast):
    def run(
        stream, cotangent, segments, owners, master, average, left_stats, right_stats, left_root,
        right_root, gains, kernel,
    ):
        ranks = lax.axis_size("mp")
        rank = lax.axis_index("mp")
        coords = (rank, lax.axis_index("x"), lax.axis_index("core"))
        rows = stream.shape[0]
        slot_dev = master.shape[1]
        chips = lax.axis_size("z") * lax.axis_size("x") * 2
        slots = slot_dev * chips
        segment_ids = segments[0]
        group = segment_ids.shape[0]
        unused, blocks = offsets(ranks)

        if fast:
            pair = jnp.concatenate([owners, swap(owners, "mp")])
            owners_all = jnp.where(rank == 0, pair, pair[::-1])
        else:
            owners_all = lax.all_gather(owners, "mp", axis=0, tiled=True)
        places = jnp.asarray(weight_places(ranks))
        if fast:
            table, arrivals, good = scatter_tables(owners_all, coords, slot_dev, blocks)
        else:
            table = (owners_all + jnp.arange(ranks)[:, None] * slots).reshape(-1)
            arrivals = jnp.arange(slot_dev, dtype=jnp.int32)

        slopes = 2.0 ** (-8.0 * (jnp.arange(HEADS).astype(f32) + 1.0) / HEADS)
        padded = jnp.pad(segment_ids, (HALO, HALO), constant_values=-1)
        wide_ids = jnp.pad(padded, (2, 2), constant_values=-2)
        tall = rows + 2 * HALO
        here = lax.dynamic_slice_in_dim(padded, rank * rows, tall)
        masks = jnp.stack(
            [
                (lax.dynamic_slice_in_dim(wide_ids, rank * rows + k, tall) == here).astype(f32)
                for k in range(KERNEL)
            ]
        )
        masks = jnp.broadcast_to(masks[:, :, None], (KERNEL, tall, 128))
        windows = key_windows(segment_ids, rank, rows)

        def gain(n):
            return gains[n : n + 1]

        starts = [offsets(ranks)[0][first] for first, unused in GROUPS] + [blocks]
        low = master[0].astype(bf16)
        if fast:
            across = 1 - rank
            dp = ("z", "x", "core")
            normed_own = norm_rows(stream, gain(0))
            low_other, normed_other = swap(low, "mp"), swap(normed_own, "mp")
            column = lax.all_gather(low, dp, axis=0, tiled=True)
            column, normed_other, table, arrivals, good, windows, masks = tied(
                column, normed_other, table, arrivals, good, windows, masks
            )
            low_other, column = tied(low_other, column)
            column_other = lax.all_gather(low_other, dp, axis=0, tiled=True)

            def of_index(slots, index, number, into=None):
                here = slice(starts[number], starts[number + 1])
                return unsort(
                    slots, owners_all[index, here], places[index, here], GROUP_CHUNKS[number], into
                )

            w_one = of_index(column, rank, 0)
            (product,) = ffn_part(normed_other, w_one, UP1, DOWN1, 2 * rank, 2, False)
            own_product, pre_first = ffn_part(normed_own, w_one, UP1, DOWN1, 2 * rank, 2, True)
            w_attn, w_conv, w_two = [of_index(column, rank, number) for number in (1, 2, 3)]
            (product,), (own_product, w_attn, w_conv, w_two) = together(
                [(product, "mp")], own_product, w_attn, w_conv, w_two
            )
            after_first, normed_attn = join(stream, [own_product, product], gain(1))
            (other,), unused = together([(normed_attn, "mp")])
            column_other, other = tied(column_other, other)

            w_attn = of_index(column_other, across, 1, w_attn)
            queries = project(normed_attn, w_attn, QUERY, 1)
            keys = project(normed_attn, w_attn, KEY, 2, rank, 2)
            keys = project(other, w_attn, KEY, 2, across, 2, keys)
            attended, logs = attention_forward(
                queries, keys, segment_ids, rank, windows, slopes
            )
            after_attn = project_out(attended, w_attn, OUT, after_first)
            w_conv = of_index(column_other, across, 2, w_conv)
            w_two = of_index(column_other, across, 3, w_two)
            w_one = of_index(column_other, across, 0, tied(w_one, own_product)[0])
            before, behind = edges(after_attn[:HALO], after_attn[-HALO:], ranks)
            after_conv, linear, gate, normed_two = conv_forward(
                after_attn, before, behind, gain(2), gain(3), w_conv, kernel, masks
            )
            product, pre_second = ffn_part(
                normed_two, w_two, UP2, DOWN2, jnp.zeros((), jnp.int32), 4, True
            )
            after_second, output = join(after_conv, [product], gain(4))
            sources = [(normed_attn, rank), (other, across)]
        else:
            everything = lax.all_gather(low, ("mp", "z", "x", "core"), axis=0, tiled=True)
            slot_of = owners_all + jnp.arange(ranks)[:, None] * slots
            arrays = []
            for number, chunks in enumerate(GROUP_CHUNKS):
                here = slice(starts[number], starts[number + 1])
                array = unsort(
                    everything, slot_of[:, here].reshape(-1).astype(jnp.int32),
                    places[:, here].reshape(-1), chunks,
                )
                arrays.append(array)
            w_one, w_attn, w_conv, w_two = arrays
            after_first, pre_first, normed_attn = ffn_forward(
                stream, gain(0), gain(1), w_one, UP1, DOWN1
            )
            other = lax.all_gather(normed_attn, "mp", axis=0, tiled=True)
            queries = project(normed_attn, w_attn, QUERY, 1)
            keys = project(other, w_attn, KEY, 2)
            sources = [(other, 0)]
            attended, logs = attention_forward(
                queries, keys, segment_ids, rank, windows, slopes
            )
            after_attn = project_out(attended, w_attn, OUT, after_first)
            before, behind = edges(after_attn[:HALO], after_attn[-HALO:], ranks)
            after_conv, linear, gate, normed_two = conv_forward(
                after_attn, before, behind, gain(2), gain(3), w_conv, kernel, masks
            )
            after_second, pre_second, output = ffn_forward(
                after_conv, gain(3), gain(4), w_two, UP2, DOWN2
            )

        if fast:
            last = 32 * ROUNDS[LARGE]
            sums = ((ranks * slots - last, BLOCK, BLOCK), (last, BLOCK, BLOCK))
        else:
            sums = ((ranks * slots, BLOCK, BLOCK),)
            if slots > blocks:
                sums = (jnp.zeros(sums[0], bf16),)
        grad_conv, gains_a, *sums = ffn_backward(
            after_second, gain(4), [cotangent], None, after_conv, gain(3), pre_second, w_two,
            UP2, DOWN2, sums, table, ranks,
        )
        if fast:
            rounds = Rounds(*sums)
            rounds.add_round(0)
            sums = rounds.hold()
        before, behind = edges(
            grad_conv[:HALO].astype(bf16), grad_conv[-HALO:].astype(bf16), ranks
        )
        grad_attn, gains_b, tap_grads, *sums = conv_backward(
            grad_conv, before, behind, after_attn, gain(2), linear, gate, w_conv, kernel, masks,
            sums, table, ranks,
        )
        if fast:
            grad_attn, gains_b, tap_grads = rounds.step(
                [0], grad_attn, gains_b, tap_grads, sums=sums
            )
            rounds.add_round(1)
            sums = rounds.hold()
        mixed_grad, *sums = project_out_back(
            grad_attn, w_attn, OUT, attended, sums, table, ranks
        )
        query_grad, key_grad, value_grad = attention_backward(
            queries, keys, segment_ids, rank, windows, slopes, logs, mixed_grad, attended
        )
        if fast:
            away = input_gradient(key_grad, value_grad, w_attn, 1 - rank, rows)
            query_grad, key_grad, value_grad, away = rounds.step(
                [0, 1], query_grad, key_grad, value_grad, away, sums=sums
            )
            sums = rounds.hold()
        else:
            away = input_gradient(key_grad, value_grad, w_attn, jnp.zeros((), jnp.int32), group)
            arrived = lax.psum_scatter(away, "mp", scatter_dimension=0, tiled=True)
        near, *sums = projections_back(
            normed_attn, query_grad, key_grad, value_grad, sources, fast, w_attn, sums, table, ranks
        )
        if fast:
            rounds.add("away", both_swaps(away, ["mp"]))
            (near,) = rounds.step(["away"], near, sums=sums)
            (arrived,) = rounds.results.pop("away")
            rounds.add_round(2)
            sums = rounds.hold()
        first_args = (gain(0), pre_first, w_one, UP1, DOWN1)
        if fast:
            middle = FF // 512 // 2
            so_far, gains_c, *sums, carry = ffn_backward(
                after_first, gain(1), [near, arrived], grad_attn, stream, *first_args, sums, table,
                ranks, rank, 0, middle,
            )
            so_far, gains_c, carry = rounds.step([0, 1, 2], so_far, gains_c, carry, sums=sums)
            sums = rounds.hold()
            stream_grad, gains_d, *sums = ffn_backward(
                None, None, [], so_far, stream, *first_args, sums, table, ranks, rank, middle,
                carry=carry,
            )
            stream_grad, gains_d = rounds.step([1, 2], stream_grad, gains_d, sums=sums)
            gains_c = jnp.concatenate([gains_c[0:1], gains_d[1:2]])
        else:
            stream_grad, gains_c, *sums = ffn_backward(
                after_first, gain(1), [near, arrived], grad_attn, stream, *first_args, sums, table,
                ranks,
            )
        small = jnp.concatenate(
            [gains_c[1:2], gains_c[0:1], gains_b, gains_a[1:2], gains_a[0:1], tap_grads]
        )
        everywhere = ("mp", "z", "x", "core")
        if fast:
            rounds.add("small", total_steps(small))
            sums = (rounds.sums, rounds.tail)
            own_grads = finish_rounds(rounds)
            small = rounds.results["small"]
            own_grads = lax.cond(
                good,
                lambda sums, tail, own: own,
                lambda sums, tail, own: all_rounds(sums, tail),
                *sums,
                own_grads,
            )
        else:
            own_grads = lax.psum_scatter(sums[0], everywhere, scatter_dimension=0, tiled=True)
            small = lax.psum(small, everywhere)
        gain_grads, kernel_grads = small[:5], small[5:]
        block_grads, left_new, right_new, master_new, average_new = shampoo(
            own_grads, arrivals, left_stats[0], right_stats[0], left_root[0], right_root[0], master[0],
            average[0],
        )
        return (
            output,
            stream_grad,
            block_grads[None],
            left_new[None],
            right_new[None],
            master_new[None],
            average_new[None],
            gain_grads,
            vector_step(gains, gain_grads),
            kernel_grads,
            vector_step(kernel, kernel_grads),
        )

    return run


def solution(mesh):
    ranks, pieces = mesh.shape["mp"], mesh.shape["dp"]
    fast = ranks == 2 and pieces == 16
    xs = 2 if fast else 1
    grid = Mesh(
        np.asarray(mesh.devices).reshape(ranks, pieces // (2 * xs), xs, 2), ("mp", "z", "x", "core")
    )
    dp = ("z", "x", "core")
    rows = P((*dp, "mp"), None)
    slots = P("mp", dp, None, None)
    return jax.shard_map(
        local(fast),
        mesh=grid,
        in_specs=(
            rows, rows, P(dp, None), P("mp", None), slots, slots, slots, slots, slots, slots, P(),
            P(),
        ),
        out_specs=(rows, rows, slots, slots, slots, slots, slots, P(), P(), P(), P()),
        check_vma=False,
    )
```
